128 devices in a mesh: lat: 16 (over z, x), lon: 8 (over y, core).
Axes of the slice: x: 4, y: 4, z: 4, core: 2. Of those that a mesh axis runs over, the one named last changes fastest.
Arguments:
- grid: bfloat16 [128, 512, 512], P('lat', 'lon'), may hold values from -6 to 6
- mesh_nodes: bfloat16 [16, 8, 256, 512], P('lat', 'lon'), may hold values from -6 to 6
- grid_cot: bfloat16 [128, 512, 512], P('lat', 'lon'), may hold values from -6 to 6
- enc_send: bfloat16 [512, 512], replicated, may hold values from -0.25 to 0.25
- enc_recv: bfloat16 [512, 512], replicated, may hold values from -0.25 to 0.25
- enc_out: bfloat16 [512, 512], replicated, may hold values from -0.25 to 0.25
- dec_send: bfloat16 [512, 512], replicated, may hold values from -0.25 to 0.25
- dec_recv: bfloat16 [512, 512], replicated, may hold values from -0.25 to 0.25
- dec_out: bfloat16 [512, 512], replicated, may hold values from -0.25 to 0.25
- enc_src: int32 [16, 8, 256, 32], P('lat', 'lon'), may hold values from 0 to 65535, as said below
- enc_live: int32 [16, 8, 256, 32], P('lat', 'lon'), may hold values from 0 to 1, as said below
- dec_src: int32 [3, 128, 512], P(None, 'lat', 'lon'), may hold values from 0 to 32767, as said below
Outputs:
- grid_new: bfloat16 [128, 512, 512], P('lat', 'lon')
- grid_grad: bfloat16 [128, 512, 512], P('lat', 'lon')
- mesh_grad: bfloat16 [16, 8, 256, 512], P('lat', 'lon')
- enc_send_grad: float32 [512, 512], replicated
- enc_recv_grad: float32 [512, 512], replicated
- enc_out_grad: float32 [512, 512], replicated
- dec_send_grad: float32 [512, 512], replicated
- dec_recv_grad: float32 [512, 512], replicated
- dec_out_grad: float32 [512, 512], replicated
The draws below stay inside these ranges and needn't reach their ends.
Inputs may be any that keep to these rules, and one draw needn't show every extreme that they name: `enc_src`: every sender named by the mesh nodes of block (a, b), padded slots included, lies in grid rows a * 8 - 4 to (a + 1) * 8 + 3 and, cyclically, columns b * 64 - 4 to (b + 1) * 64 + 3; these bounds are reached. `enc_live`: the live slots of a mesh node are its first ones, 2 to 32 of them; some node has all 32. `dec_src`: the block (a, b) of every sender of a grid node is at most one block from the node's own block in latitude and, cyclically, in longitude; offsets of one are reached both ways.
All inputs are finite; a program needn't handle non-finite values.
Results may differ from the reference program's by a relative error of at most 0.013.
Values may be sent and summed in bfloat16 or wider, within the bound.
No kernel may reach another device: no remote copies, remote signals or barrier semaphores. Data moves between devices by JAX's collectives and lax.ppermute only.
A program may use at most 192 MiB of HBM per device.

```python
import jax
import jax.numpy as jnp
from jax import lax

D = 512
GR = 8
GC = 64
M_DEV = 256
K_E = 32
HALO = 4
NLAT = 128
NLON = 512
N_LAT = 16
N_LON = 8


def draw_enc_src(key, part):
    key = jax.random.fold_in(key, 11)
    key_list = jax.random.split(key, 4)
    full_shape = (N_LAT, N_LON, M_DEV, K_E)
    centre_shape = (N_LAT, N_LON, M_DEV, 1)
    lat_block = jnp.arange(N_LAT).reshape(N_LAT, 1, 1, 1)
    lon_block = jnp.arange(N_LON).reshape(1, N_LON, 1, 1)
    slot_index = jnp.arange(M_DEV).reshape(1, 1, M_DEV, 1)
    edge_index = jnp.arange(K_E).reshape(1, 1, 1, K_E)
    low_slot = slot_index == 0
    high_slot = slot_index == 1
    first_edge = edge_index == 0
    second_edge = edge_index == 1
    centre_row = lat_block * GR + jax.random.randint(key_list[0], centre_shape, 0, GR)
    centre_col = lon_block * GC + jax.random.randint(key_list[1], centre_shape, 0, GC)
    centre_row = jnp.where(low_slot, lat_block * GR, jnp.where(high_slot, lat_block * GR + GR - 1, centre_row))
    centre_col = jnp.where(low_slot, lon_block * GC, jnp.where(high_slot, lon_block * GC + GC - 1, centre_col))
    step_row = jax.random.randint(key_list[2], full_shape, -HALO, HALO + 1)
    step_col = jax.random.randint(key_list[3], full_shape, -HALO, HALO + 1)
    forced = low_slot | high_slot
    step_row = jnp.where(low_slot & first_edge, -HALO, jnp.where(high_slot & first_edge, HALO, jnp.where(forced & second_edge, 0, step_row)))
    step_col = jnp.where(low_slot & second_edge, -HALO, jnp.where(high_slot & second_edge, HALO, jnp.where(forced & first_edge, 0, step_col)))
    grid_row = jnp.clip(centre_row + step_row, 0, GR * N_LAT - 1)
    grid_col = (centre_col + step_col) % (GC * N_LON)
    return (grid_row * (GC * N_LON) + grid_col).astype(jnp.int32)


def draw_enc_live(key, part):
    key = jax.random.fold_in(key, 23)
    lat_block = jnp.arange(N_LAT).reshape(N_LAT, 1, 1, 1)
    slot_index = jnp.arange(M_DEV).reshape(1, 1, M_DEV, 1)
    distance = jnp.abs(2 * lat_block + 1 - N_LAT)
    ceiling = K_E // 2 + (K_E - K_E // 2) * distance // max(N_LAT - 1, 1)
    floor_count = jnp.maximum(ceiling // 2, 2)
    drawn = jax.random.randint(key, (N_LAT, N_LON, M_DEV, 1), 0, K_E + 1)
    live_count = floor_count + drawn % (ceiling - floor_count + 1)
    live_count = jnp.where((slot_index == 0) & (lat_block == 0), K_E, live_count)
    return (jnp.arange(K_E).reshape(1, 1, 1, K_E) < live_count).astype(jnp.int32)


def draw_dec_src(key, part):
    key = jax.random.fold_in(key, 37)
    key_list = jax.random.split(key, 3)
    full_shape = (3, GR * N_LAT, GC * N_LON)
    row_index = jnp.arange(GR * N_LAT).reshape(1, -1, 1)
    col_index = jnp.arange(GC * N_LON).reshape(1, 1, -1)
    vertex = jnp.arange(3).reshape(3, 1, 1)
    first_cell = (row_index % GR == 0) & (col_index % GC == 0)
    last_cell = (row_index % GR == GR - 1) & (col_index % GC == GC - 1)
    step_lat = jax.random.randint(key_list[0], full_shape, -1, 2)
    step_lon = jax.random.randint(key_list[1], full_shape, -1, 2)
    slot_pick = jax.random.randint(key_list[2], full_shape, 0, M_DEV)
    home_zero = first_cell & (vertex == 0) | last_cell & (vertex == 1)
    step_lat = jnp.where(home_zero, 0, step_lat)
    step_lon = jnp.where(home_zero, 0, step_lon)
    step_lat = jnp.where(first_cell & (vertex == 2), 1, jnp.where(last_cell & (vertex == 2), -1, step_lat))
    step_lon = jnp.where(first_cell & (vertex == 2), 1, jnp.where(last_cell & (vertex == 2), -1, step_lon))
    slot_pick = jnp.where(first_cell & (vertex == 0), 0, slot_pick)
    slot_pick = jnp.where(last_cell & (vertex == 1), M_DEV - 1, slot_pick)
    owner_lat = jnp.clip(row_index // GR + step_lat, 0, N_LAT - 1)
    owner_lon = (col_index // GC + step_lon) % N_LON
    return ((owner_lat * N_LON + owner_lon) * M_DEV + slot_pick).astype(jnp.int32)


def level_of(stream_key, shape, shards, low, high):
    gain = 1.0
    for position, blocks in shards:
        draws = jax.random.uniform(jax.random.fold_in(jax.random.fold_in(stream_key, 6), position), (blocks,), jnp.float32, low / len(shards), high / len(shards))
        gain = gain * jnp.repeat(jnp.exp(draws), shape[position] // blocks).reshape((-1,) + (1,) * (len(shape) - 1 - position))
    return gain


def bell_draw(rng, shape, scale, most, shards=(), held_as=jnp.bfloat16):
    level = level_of(rng, shape, shards, -0.22, 0.18) if shards else 1.0
    array = jax.random.normal(rng, shape, jnp.float32) * scale * level
    return jnp.minimum(jnp.maximum(array, -most), most).astype(held_as)


def setup_inputs(seed: int = 0) -> dict:
    streams_of = jax.random.split(jax.random.key(seed), 13)
    grid = bell_draw(streams_of[0], (NLAT, NLON, D), 1.0, 6.0, ((0, 16), (1, 8)))
    mesh_nodes = bell_draw(streams_of[1], (N_LAT, N_LON, M_DEV, D), 1.0, 6.0, ((0, 16), (1, 8)))
    grid_cot = bell_draw(streams_of[2], (NLAT, NLON, D), 1.0, 6.0, ((0, 16), (1, 8)))
    enc_send = bell_draw(streams_of[3], (D, D), D ** -0.5, 0.25)
    enc_recv = bell_draw(streams_of[4], (D, D), D ** -0.5, 0.25)
    enc_out = bell_draw(streams_of[5], (D, D), D ** -0.5, 0.25)
    dec_send = bell_draw(streams_of[6], (D, D), D ** -0.5, 0.25)
    dec_recv = bell_draw(streams_of[7], (D, D), D ** -0.5, 0.25)
    dec_out = bell_draw(streams_of[8], (D, D), D ** -0.5, 0.25)
    enc_src = draw_enc_src(jax.random.fold_in(streams_of[12], 71), 0)
    enc_live = draw_enc_live(jax.random.fold_in(streams_of[12], 71), 0)
    dec_src = draw_dec_src(jax.random.fold_in(streams_of[12], 71), 0)
    return {"grid": grid, "mesh_nodes": mesh_nodes, "grid_cot": grid_cot, "enc_send": enc_send, "enc_recv": enc_recv, "enc_out": enc_out, "dec_send": dec_send, "dec_recv": dec_recv, "dec_out": dec_out, "enc_src": enc_src, "enc_live": enc_live, "dec_src": dec_src}


NORM_EPSILON = 1e-05

def layer_norm(message):
    centred = message - lax.optimization_barrier(jnp.mean(message, axis=-1, keepdims=True))
    factor = lax.rsqrt(lax.optimization_barrier(jnp.mean(centred * centred, axis=-1, keepdims=True)) + NORM_EPSILON)
    return (centred * factor, factor)

def edge_forward(senders, node_rows, recv_weight, out_weight, weight_mask, factor):
    receivers, degree, features = senders.shape
    received = jnp.dot(node_rows, recv_weight, preferred_element_type=jnp.float32)
    before = senders + received[:, None, :]
    hidden = jax.nn.silu(before).astype(jnp.bfloat16).reshape(receivers * degree, features)
    message = jnp.dot(hidden, out_weight, preferred_element_type=jnp.float32)
    normed, inverse = layer_norm(message)
    masked = normed.reshape(receivers, degree, features)
    if weight_mask is not None:
        masked = masked * weight_mask[:, :, None]
    summed = lax.optimization_barrier(jnp.sum(masked, axis=1))
    new_rows = (node_rows.astype(jnp.float32) + factor * summed).astype(jnp.bfloat16)
    return (new_rows, (before, hidden, normed, inverse))

def edge_backward(stored, node_rows, recv_weight, out_weight, weight_mask, factor, node_cot):
    before, hidden, normed, inverse = stored
    receivers, degree, features = before.shape
    spread = jnp.broadcast_to((factor * node_cot)[:, None, :], (receivers, degree, features))
    if weight_mask is not None:
        spread = spread * weight_mask[:, :, None]
    spread = spread.reshape(receivers * degree, features)
    message_cot = inverse * (spread - lax.optimization_barrier(jnp.mean(spread, axis=-1, keepdims=True)) - normed * lax.optimization_barrier(jnp.mean(spread * normed, axis=-1, keepdims=True)))
    message_cot = message_cot.astype(jnp.bfloat16)
    out_grad = jnp.dot(hidden.T, message_cot, preferred_element_type=jnp.float32)
    hidden_cot = jnp.dot(message_cot, out_weight.T, preferred_element_type=jnp.float32)
    hidden_cot = hidden_cot.reshape(receivers, degree, features)
    sigmoid = jax.nn.sigmoid(before)
    before_cot = hidden_cot * sigmoid * (1.0 + before * (1.0 - sigmoid))
    received_cot = lax.optimization_barrier(jnp.sum(before_cot, axis=1)).astype(jnp.bfloat16)
    recv_grad = jnp.dot(node_rows.T, received_cot, preferred_element_type=jnp.float32)
    node_grad = node_cot + jnp.dot(received_cot, recv_weight.T, preferred_element_type=jnp.float32)
    return (before_cot, node_grad, recv_grad, out_grad)

def reference(grid, mesh_nodes, grid_cot, enc_send, enc_recv, enc_out, dec_send, dec_recv, dec_out, enc_src, enc_live, dec_src):
    features = grid.shape[-1]
    blocks = N_LAT * N_LON
    scaling = K_E ** (-0.5)
    grid_rows = grid.reshape(NLAT * NLON, features)
    sent = jnp.dot(grid_rows, enc_send, preferred_element_type=jnp.float32).astype(jnp.bfloat16)
    sent_wide = lax.optimization_barrier(sent).astype(jnp.float32)
    mesh_blocks = mesh_nodes.reshape(blocks, M_DEV, features)
    source_blocks = enc_src.reshape(blocks, M_DEV, K_E)
    live_blocks = enc_live.reshape(blocks, M_DEV, K_E).astype(jnp.float32)

    def encode(item):
        node_rows, sources, live = item
        return edge_forward(sent_wide[sources], node_rows, enc_recv, enc_out, live, scaling)[0]
    mesh_new = lax.map(encode, (mesh_blocks, source_blocks, live_blocks))
    mesh_flat = mesh_new.reshape(blocks * M_DEV, features)
    moved = jnp.dot(mesh_flat, dec_send, preferred_element_type=jnp.float32).astype(jnp.bfloat16)
    moved_wide = lax.optimization_barrier(moved).astype(jnp.float32)
    grid_bands = grid.reshape(N_LAT, GR * NLON, features)
    cot_bands = grid_cot.reshape(N_LAT, GR * NLON, features)
    dec_sources = jnp.transpose(dec_src, (1, 2, 0)).reshape(N_LAT, GR * NLON, 3)

    def decode(carry, item):
        mesh_cot, recv_sum, out_sum = carry
        node_rows, sources, node_cot = item
        senders = moved_wide[sources]
        new_rows, stored = edge_forward(senders, node_rows, dec_recv, dec_out, None, 1.0)
        sender_cot, node_grad, recv_grad, out_grad = edge_backward(stored, node_rows, dec_recv, dec_out, None, 1.0, node_cot.astype(jnp.float32))
        mesh_cot = mesh_cot.at[sources.reshape(-1)].add(sender_cot.reshape(-1, features))
        return ((mesh_cot, recv_sum + recv_grad, out_sum + out_grad), (new_rows, node_grad))
    square = jnp.zeros((features, features), jnp.float32)
    start = (jnp.zeros((blocks * M_DEV, features), jnp.float32), square, square)
    (mesh_cot, dec_recv_grad, dec_out_grad), (grid_new, grid_part) = lax.scan(decode, start, (grid_bands, dec_sources, cot_bands))
    moved_cot = mesh_cot.astype(jnp.bfloat16)
    dec_send_grad = jnp.dot(mesh_flat.T, moved_cot, preferred_element_type=jnp.float32)
    mesh_new_cot = jnp.dot(moved_cot, dec_send.T, preferred_element_type=jnp.float32)
    mesh_new_cot = mesh_new_cot.reshape(blocks, M_DEV, features)

    def encode_back(carry, item):
        sent_cot, recv_sum, out_sum = carry
        node_rows, sources, live, node_cot = item
        senders = sent_wide[sources]
        stored = edge_forward(senders, node_rows, enc_recv, enc_out, live, scaling)[1]
        sender_cot, node_grad, recv_grad, out_grad = edge_backward(stored, node_rows, enc_recv, enc_out, live, scaling, node_cot)
        sent_cot = sent_cot.at[sources.reshape(-1)].add(sender_cot.reshape(-1, features))
        return ((sent_cot, recv_sum + recv_grad, out_sum + out_grad), node_grad.astype(jnp.bfloat16))
    start = (jnp.zeros((NLAT * NLON, features), jnp.float32), square, square)
    (sent_cot, enc_recv_grad, enc_out_grad), mesh_grad = lax.scan(encode_back, start, (mesh_blocks, source_blocks, live_blocks, mesh_new_cot))
    sent_cot = sent_cot.astype(jnp.bfloat16)
    enc_send_grad = jnp.dot(grid_rows.T, sent_cot, preferred_element_type=jnp.float32)
    grid_grad = (grid_part.reshape(NLAT * NLON, features) + jnp.dot(sent_cot, enc_send.T, preferred_element_type=jnp.float32)).astype(jnp.bfloat16)
    return (grid_new.reshape(NLAT, NLON, features), grid_grad.reshape(NLAT, NLON, features), mesh_grad.reshape(N_LAT, N_LON, M_DEV, features), enc_send_grad, enc_recv_grad, enc_out_grad, dec_send_grad, dec_recv_grad, dec_out_grad)
```

```python
import jax
import jax.numpy as jnp
from jax import lax
from jax.experimental import pallas as pl
from jax.experimental.pallas import tpu as pltpu
from jax.sharding import PartitionSpec as P

REACH = 4
NORM_EPSILON = 1e-05
BF = jnp.bfloat16
F32 = jnp.float32
VMEM_LIMIT = 56 * 1024 * 1024
ENC_TILE = 32
ENC_CHUNK = 8
DEC_TILE = 128


def dot(a, b):
    return jnp.dot(a, b, preferred_element_type=F32)


def dot_nt(a, b):
    return lax.dot_general(a, b, (((1,), (1,)), ((), ())), preferred_element_type=F32)


def dot_tn(a, b):
    return lax.dot_general(a, b, (((0,), (0,)), ((), ())), preferred_element_type=F32)


def sigma(v):
    return 0.5 * jnp.tanh(0.5 * v) + 0.5


def normalise(message):
    centred = message - jnp.mean(message, axis=-1, keepdims=True)
    factor = lax.rsqrt(jnp.mean(centred * centred, axis=-1, keepdims=True) + NORM_EPSILON)
    return centred, factor


def whole(shape):
    return pl.BlockSpec(shape, lambda t: (0,) * len(shape))


def rows_of(count, width):
    return pl.BlockSpec((count, width), lambda t: (t, 0))


def enc_forward_kernel(
    idx_ref, live_ref, mesh_ref, own_ref, high_ref, low_ref, left_ref, right_ref,
    send_ref, recv_ref, out_ref, dec_send_ref,
    new_ref, moved_ref, before_ref, normed_ref, scale_ref,
    band, onehot,
):
    tile, degree = idx_ref.shape
    width = mesh_ref.shape[1]
    band_rows = band.shape[0]

    @pl.when(pl.program_id(0) == 0)
    def _():
        at = 0
        for piece in (own_ref, high_ref, low_ref, left_ref, right_ref):
            count = piece.shape[0]
            band[at : at + count, :] = dot(piece[...], send_ref[...]).astype(BF)
            at += count

    column = lax.broadcasted_iota(jnp.int32, (tile, band_rows), 1)
    for k in range(degree):
        hit = idx_ref[:, k : k + 1] == column
        onehot[k * tile : (k + 1) * tile, :] = jnp.where(hit, 1.0, 0.0).astype(BF)

    nodes = mesh_ref[...]
    received = dot(nodes, recv_ref[...])
    total = jnp.zeros((tile, width), F32)
    lane = lax.broadcasted_iota(jnp.int32, (tile, degree), 1)
    scales = jnp.zeros((tile, degree), F32)
    rows = ENC_CHUNK * tile
    for c in range(degree // ENC_CHUNK):
        part = pl.ds(c * rows, rows)
        gathered = dot(onehot[part, :], band[...])
        before = gathered.reshape(ENC_CHUNK, tile, width) + received[None]
        before_ref[part, :] = before.reshape(rows, width).astype(BF)
        hidden = (before * sigma(before)).reshape(rows, width).astype(BF)
        centred, factor = normalise(dot(hidden, out_ref[...]))
        normed = (centred * factor).reshape(ENC_CHUNK, tile, width)
        normed_ref[part, :] = normed.reshape(rows, width).astype(BF)
        factor = factor.reshape(ENC_CHUNK, tile, 1)
        for j in range(ENC_CHUNK):
            k = c * ENC_CHUNK + j
            live = live_ref[:, k : k + 1]
            total = total + normed[j] * live
            scales = jnp.where(lane == k, factor[j] * live, scales)
    scale_ref[...] = scales
    new = (nodes.astype(F32) + degree ** (-0.5) * total).astype(BF)
    new_ref[...] = new
    moved_ref[...] = dot(new, dec_send_ref[...]).astype(BF)


def enc_forward(idx, live, mesh_rows, pieces, enc_send, enc_recv, enc_out, dec_send):
    nodes, degree = idx.shape
    width = mesh_rows.shape[1]
    tile = ENC_TILE
    edges = tile * degree
    band_rows = sum(p.shape[0] for p in pieces)
    square = whole((width, width))
    return pl.pallas_call(
        enc_forward_kernel,
        name="enc_forward",
        grid=(nodes // tile,),
        in_specs=[rows_of(tile, degree), rows_of(tile, degree), rows_of(tile, width)]
        + [whole(p.shape) for p in pieces]
        + [square] * 4,
        out_specs=[
            rows_of(tile, width), rows_of(tile, width),
            rows_of(edges, width), rows_of(edges, width), rows_of(tile, degree),
        ],
        out_shape=[
            jax.ShapeDtypeStruct((nodes, width), BF),
            jax.ShapeDtypeStruct((nodes, width), BF),
            jax.ShapeDtypeStruct((nodes * degree, width), BF),
            jax.ShapeDtypeStruct((nodes * degree, width), BF),
            jax.ShapeDtypeStruct((nodes, degree), F32),
        ],
        scratch_shapes=[
            pltpu.VMEM((band_rows, width), BF),
            pltpu.VMEM((edges, band_rows), BF),
        ],
        compiler_params=pltpu.CompilerParams(vmem_limit_bytes=VMEM_LIMIT),
    )(idx, live, mesh_rows, *pieces, enc_send, enc_recv, enc_out, dec_send)


def decoder_kernel(
    idx_ref, idx_row_ref, grid_ref, cot_ref, centre_ref, left_ref, right_ref,
    recv_ref, out_ref,
    new_ref, part_ref, out_grad_ref, recv_grad_ref, centre_tot_ref, left_tot_ref, right_tot_ref,
    onehot, onehot_t, totals, out_acc, recv_acc,
):
    step = pl.program_id(0)
    tile, width = grid_ref.shape
    degree = idx_ref.shape[1]
    cycle = onehot.shape[1]
    third = cycle // 3
    edges = tile * degree

    @pl.when(step == 0)
    def _():
        totals[...] = jnp.zeros_like(totals)
        out_acc[...] = jnp.zeros_like(out_acc)
        recv_acc[...] = jnp.zeros_like(recv_acc)

    column = lax.broadcasted_iota(jnp.int32, (tile, cycle), 1)
    row = lax.broadcasted_iota(jnp.int32, (cycle, tile), 0)
    for j in range(degree):
        hit = idx_ref[:, j : j + 1] == column
        onehot[j * tile : (j + 1) * tile, :] = jnp.where(hit, 1.0, 0.0).astype(BF)
        hit = idx_row_ref[j : j + 1, :] == row
        onehot_t[:, j * tile : (j + 1) * tile] = jnp.where(hit, 1.0, 0.0).astype(BF)

    nodes = grid_ref[...]
    received = dot(nodes, recv_ref[...])
    gathered = dot(onehot[:, :third], centre_ref[...])
    gathered = gathered + dot(onehot[:, third : 2 * third], left_ref[...])
    gathered = gathered + dot(onehot[:, 2 * third :], right_ref[...])
    before = gathered.reshape(degree, tile, width) + received[None]
    sig = sigma(before)
    silu = before * sig
    hidden = silu.reshape(edges, width).astype(BF)
    centred, factor = normalise(dot(hidden, out_ref[...]))
    normed = (centred * factor).reshape(degree, tile, width)
    factor = factor.reshape(degree, tile, 1)
    new_ref[...] = (nodes.astype(F32) + jnp.sum(normed, axis=0)).astype(BF)

    cot = cot_ref[...].astype(F32)
    level = cot - jnp.mean(cot, axis=-1, keepdims=True)
    along = jnp.mean(cot[None] * normed, axis=-1, keepdims=True)
    message_cot = (factor * (level[None] - normed * along)).reshape(edges, width).astype(BF)
    out_acc[...] += dot_tn(hidden, message_cot)
    hidden_cot = dot_nt(message_cot, out_ref[...]).reshape(degree, tile, width)
    before_cot = hidden_cot * (sig + silu * (1.0 - sig))
    received_cot = jnp.sum(before_cot, axis=0).astype(BF)
    recv_acc[...] += dot_tn(nodes, received_cot)
    part_ref[...] = cot + dot_nt(received_cot, recv_ref[...])
    totals[...] += dot(onehot_t[...], before_cot.reshape(edges, width).astype(BF))

    @pl.when(step == pl.num_programs(0) - 1)
    def _():
        out_grad_ref[...] = out_acc[...].astype(BF)
        recv_grad_ref[...] = recv_acc[...].astype(BF)
        centre_tot_ref[...] = totals[:third, :].astype(BF)
        left_tot_ref[...] = totals[third : 2 * third, :].astype(BF)
        right_tot_ref[...] = totals[2 * third :, :].astype(BF)


def decoder(idx, grid_rows, cot_rows, centre, left, right, dec_recv, dec_out):
    nodes, width = grid_rows.shape
    degree = idx.shape[1]
    tile = DEC_TILE
    third = centre.shape[0]
    square = whole((width, width))
    return pl.pallas_call(
        decoder_kernel,
        name="decoder",
        grid=(nodes // tile,),
        in_specs=[
            rows_of(tile, degree),
            pl.BlockSpec((degree, tile), lambda t: (0, t)),
            rows_of(tile, width), rows_of(tile, width),
            whole(centre.shape), whole(centre.shape), whole(centre.shape),
            square, square,
        ],
        out_specs=[
            rows_of(tile, width), rows_of(tile, width), square, square,
            whole(centre.shape), whole(centre.shape), whole(centre.shape),
        ],
        out_shape=[
            jax.ShapeDtypeStruct((nodes, width), BF),
            jax.ShapeDtypeStruct((nodes, width), F32),
            jax.ShapeDtypeStruct((width, width), BF),
            jax.ShapeDtypeStruct((width, width), BF),
            jax.ShapeDtypeStruct(centre.shape, BF),
            jax.ShapeDtypeStruct(centre.shape, BF),
            jax.ShapeDtypeStruct(centre.shape, BF),
        ],
        scratch_shapes=[
            pltpu.VMEM((degree * tile, 3 * third), BF),
            pltpu.VMEM((3 * third, degree * tile), BF),
            pltpu.VMEM((3 * third, width), F32),
            pltpu.VMEM((width, width), F32),
            pltpu.VMEM((width, width), F32),
        ],
        compiler_params=pltpu.CompilerParams(vmem_limit_bytes=VMEM_LIMIT),
    )(idx, idx.T, grid_rows, cot_rows, centre, left, right, dec_recv, dec_out)


def enc_backward_kernel(
    idx_row_ref, scale_ref, mesh_ref, moved_cot_ref, before_ref, normed_ref,
    own_ref, high_ref, low_ref, left_ref, right_ref,
    dec_send_ref, recv_ref, out_ref,
    mesh_grad_ref, band_cot_ref, send_grad_ref, recv_grad_ref, out_grad_ref,
    onehot_t, hidden_all, message_cot_all, before_cot_all, totals, out_acc, recv_acc,
):
    step = pl.program_id(0)
    tile, width = mesh_ref.shape
    degree = scale_ref.shape[1]
    band_rows = totals.shape[0]

    @pl.when(step == 0)
    def _():
        totals[...] = jnp.zeros_like(totals)
        out_acc[...] = jnp.zeros_like(out_acc)
        recv_acc[...] = jnp.zeros_like(recv_acc)

    row = lax.broadcasted_iota(jnp.int32, (band_rows, tile * degree), 0)
    onehot_t[...] = jnp.where(idx_row_ref[0] == row, 1.0, 0.0).astype(BF)

    nodes = mesh_ref[...]
    node_cot = dot_nt(moved_cot_ref[...], dec_send_ref[...])
    spread = degree ** (-0.5) * node_cot
    level = spread - jnp.mean(spread, axis=-1, keepdims=True)
    received_cot = jnp.zeros((tile, width), F32)
    rows = ENC_CHUNK * tile
    for c in range(degree // ENC_CHUNK):
        part = pl.ds(c * rows, rows)
        normed = normed_ref[part, :].astype(F32).reshape(ENC_CHUNK, tile, width)
        along = jnp.mean(spread[None] * normed, axis=-1, keepdims=True)
        message_cot = []
        for j in range(ENC_CHUNK):
            k = c * ENC_CHUNK + j
            scale = scale_ref[:, k : k + 1]
            message_cot.append((scale * (level - normed[j] * along[j])).astype(BF))
        message_cot = jnp.concatenate(message_cot, axis=0)
        message_cot_all[part, :] = message_cot
        before = before_ref[part, :].astype(F32)
        sig = sigma(before)
        silu = before * sig
        hidden_all[part, :] = silu.astype(BF)
        hidden_cot = dot_nt(message_cot, out_ref[...])
        before_cot = hidden_cot * (sig + silu * (1.0 - sig))
        before_cot_all[part, :] = before_cot.astype(BF)
        received_cot = received_cot + jnp.sum(before_cot.reshape(ENC_CHUNK, tile, width), axis=0)
    out_acc[...] += dot_tn(hidden_all[...], message_cot_all[...])
    received_cot = received_cot.astype(BF)
    recv_acc[...] += dot_tn(nodes, received_cot)
    mesh_grad_ref[...] = (node_cot + dot_nt(received_cot, recv_ref[...])).astype(BF)
    totals[...] += dot(onehot_t[...], before_cot_all[...])

    @pl.when(step == pl.num_programs(0) - 1)
    def _():
        out_grad_ref[...] = out_acc[...].astype(BF)
        recv_grad_ref[...] = recv_acc[...].astype(BF)
        band_cot_ref[...] = totals[...].astype(BF)
        at = 0
        send_grad = jnp.zeros((width, width), F32)
        for piece in (own_ref, high_ref, low_ref, left_ref, right_ref):
            count = piece.shape[0]
            send_grad = send_grad + dot_tn(piece[...], band_cot_ref[at : at + count, :])
            at += count
        send_grad_ref[...] = send_grad.astype(BF)


def enc_backward(idx_rows, scale, mesh_rows, moved_cot, before, normed, pieces, dec_send, enc_recv, enc_out):
    nodes, degree = scale.shape
    width = mesh_rows.shape[1]
    tile = ENC_TILE
    edges = tile * degree
    band_rows = sum(p.shape[0] for p in pieces)
    square = whole((width, width))
    return pl.pallas_call(
        enc_backward_kernel,
        name="enc_backward",
        grid=(nodes // tile,),
        in_specs=[
            pl.BlockSpec((1, 1, edges), lambda t: (t, 0, 0)),
            rows_of(tile, degree), rows_of(tile, width), rows_of(tile, width),
            rows_of(edges, width), rows_of(edges, width),
        ]
        + [whole(p.shape) for p in pieces]
        + [square] * 3,
        out_specs=[rows_of(tile, width), whole((band_rows, width)), square, square, square],
        out_shape=[
            jax.ShapeDtypeStruct((nodes, width), BF),
            jax.ShapeDtypeStruct((band_rows, width), BF),
            jax.ShapeDtypeStruct((width, width), BF),
            jax.ShapeDtypeStruct((width, width), BF),
            jax.ShapeDtypeStruct((width, width), BF),
        ],
        scratch_shapes=[
            pltpu.VMEM((band_rows, edges), BF),
            pltpu.VMEM((edges, width), BF),
            pltpu.VMEM((edges, width), BF),
            pltpu.VMEM((edges, width), BF),
            pltpu.VMEM((band_rows, width), F32),
            pltpu.VMEM((width, width), F32),
            pltpu.VMEM((width, width), F32),
        ],
        compiler_params=pltpu.CompilerParams(vmem_limit_bytes=VMEM_LIMIT),
    )(idx_rows, scale, mesh_rows, moved_cot, before, normed, *pieces, dec_send, enc_recv, enc_out)


def to_lon(shard, by):
    count = lax.axis_size("lon")
    return lax.ppermute(shard, "lon", [(i, (i + by) % count) for i in range(count)])


def to_lat(shard, by):
    count = lax.axis_size("lat")
    return lax.ppermute(shard, "lat", [(i, i + by) for i in range(count) if 0 <= i + by < count])


def summed_everywhere(stack):
    axes = ("lat", "lon")
    lon_count = lax.axis_size("lon")
    count = lax.axis_size("lat") * lon_count
    rows, width = stack.shape
    half = rows // 2
    core = lax.axis_index("lon") % 2
    swap = [(i, i ^ 1) for i in range(lon_count)]
    alike = [[i for i in range(count) if i % 2 == c] for c in range(2)]
    kept = lax.dynamic_slice_in_dim(stack, core * half, half, 0).astype(F32)
    given = lax.dynamic_slice_in_dim(stack, (1 - core) * half, half, 0)
    kept = kept + lax.ppermute(given, "lon", swap).astype(F32)
    parts = kept.astype(BF).reshape(count // 2, 2 * half // count, width)
    got = lax.all_to_all(parts, axes, 0, 0, axis_index_groups=alike, tiled=True)
    mine = jnp.sum(got.astype(F32), axis=0).astype(BF)
    spread = jnp.broadcast_to(mine[None], parts.shape)
    ours = lax.all_to_all(spread, axes, 0, 0, axis_index_groups=alike, tiled=True).reshape(half, width)
    theirs = lax.ppermute(ours, "lon", swap)
    first = jnp.where(core == 0, ours, theirs).astype(F32)
    second = jnp.where(core == 0, theirs, ours).astype(F32)
    return first, second


def on_device(
    grid, mesh_nodes, grid_cot, enc_send, enc_recv, enc_out, dec_send, dec_recv, dec_out,
    enc_src, enc_live, dec_src,
):
    lat_cells, lon_cells, width = grid.shape
    slots, degree = enc_src.shape[2:]
    lat_index = lax.axis_index("lat")
    lon_index = lax.axis_index("lon")
    lon_count = lax.axis_size("lon")
    lon_total = lon_cells * lon_count
    cells = lat_cells * lon_cells
    edge_rows = REACH * lon_cells
    tall = lat_cells + 2 * REACH

    grid_rows = grid.reshape(cells, width)
    mesh_rows = mesh_nodes.reshape(slots, width)
    high = to_lat(grid_rows[:edge_rows], -1)
    low = to_lat(grid_rows[cells - edge_rows :], 1)
    inner = jnp.concatenate([grid_rows, high, low], axis=0).reshape(tall, lon_cells, width)
    left = to_lon(inner[:, lon_cells - REACH :].reshape(tall * REACH, width), 1)
    right = to_lon(inner[:, :REACH].reshape(tall * REACH, width), -1)
    pieces = (grid_rows, high, low, left, right)

    source = enc_src.reshape(slots, degree)
    row = (source // lon_total - lat_index * lat_cells) % tall
    col = (source % lon_total - lon_index * lon_cells + REACH) % lon_total - REACH
    inner_rows = tall * lon_cells
    enc_idx = jnp.where(
        col < 0,
        inner_rows + row * REACH + col + REACH,
        jnp.where(
            col >= lon_cells,
            inner_rows + tall * REACH + row * REACH + col - lon_cells,
            row * lon_cells + col,
        ),
    )
    tiles = slots // ENC_TILE
    enc_idx_rows = enc_idx.reshape(tiles, ENC_TILE, degree).transpose(0, 2, 1)
    enc_idx_rows = enc_idx_rows.reshape(tiles, 1, ENC_TILE * degree)
    live = enc_live.reshape(slots, degree).astype(F32)

    picks = dec_src.reshape(3, cells).T
    owner = picks // slots
    owner_lat = (owner // lon_count - lat_index) % 3
    owner_lon = (owner % lon_count - lon_index + lon_count) % lon_count
    owner_lon = jnp.where(owner_lon == lon_count - 1, 1, owner_lon * 2)
    dec_idx = (owner_lon * 3 + owner_lat) * slots + picks % slots

    mesh_new, moved, before, normed, scale = enc_forward(
        enc_idx, live, mesh_rows, pieces, enc_send, enc_recv, enc_out, dec_send
    )

    above = to_lat(moved, -1)
    below = to_lat(moved, 1)
    centre = jnp.concatenate([moved, above, below], axis=0)
    west = to_lon(centre, 1)
    east = to_lon(centre, -1)
    grid_new, grid_part, dec_out_grad, dec_recv_grad, centre_tot, west_tot, east_tot = decoder(
        dec_idx, grid_rows, grid_cot.reshape(cells, width), centre, west, east, dec_recv, dec_out
    )
    from_east = to_lon(west_tot, -1)
    from_west = to_lon(east_tot, 1)
    column = centre_tot.astype(F32) + from_east.astype(F32) + from_west.astype(F32)
    from_below = to_lat(column[slots : 2 * slots].astype(BF), 1)
    from_above = to_lat(column[2 * slots :].astype(BF), -1)
    moved_cot = column[:slots] + from_below.astype(F32) + from_above.astype(F32)
    moved_cot = moved_cot.astype(BF)
    dec_send_grad = dot_tn(mesh_new, moved_cot).astype(BF)

    mesh_grad, band_cot, enc_send_grad, enc_recv_grad, enc_out_grad = enc_backward(
        enc_idx_rows, scale, mesh_rows, moved_cot, before, normed, pieces, dec_send, enc_recv, enc_out
    )
    enc_grads, dec_grads = summed_everywhere(
        jnp.concatenate(
            [enc_send_grad, enc_recv_grad, enc_out_grad, dec_send_grad, dec_recv_grad, dec_out_grad], axis=0
        )
    )

    side = tall * REACH
    from_right = to_lon(band_cot[inner_rows : inner_rows + side], -1)
    from_left = to_lon(band_cot[inner_rows + side :], 1)
    inner_cot = band_cot[:inner_rows].astype(F32).reshape(tall, lon_cells, width)
    inner_cot = inner_cot.at[:, lon_cells - REACH :].add(from_right.astype(F32).reshape(tall, REACH, width))
    inner_cot = inner_cot.at[:, :REACH].add(from_left.astype(F32).reshape(tall, REACH, width))
    inner_cot = inner_cot.reshape(inner_rows, width)
    from_low = to_lat(inner_cot[cells : cells + edge_rows].astype(BF), 1)
    from_high = to_lat(inner_cot[cells + edge_rows :].astype(BF), -1)
    sent_cot = inner_cot[:cells] + jnp.concatenate([from_low, from_high], axis=0).astype(F32)
    grid_grad = (grid_part + dot_nt(sent_cot.astype(BF), enc_send)).astype(BF)

    return (
        grid_new.reshape(grid.shape),
        grid_grad.reshape(grid.shape),
        mesh_grad.reshape(mesh_nodes.shape),
        enc_grads[:width],
        enc_grads[width : 2 * width],
        enc_grads[2 * width :],
        dec_grads[:width],
        dec_grads[width : 2 * width],
        dec_grads[2 * width :],
    )


def solution(mesh):
    node = P("lat", "lon", None)
    block = P("lat", "lon", None, None)
    placed = (
        node, block, node, P(), P(), P(), P(), P(), P(), block, block, P(None, "lat", "lon"),
    )
    return jax.shard_map(
        on_device,
        mesh=mesh,
        in_specs=placed,
        out_specs=(node, node, block, P(), P(), P(), P(), P(), P()),
        check_vma=False,
    )
```

```python
import jax
import jax.numpy as jnp
from jax import lax
from jax.experimental import pallas as pl
from jax.experimental.pallas import tpu as pltpu
from jax.sharding import PartitionSpec as P

REACH = 4
NORM_EPSILON = 1e-05
BF = jnp.bfloat16
F32 = jnp.float32
VMEM_LIMIT = 56 * 1024 * 1024
ENC_TILE = 32
ENC_CHUNK = 4
STRIP = 16
DEC_TILE = 256


def dot(a, b):
    return jnp.dot(a, b, preferred_element_type=F32)


def dot_nt(a, b):
    return lax.dot_general(a, b, (((1,), (1,)), ((), ())), preferred_element_type=F32)


def dot_tn(a, b):
    return lax.dot_general(a, b, (((0,), (0,)), ((), ())), preferred_element_type=F32)


def sigma(v):
    return 0.5 * jnp.tanh(0.5 * v) + 0.5


def normalise(message):
    centred = message - jnp.mean(message, axis=-1, keepdims=True)
    factor = lax.rsqrt(jnp.mean(centred * centred, axis=-1, keepdims=True) + NORM_EPSILON)
    return centred, factor


def one_hot(index, places):
    return jnp.where(index == places, BF(1.0), BF(0.0))


def places_of(shape, dim):
    return lax.broadcasted_iota(jnp.int32, shape, dim).astype(jnp.int16)


def staggered(stages, count):
    for i in range(count + len(stages) - 1):
        for d in range(len(stages) - 1, -1, -1):
            if 0 <= i - d < count:
                stages[d](i - d)


def kernel_params():
    return pltpu.CompilerParams(vmem_limit_bytes=VMEM_LIMIT)


def whole(shape):
    return pl.BlockSpec(shape, lambda t: (0,) * len(shape))


def rows_of(count, width):
    return pl.BlockSpec((count, width), lambda t: (t, 0))


def enc_forward_kernel(
    idx_ref, count_ref, mesh_ref, own_ref, high_ref, low_ref, left_ref, right_ref,
    send_ref, recv_ref, out_ref, dec_send_ref,
    new_ref, moved_ref, before_ref, normed_ref, scale_ref,
    band, onehot, received_all,
):
    step = pl.program_id(0)
    tile, degree = idx_ref.shape
    width = mesh_ref.shape[1]
    band_rows = band.shape[0]
    own = pl.ds(pl.multiple_of(step * tile, tile), tile)

    @pl.when(step == 0)
    def _():
        received_all[...] = dot(mesh_ref[...], recv_ref[...])
        at = 0
        for piece in (own_ref, high_ref, low_ref, left_ref, right_ref):
            count = piece.shape[0]
            band[at : at + count, :] = dot(piece[...], send_ref[...]).astype(BF)
            at += count

    places = places_of((tile, band_rows), 1)
    index = idx_ref[...].astype(jnp.int16)
    received = received_all[own, :]
    lane = lax.broadcasted_iota(jnp.int32, (tile, degree), 1)
    rows = ENC_CHUNK * tile
    state = {"total": jnp.zeros((tile, width), F32), "scales": jnp.zeros((tile, degree), F32)}
    held = {}

    def place(c):
        for k in range(c * ENC_CHUNK, (c + 1) * ENC_CHUNK):
            onehot[k * tile : (k + 1) * tile, :] = one_hot(index[:, k : k + 1], places)

    def gather(c):
        held["gathered", c] = dot(onehot[c * rows : (c + 1) * rows, :], band[...])

    def activate(c):
        before = held.pop(("gathered", c)).reshape(ENC_CHUNK, tile, width) + received[None]
        before_ref[c * rows : (c + 1) * rows, :] = before.reshape(rows, width).astype(BF)
        held["hidden", c] = (before * sigma(before)).reshape(rows, width).astype(BF)

    def project(c):
        held["message", c] = dot(held.pop(("hidden", c)), out_ref[...])

    def norm(c):
        centred, factor = normalise(held.pop(("message", c)))
        normed = (centred * factor).reshape(ENC_CHUNK, tile, width)
        normed_ref[c * rows : (c + 1) * rows, :] = normed.reshape(rows, width).astype(BF)
        factor = factor.reshape(ENC_CHUNK, tile, 1)
        for j in range(ENC_CHUNK):
            k = c * ENC_CHUNK + j
            live = jnp.where(count_ref[...] > k, 1.0, 0.0)
            state["total"] = state["total"] + normed[j] * live
            state["scales"] = jnp.where(lane == k, factor[j] * live, state["scales"])

    staggered([place, gather, activate, project, norm], degree // ENC_CHUNK)
    scale_ref[...] = state["scales"]
    nodes = mesh_ref[own, :].astype(F32)
    new_ref[own, :] = (nodes + degree ** (-0.5) * state["total"]).astype(BF)

    @pl.when(step == pl.num_programs(0) - 1)
    def _():
        moved_ref[...] = dot(new_ref[...], dec_send_ref[...]).astype(BF)


def enc_forward(idx, counts, mesh_rows, pieces, enc_send, enc_recv, enc_out, dec_send):
    nodes, degree = idx.shape
    width = mesh_rows.shape[1]
    tile = ENC_TILE
    edges = tile * degree
    band_rows = sum(p.shape[0] for p in pieces)
    square = whole((width, width))
    return pl.pallas_call(
        enc_forward_kernel,
        name="enc_forward",
        grid=(nodes // tile,),
        in_specs=[rows_of(tile, degree), rows_of(tile, 1), whole((nodes, width))]
        + [whole(p.shape) for p in pieces]
        + [square] * 4,
        out_specs=[
            whole((nodes, width)), whole((nodes, width)),
            rows_of(edges, width), rows_of(edges, width), rows_of(tile, degree),
        ],
        out_shape=[
            jax.ShapeDtypeStruct((nodes, width), BF),
            jax.ShapeDtypeStruct((nodes, width), BF),
            jax.ShapeDtypeStruct((nodes * degree, width), BF),
            jax.ShapeDtypeStruct((nodes * degree, width), BF),
            jax.ShapeDtypeStruct((nodes, degree), F32),
        ],
        scratch_shapes=[
            pltpu.VMEM((band_rows, width), BF),
            pltpu.VMEM((edges, band_rows), BF),
            pltpu.VMEM((nodes, width), F32),
        ],
        compiler_params=kernel_params(),
    )(idx, counts, mesh_rows, *pieces, enc_send, enc_recv, enc_out, dec_send)


def enc_between_kernel(scale_ref, before_ref, normed_ref, out_ref, turned_ref, slope_ref, hidden_ref, sum_ref):
    tile, degree = scale_ref.shape
    width = before_ref.shape[1]
    rows = ENC_CHUNK * tile
    scales = scale_ref[...]
    totals = [jnp.zeros((STRIP, width), F32)] * (tile // STRIP)
    for c in range(degree // ENC_CHUNK):
        part = slice(c * rows, (c + 1) * rows)
        turned = dot_nt(normed_ref[part, :], out_ref[...])
        for k in range(c * ENC_CHUNK, (c + 1) * ENC_CHUNK):
            for i in range(tile // STRIP):
                at = slice(k * tile + i * STRIP, k * tile + (i + 1) * STRIP)
                scale = scales[i * STRIP : (i + 1) * STRIP, k : k + 1]
                before = before_ref[at, :].astype(F32)
                sig = sigma(before)
                silu = before * sig
                slope_ref[at, :] = ((sig + silu * (1.0 - sig)) * scale).astype(BF)
                hidden = silu * scale
                totals[i] = totals[i] + hidden
                hidden_ref[at, :] = hidden.astype(BF)
        turned_ref[part, :] = turned.astype(BF)
    sum_ref[...] = jnp.concatenate(totals, axis=0).astype(BF)


def enc_between(scale, before, normed, enc_out):
    nodes, degree = scale.shape
    width = before.shape[1]
    tile = ENC_TILE
    edges = tile * degree
    per_edge = rows_of(edges, width)
    return pl.pallas_call(
        enc_between_kernel,
        name="enc_between",
        grid=(nodes // tile,),
        in_specs=[rows_of(tile, degree), per_edge, per_edge, whole((width, width))],
        out_specs=[per_edge, per_edge, per_edge, rows_of(tile, width)],
        out_shape=[jax.ShapeDtypeStruct(before.shape, BF)] * 3 + [jax.ShapeDtypeStruct((nodes, width), BF)],
        compiler_params=kernel_params(),
        cost_estimate=pl.CostEstimate(
            flops=2 * before.size * width, bytes_accessed=10 * before.size, transcendentals=before.size
        ),
    )(scale, before, normed, enc_out)


def decoder_kernel(
    idx_ref, idx_row_ref, grid_ref, cot_ref, centre_ref, left_ref, right_ref,
    recv_ref, out_ref,
    new_ref, hidden_ref, message_cot_ref, before_cot_ref, received_cot_ref, left_tot_ref, right_tot_ref,
    onehot, onehot_t, received_all, new_all, received_cot_all,
):
    nodes, width = grid_ref.shape
    degree = idx_ref.shape[1]
    third = centre_ref.shape[0]
    tile = DEC_TILE
    parts = nodes // tile
    index = idx_ref[...].astype(jnp.int16)
    places = places_of((tile, 3 * third), 1)
    held = {}

    received_all[...] = dot(grid_ref[...], recv_ref[...])

    def spot(i):
        h, j = divmod(i, degree)
        return j, slice(h * tile, (h + 1) * tile), slice(i * tile, (i + 1) * tile)

    def place(i):
        j, at, edges = spot(i)
        onehot[edges, :] = one_hot(index[at, j : j + 1], places)

    def gather(i):
        j, at, edges = spot(i)
        gathered = dot(onehot[edges, :third], centre_ref[...])
        gathered = gathered + dot(onehot[edges, third : 2 * third], left_ref[...])
        held["gathered", i] = gathered + dot(onehot[edges, 2 * third :], right_ref[...])

    def activate(i):
        j, at, edges = spot(i)
        before = held.pop(("gathered", i)) + received_all[at, :]
        sig = sigma(before)
        silu = before * sig
        hidden = silu.astype(BF)
        hidden_ref[edges, :] = hidden
        held["slope", i] = sig + silu * (1.0 - sig)
        held["message", i] = dot(hidden, out_ref[...])

    def norm(i):
        j, at, edges = spot(i)
        centred, factor = normalise(held.pop(("message", i)))
        normed = centred * factor
        cot = cot_ref[at, :].astype(F32)
        level = cot - jnp.mean(cot, axis=-1, keepdims=True)
        along = jnp.mean(cot * normed, axis=-1, keepdims=True)
        message_cot = (factor * (level - normed * along)).astype(BF)
        message_cot_ref[edges, :] = message_cot
        held["hidden_cot", i] = dot_nt(message_cot, out_ref[...])
        if j == 0:
            new_all[at, :] = grid_ref[at, :].astype(F32) + normed
        else:
            new_all[at, :] += normed

    def back(i):
        j, at, edges = spot(i)
        before_cot = held.pop(("hidden_cot", i)) * held.pop(("slope", i))
        before_cot_ref[edges, :] = before_cot.astype(BF)
        if j == 0:
            received_cot_all[at, :] = before_cot
        else:
            received_cot_all[at, :] += before_cot
        rows = lax.broadcasted_iota(jnp.int32, (2 * third, tile), 0) + third
        picks = jnp.broadcast_to(idx_row_ref[j : j + 1, at], (16, tile)).astype(jnp.int16)[:1]
        onehot_t[:, edges] = one_hot(picks, rows.astype(jnp.int16))

    staggered([place, gather, activate, norm, back], degree * parts)
    left_tot_ref[...] = dot(onehot_t[:third, :], before_cot_ref[...]).astype(BF)
    new_ref[...] = new_all[...].astype(BF)
    right_tot_ref[...] = dot(onehot_t[third:, :], before_cot_ref[...]).astype(BF)
    received_cot_ref[...] = received_cot_all[...].astype(BF)


def decoder(idx, idx_rows, grid_rows, cot_rows, centre, left, right, dec_recv, dec_out):
    nodes, width = grid_rows.shape
    degree = idx.shape[1]
    third = centre.shape[0]
    edge_shape = jax.ShapeDtypeStruct((degree * nodes, width), BF)
    node_shape = jax.ShapeDtypeStruct((nodes, width), BF)
    side_shape = jax.ShapeDtypeStruct((third, width), BF)
    return pl.pallas_call(
        decoder_kernel,
        name="decoder",
        out_shape=[node_shape, edge_shape, edge_shape, edge_shape, node_shape, side_shape, side_shape],
        scratch_shapes=[
            pltpu.VMEM((degree * nodes, 3 * third), BF),
            pltpu.VMEM((2 * third, degree * nodes), BF),
            pltpu.VMEM((nodes, width), F32),
            pltpu.VMEM((nodes, width), F32),
            pltpu.VMEM((nodes, width), F32),
        ],
        compiler_params=kernel_params(),
    )(idx, idx_rows, grid_rows, cot_rows, centre, left, right, dec_recv, dec_out)


def decoder_rest_kernel(
    idx_row_ref, grid_ref, cot_ref, hidden_ref, message_cot_ref, before_cot_ref, received_cot_ref, recv_ref,
    part_ref, out_grad_ref, recv_grad_ref, centre_tot_ref,
    onehot_t,
):
    third, width = centre_tot_ref.shape
    degree, nodes = idx_row_ref.shape
    tile = DEC_TILE
    rows = places_of((third, tile), 0)
    for i in range(degree * nodes // tile):
        h, j = divmod(i, degree)
        picks = jnp.broadcast_to(idx_row_ref[j : j + 1, h * tile : (h + 1) * tile], (16, tile))
        onehot_t[:, i * tile : (i + 1) * tile] = one_hot(picks.astype(jnp.int16)[:1], rows)
    centre_tot_ref[...] = dot(onehot_t[...], before_cot_ref[...]).astype(BF)
    out_grad_ref[...] = dot_tn(hidden_ref[...], message_cot_ref[...]).astype(BF)
    received_cot = received_cot_ref[...]
    recv_grad_ref[...] = dot_tn(grid_ref[...], received_cot).astype(BF)
    part_ref[...] = cot_ref[...].astype(F32) + dot_nt(received_cot, recv_ref[...])


def decoder_rest(idx_rows, grid_rows, cot_rows, hidden, message_cot, before_cot, received_cot, dec_recv, third):
    degree, nodes = idx_rows.shape
    width = hidden.shape[1]
    return pl.pallas_call(
        decoder_rest_kernel,
        name="decoder_rest",
        out_shape=[
            jax.ShapeDtypeStruct((nodes, width), F32),
            jax.ShapeDtypeStruct((width, width), BF),
            jax.ShapeDtypeStruct((width, width), BF),
            jax.ShapeDtypeStruct((third, width), BF),
        ],
        scratch_shapes=[pltpu.VMEM((third, degree * nodes), BF)],
        compiler_params=kernel_params(),
        cost_estimate=pl.CostEstimate(
            flops=2 * degree * nodes * width * (third + 2 * width), bytes_accessed=8 * degree * nodes * width,
            transcendentals=0,
        ),
    )(idx_rows, grid_rows, cot_rows, hidden, message_cot, before_cot, received_cot, dec_recv)


def enc_backward_kernel(
    idx_row_ref, mesh_ref, moved_cot_ref, sum_ref, normed_ref, turned_ref, slope_ref, hidden_ref,
    own_ref, high_ref, low_ref, left_ref, right_ref,
    dec_send_ref, recv_ref, out_ref,
    mesh_grad_ref, band_cot_ref, grads_ref,
    onehot_t0, onehot_t1, cot0, cot1, weighted, totals, out_acc, node_cot, turned_level, received_cot,
):
    step = pl.program_id(0)
    nodes, width = mesh_ref.shape
    edges = normed_ref.shape[0]
    band_rows = totals.shape[0]
    tiles = pl.num_programs(0) - 1
    tile = ENC_TILE
    degree = edges // tile
    scaling = degree ** (-0.5)
    cots = (cot0, cot1)
    onehots = (onehot_t0, onehot_t1)

    @pl.when(step == 0)
    def _():
        totals[...] = jnp.zeros_like(totals)
        cot = dot_nt(moved_cot_ref[...], dec_send_ref[...])
        node_cot[...] = cot
        spread = scaling * cot
        level = (spread - jnp.mean(spread, axis=-1, keepdims=True)).astype(BF)
        turned_level[...] = dot_nt(level, out_ref[...])
        out_acc[...] = dot_tn(sum_ref[...], level)

    def scatter(slot, n):
        half = width // 2
        at = slice(n * half, (n + 1) * half)
        totals[:, at] += dot(onehots[slot][...], cots[slot][:, at])

    def edge_part(slot, beside):
        strips = tile // STRIP
        total = [jnp.zeros((STRIP, width), F32)] * strips
        for n in range(2):
            if beside is not None:
                scatter(beside, n)
            for k in range(n * degree // 2, (n + 1) * degree // 2):
                for i in range(strips):
                    at = slice(k * tile + i * STRIP, k * tile + (i + 1) * STRIP)
                    mine = pl.ds(pl.multiple_of(step * tile + i * STRIP, STRIP), STRIP)
                    spread = scaling * node_cot[mine, :]
                    along = jnp.mean(spread * normed_ref[at, :].astype(F32), axis=-1, keepdims=True)
                    turned = turned_level[mine, :] - along * turned_ref[at, :].astype(F32)
                    before_cot = slope_ref[at, :].astype(F32) * turned
                    total[i] = total[i] + before_cot
                    cots[slot][at, :] = before_cot.astype(BF)
                    weighted[at, :] = (hidden_ref[at, :].astype(F32) * (-along)).astype(BF)
            part = slice(n * edges // 2, (n + 1) * edges // 2)
            out_acc[...] += dot_tn(weighted[part, :], normed_ref[part, :])
        places = places_of((band_rows, edges), 0)
        spot = jnp.broadcast_to(idx_row_ref[0], (16, edges)).astype(jnp.int16)[:1]
        onehots[slot][...] = one_hot(spot, places)
        received_cot[pl.ds(pl.multiple_of(step * tile, tile), tile), :] = jnp.concatenate(total, axis=0).astype(BF)

    @pl.when(step == 0)
    def _():
        edge_part(0, None)

    for parity in range(2):
        @pl.when((step > 0) & (step < tiles) & (step % 2 == parity))
        def _():
            edge_part(parity, 1 - parity)

    @pl.when(step == tiles)
    def _():
        scatter(1, 0)
        scatter(1, 1)
        grads_ref[width : 2 * width, :] = dot_tn(mesh_ref[...], received_cot[...]).astype(BF)
        grads_ref[2 * width :, :] = out_acc[...].astype(BF)
        mesh_grad_ref[...] = (node_cot[...] + dot_nt(received_cot[...], recv_ref[...])).astype(BF)
        band_cot_ref[...] = totals[...].astype(BF)
        at = 0
        send_grad = jnp.zeros((width, width), F32)
        for piece in (own_ref, high_ref, low_ref, left_ref, right_ref):
            count = piece.shape[0]
            send_grad = send_grad + dot_tn(piece[...], band_cot_ref[at : at + count, :])
            at += count
        grads_ref[:width, :] = send_grad.astype(BF)


def enc_backward(idx_rows, mesh_rows, moved_cot, sums, normed, turned, slope, hidden, pieces, dec_send, enc_recv, enc_out):
    nodes, width = mesh_rows.shape
    tile = ENC_TILE
    tiles = nodes // tile
    assert tiles % 2 == 0
    edges = normed.shape[0] // tiles
    band_rows = sum(p.shape[0] for p in pieces)
    square = whole((width, width))
    last = tiles - 1
    per_node = whole((nodes, width))
    per_edge = pl.BlockSpec((edges, width), lambda t: (jnp.minimum(t, last), 0))
    return pl.pallas_call(
        enc_backward_kernel,
        name="enc_backward",
        grid=(tiles + 1,),
        in_specs=[pl.BlockSpec((1, 1, edges), lambda t: (jnp.minimum(t, last), 0, 0))]
        + [per_node] * 3
        + [per_edge] * 4
        + [whole(p.shape) for p in pieces]
        + [square] * 3,
        out_specs=[per_node, whole((band_rows, width)), whole((3 * width, width))],
        out_shape=[
            jax.ShapeDtypeStruct((nodes, width), BF),
            jax.ShapeDtypeStruct((band_rows, width), BF),
            jax.ShapeDtypeStruct((3 * width, width), BF),
        ],
        scratch_shapes=[
            pltpu.VMEM((band_rows, edges), BF),
            pltpu.VMEM((band_rows, edges), BF),
            pltpu.VMEM((edges, width), BF),
            pltpu.VMEM((edges, width), BF),
            pltpu.VMEM((edges, width), BF),
            pltpu.VMEM((band_rows, width), F32),
            pltpu.VMEM((width, width), F32),
            pltpu.VMEM((nodes, width), F32),
            pltpu.VMEM((nodes, width), F32),
            pltpu.VMEM((nodes, width), BF),
        ],
        compiler_params=kernel_params(),
    )(idx_rows, mesh_rows, moved_cot, sums, normed, turned, slope, hidden, *pieces, dec_send, enc_recv, enc_out)


def to_lon(shard, by):
    count = lax.axis_size("lon")
    return lax.ppermute(shard, "lon", [(i, (i + by) % count) for i in range(count)])


def to_lat(shard, by):
    count = lax.axis_size("lat")
    return lax.ppermute(shard, "lat", [(i, i + by) for i in range(count) if 0 <= i + by < count])


def summed_everywhere(first, second):
    axes = ("lat", "lon")
    lon_count = lax.axis_size("lon")
    count = lax.axis_size("lat") * lon_count
    rows, width = first.shape
    leads = lax.axis_index("lon") % 2 == 0
    swap = [(i, i ^ 1) for i in range(lon_count)]
    alike = [[i for i in range(count) if i % 2 == c] for c in range(2)]
    given = jnp.where(leads, second, first)
    kept = jnp.where(leads, first, second).astype(F32) + lax.ppermute(given, "lon", swap).astype(F32)
    parts = kept.astype(BF).reshape(count // 2, 2 * rows // count, width)
    got = lax.all_to_all(parts, axes, 0, 0, axis_index_groups=alike, tiled=True)
    mine = jnp.sum(got.astype(F32), axis=0).astype(BF)
    spread = jnp.broadcast_to(mine[None], parts.shape)
    ours = lax.all_to_all(spread, axes, 0, 0, axis_index_groups=alike, tiled=True).reshape(rows, width)
    theirs = lax.ppermute(ours, "lon", swap)
    return jnp.where(leads, ours, theirs).astype(F32), jnp.where(leads, theirs, ours).astype(F32)


def on_device(
    grid, mesh_nodes, grid_cot, enc_send, enc_recv, enc_out, dec_send, dec_recv, dec_out,
    enc_src, enc_live, dec_src,
):
    lat_cells, lon_cells, width = grid.shape
    slots, degree = enc_src.shape[2:]
    lat_index = lax.axis_index("lat")
    lon_index = lax.axis_index("lon")
    lon_count = lax.axis_size("lon")
    lon_total = lon_cells * lon_count
    cells = lat_cells * lon_cells
    edge_rows = REACH * lon_cells
    tall = lat_cells + 2 * REACH

    grid_rows = grid.reshape(cells, width)
    mesh_rows = mesh_nodes.reshape(slots, width)
    high = to_lat(grid_rows[:edge_rows], -1)
    low = to_lat(grid_rows[cells - edge_rows :], 1)
    inner = jnp.concatenate([grid_rows, high, low], axis=0).reshape(tall, lon_cells, width)
    left = to_lon(inner[:, lon_cells - REACH :].reshape(tall * REACH, width), 1)
    right = to_lon(inner[:, :REACH].reshape(tall * REACH, width), -1)
    pieces = (grid_rows, high, low, left, right)

    source = enc_src.reshape(slots, degree)
    row = (source // lon_total - lat_index * lat_cells) % tall
    col = (source % lon_total - lon_index * lon_cells + REACH) % lon_total - REACH
    inner_rows = tall * lon_cells
    enc_idx = jnp.where(
        col < 0,
        inner_rows + row * REACH + col + REACH,
        jnp.where(
            col >= lon_cells,
            inner_rows + tall * REACH + row * REACH + col - lon_cells,
            row * lon_cells + col,
        ),
    )
    tiles = slots // ENC_TILE
    enc_idx_rows = enc_idx.reshape(tiles, ENC_TILE, degree).transpose(0, 2, 1)
    enc_idx_rows = enc_idx_rows.reshape(tiles, 1, ENC_TILE * degree)
    counts = jnp.sum(enc_live.reshape(slots, degree), axis=1, keepdims=True)

    picks = dec_src.reshape(3, cells)
    owner = picks // slots
    owner_lat = (owner // lon_count - lat_index) % 3
    owner_lon = (owner % lon_count - lon_index + lon_count) % lon_count
    owner_lon = jnp.where(owner_lon == lon_count - 1, 1, owner_lon * 2)
    dec_idx_rows = (owner_lon * 3 + owner_lat) * slots + picks % slots

    mesh_new, moved, before, normed, scale = enc_forward(
        enc_idx, counts, mesh_rows, pieces, enc_send, enc_recv, enc_out, dec_send
    )

    above = to_lat(moved, -1)
    below = to_lat(moved, 1)
    turned, slope, hidden, sums = enc_between(scale, before, normed, enc_out)
    centre = jnp.concatenate([moved, above, below], axis=0)
    west = to_lon(centre, 1)
    east = to_lon(centre, -1)
    cot_rows = grid_cot.reshape(cells, width)
    grid_new, dec_hidden, dec_message_cot, dec_before_cot, dec_received_cot, west_tot, east_tot = decoder(
        dec_idx_rows.T, dec_idx_rows, grid_rows, cot_rows, centre, west, east, dec_recv, dec_out
    )
    from_east = to_lon(west_tot, -1)
    from_west = to_lon(east_tot, 1)
    grid_part, dec_out_grad, dec_recv_grad, centre_tot = decoder_rest(
        dec_idx_rows, grid_rows, cot_rows, dec_hidden, dec_message_cot, dec_before_cot, dec_received_cot,
        dec_recv, 3 * slots,
    )
    column = centre_tot.astype(F32) + from_east.astype(F32) + from_west.astype(F32)
    from_below = to_lat(column[slots : 2 * slots].astype(BF), 1)
    from_above = to_lat(column[2 * slots :].astype(BF), -1)
    moved_cot = column[:slots] + from_below.astype(F32) + from_above.astype(F32)
    moved_cot = moved_cot.astype(BF)
    dec_send_grad = dot_tn(mesh_new, moved_cot).astype(BF)

    mesh_grad, band_cot, enc_stack = enc_backward(
        enc_idx_rows, mesh_rows, moved_cot, sums, normed, turned, slope, hidden, pieces, dec_send, enc_recv, enc_out
    )
    dec_stack = jnp.concatenate([dec_send_grad, dec_recv_grad, dec_out_grad], axis=0)
    enc_grads, dec_grads = summed_everywhere(enc_stack, dec_stack)

    side = tall * REACH
    from_right = to_lon(band_cot[inner_rows : inner_rows + side], -1)
    from_left = to_lon(band_cot[inner_rows + side :], 1)
    inner_cot = band_cot[:inner_rows].astype(F32).reshape(tall, lon_cells, width)
    inner_cot = inner_cot.at[:, lon_cells - REACH :].add(from_right.astype(F32).reshape(tall, REACH, width))
    inner_cot = inner_cot.at[:, :REACH].add(from_left.astype(F32).reshape(tall, REACH, width))
    inner_cot = inner_cot.reshape(inner_rows, width)
    from_low = to_lat(inner_cot[cells : cells + edge_rows].astype(BF), 1)
    from_high = to_lat(inner_cot[cells + edge_rows :].astype(BF), -1)
    sent_cot = inner_cot[:cells] + jnp.concatenate([from_low, from_high], axis=0).astype(F32)
    grid_grad = (grid_part + dot_nt(sent_cot.astype(BF), enc_send)).astype(BF)

    return (
        grid_new.reshape(grid.shape),
        grid_grad.reshape(grid.shape),
        mesh_grad.reshape(mesh_nodes.shape),
        enc_grads[:width],
        enc_grads[width : 2 * width],
        enc_grads[2 * width :],
        dec_grads[:width],
        dec_grads[width : 2 * width],
        dec_grads[2 * width :],
    )


def solution(mesh):
    node = P("lat", "lon", None)
    block = P("lat", "lon", None, None)
    placed = (
        node, block, node, P(), P(), P(), P(), P(), P(), block, block, P(None, "lat", "lon"),
    )
    return jax.shard_map(
        on_device,
        mesh=mesh,
        in_specs=placed,
        out_specs=(node, node, block, P(), P(), P(), P(), P(), P()),
        check_vma=False,
    )
```

```python
import jax
import jax.numpy as jnp
from jax import lax
from jax.experimental import pallas as pl
from jax.experimental.pallas import tpu as pltpu
from jax.sharding import PartitionSpec as P

REACH = 4
NORM_EPSILON = 1e-05
BF = jnp.bfloat16
F32 = jnp.float32
VMEM_LIMIT = 56 * 1024 * 1024
ENC_TILE = 32
ENC_CHUNK = 4
STRIP = 16
DEC_TILE = 256


def dot(a, b):
    return jnp.dot(a, b, preferred_element_type=F32)


def dot_nt(a, b):
    return lax.dot_general(a, b, (((1,), (1,)), ((), ())), preferred_element_type=F32)


def dot_tn(a, b):
    return lax.dot_general(a, b, (((0,), (0,)), ((), ())), preferred_element_type=F32)


def sigma(v):
    return 0.5 * jnp.tanh(0.5 * v) + 0.5


def normalise(message):
    centred = message - jnp.mean(message, axis=-1, keepdims=True)
    factor = lax.rsqrt(jnp.mean(centred * centred, axis=-1, keepdims=True) + NORM_EPSILON)
    return centred, factor


def one_hot(index, places):
    return jnp.where(index == places, BF(1.0), BF(0.0))


def places_of(shape, dim):
    return lax.broadcasted_iota(jnp.int32, shape, dim).astype(jnp.int16)


def staggered(stages, count):
    for i in range(count + len(stages) - 1):
        for d in range(len(stages) - 1, -1, -1):
            if 0 <= i - d < count:
                stages[d](i - d)


def kernel_params():
    return pltpu.CompilerParams(vmem_limit_bytes=VMEM_LIMIT)


def whole(shape):
    return pl.BlockSpec(shape, lambda t: (0,) * len(shape))


def rows_of(count, width):
    return pl.BlockSpec((count, width), lambda t: (t, 0))


def enc_forward_kernel(
    idx_ref, count_ref, mesh_ref, own_ref, high_ref, low_ref, left_ref, right_ref,
    send_ref, recv_ref, out_ref, dec_send_ref,
    new_ref, moved_ref, before_ref, normed_ref, scale_ref,
    band, onehot, received_all,
):
    step = pl.program_id(0)
    tile, degree = idx_ref.shape
    width = mesh_ref.shape[1]
    band_rows = band.shape[0]
    own = pl.ds(pl.multiple_of(step * tile, tile), tile)

    @pl.when(step == 0)
    def _():
        received_all[...] = dot(mesh_ref[...], recv_ref[...])
        at = 0
        for piece in (own_ref, high_ref, low_ref, left_ref, right_ref):
            count = piece.shape[0]
            band[at : at + count, :] = dot(piece[...], send_ref[...]).astype(BF)
            at += count

    places = places_of((tile, band_rows), 1)
    index = idx_ref[...].astype(jnp.int16)
    received = received_all[own, :]
    lane = lax.broadcasted_iota(jnp.int32, (tile, degree), 1)
    rows = ENC_CHUNK * tile
    state = {"total": jnp.zeros((tile, width), F32), "scales": jnp.zeros((tile, degree), F32)}
    held = {}

    def place(c):
        for k in range(c * ENC_CHUNK, (c + 1) * ENC_CHUNK):
            onehot[k * tile : (k + 1) * tile, :] = one_hot(index[:, k : k + 1], places)

    def gather(c):
        held["gathered", c] = dot(onehot[c * rows : (c + 1) * rows, :], band[...])

    def activate(c):
        before = held.pop(("gathered", c)).reshape(ENC_CHUNK, tile, width) + received[None]
        before_ref[c * rows : (c + 1) * rows, :] = before.reshape(rows, width).astype(BF)
        held["hidden", c] = (before * sigma(before)).reshape(rows, width).astype(BF)

    def project(c):
        held["message", c] = dot(held.pop(("hidden", c)), out_ref[...])

    def norm(c):
        centred, factor = normalise(held.pop(("message", c)))
        normed = (centred * factor).reshape(ENC_CHUNK, tile, width)
        normed_ref[c * rows : (c + 1) * rows, :] = normed.reshape(rows, width).astype(BF)
        factor = factor.reshape(ENC_CHUNK, tile, 1)
        for j in range(ENC_CHUNK):
            k = c * ENC_CHUNK + j
            live = jnp.where(count_ref[...] > k, 1.0, 0.0)
            state["total"] = state["total"] + normed[j] * live
            state["scales"] = jnp.where(lane == k, factor[j] * live, state["scales"])

    staggered([place, gather, activate, project, norm], degree // ENC_CHUNK)
    scale_ref[...] = state["scales"]
    nodes = mesh_ref[own, :].astype(F32)
    new_ref[own, :] = (nodes + degree ** (-0.5) * state["total"]).astype(BF)

    @pl.when(step == pl.num_programs(0) - 1)
    def _():
        moved_ref[...] = dot(new_ref[...], dec_send_ref[...]).astype(BF)


def enc_forward(idx, counts, mesh_rows, pieces, enc_send, enc_recv, enc_out, dec_send):
    nodes, degree = idx.shape
    width = mesh_rows.shape[1]
    tile = ENC_TILE
    edges = tile * degree
    band_rows = sum(p.shape[0] for p in pieces)
    square = whole((width, width))
    return pl.pallas_call(
        enc_forward_kernel,
        name="enc_forward",
        grid=(nodes // tile,),
        in_specs=[rows_of(tile, degree), rows_of(tile, 1), whole((nodes, width))]
        + [whole(p.shape) for p in pieces]
        + [square] * 4,
        out_specs=[
            whole((nodes, width)), whole((nodes, width)),
            rows_of(edges, width), rows_of(edges, width), rows_of(tile, degree),
        ],
        out_shape=[
            jax.ShapeDtypeStruct((nodes, width), BF),
            jax.ShapeDtypeStruct((nodes, width), BF),
            jax.ShapeDtypeStruct((nodes * degree, width), BF),
            jax.ShapeDtypeStruct((nodes * degree, width), BF),
            jax.ShapeDtypeStruct((nodes, degree), F32),
        ],
        scratch_shapes=[
            pltpu.VMEM((band_rows, width), BF),
            pltpu.VMEM((edges, band_rows), BF),
            pltpu.VMEM((nodes, width), F32),
        ],
        compiler_params=kernel_params(),
    )(idx, counts, mesh_rows, *pieces, enc_send, enc_recv, enc_out, dec_send)


def enc_between_kernel(scale_ref, before_ref, normed_ref, out_ref, turned_ref, slope_ref, hidden_ref, sum_ref):
    tile, degree = scale_ref.shape
    width = before_ref.shape[1]
    rows = ENC_CHUNK * tile
    scales = scale_ref[...]
    totals = [jnp.zeros((STRIP, width), F32)] * (tile // STRIP)
    for c in range(degree // ENC_CHUNK):
        part = slice(c * rows, (c + 1) * rows)
        turned = dot_nt(normed_ref[part, :], out_ref[...])
        for k in range(c * ENC_CHUNK, (c + 1) * ENC_CHUNK):
            for i in range(tile // STRIP):
                at = slice(k * tile + i * STRIP, k * tile + (i + 1) * STRIP)
                scale = scales[i * STRIP : (i + 1) * STRIP, k : k + 1]
                before = before_ref[at, :].astype(F32)
                sig = sigma(before)
                silu = before * sig
                slope_ref[at, :] = ((sig + silu * (1.0 - sig)) * scale).astype(BF)
                hidden = silu * scale
                totals[i] = totals[i] + hidden
                hidden_ref[at, :] = hidden.astype(BF)
        turned_ref[part, :] = turned.astype(BF)
    sum_ref[...] = jnp.concatenate(totals, axis=0).astype(BF)


def enc_between(scale, before, normed, enc_out, first, count, done=None):
    nodes, degree = scale.shape
    width = before.shape[1]
    tile = ENC_TILE
    edges = tile * degree
    per_edge = pl.BlockSpec((edges, width), lambda t: (t + first, 0))
    per_node = pl.BlockSpec((tile, width), lambda t: (t + first, 0))
    share = count * edges * width
    kept = () if done is None else tuple(done)
    return pl.pallas_call(
        enc_between_kernel if done is None else enc_between_more_kernel,
        name="enc_between",
        grid=(count,),
        in_specs=[
            pl.BlockSpec((tile, degree), lambda t: (t + first, 0)), per_edge, per_edge, whole((width, width)),
        ]
        + [pl.BlockSpec(memory_space=pl.ANY)] * len(kept),
        out_specs=[per_edge, per_edge, per_edge, per_node],
        out_shape=[jax.ShapeDtypeStruct(before.shape, BF)] * 3 + [jax.ShapeDtypeStruct((nodes, width), BF)],
        input_output_aliases={4 + i: i for i in range(len(kept))},
        compiler_params=kernel_params(),
        cost_estimate=pl.CostEstimate(flops=2 * share * width, bytes_accessed=10 * share, transcendentals=share),
    )(scale, before, normed, enc_out, *kept)


def enc_between_more_kernel(scale_ref, before_ref, normed_ref, out_ref, d0, d1, d2, d3, *outs):
    enc_between_kernel(scale_ref, before_ref, normed_ref, out_ref, *outs)


def decoder_kernel(
    idx_ref, idx_row_ref, grid_ref, cot_ref, centre_ref, left_ref, right_ref,
    recv_ref, out_ref,
    new_ref, hidden_ref, message_cot_ref, before_cot_ref, received_cot_ref, left_tot_ref, right_tot_ref,
    onehot, onehot_t, received_all, new_all, received_cot_all,
):
    nodes, width = grid_ref.shape
    degree = idx_ref.shape[1]
    third = centre_ref.shape[0]
    tile = DEC_TILE
    parts = nodes // tile
    index = idx_ref[...].astype(jnp.int16)
    places = places_of((tile, 3 * third), 1)
    held = {}

    received_all[...] = dot(grid_ref[...], recv_ref[...])

    def spot(i):
        h, j = divmod(i, degree)
        return j, slice(h * tile, (h + 1) * tile), slice(i * tile, (i + 1) * tile)

    def place(i):
        j, at, edges = spot(i)
        onehot[edges, :] = one_hot(index[at, j : j + 1], places)

    def gather(i):
        j, at, edges = spot(i)
        gathered = dot(onehot[edges, :third], centre_ref[...])
        gathered = gathered + dot(onehot[edges, third : 2 * third], left_ref[...])
        held["gathered", i] = gathered + dot(onehot[edges, 2 * third :], right_ref[...])

    def activate(i):
        j, at, edges = spot(i)
        before = held.pop(("gathered", i)) + received_all[at, :]
        sig = sigma(before)
        silu = before * sig
        hidden = silu.astype(BF)
        hidden_ref[edges, :] = hidden
        held["slope", i] = sig + silu * (1.0 - sig)
        held["message", i] = dot(hidden, out_ref[...])

    def norm(i):
        j, at, edges = spot(i)
        centred, factor = normalise(held.pop(("message", i)))
        normed = centred * factor
        cot = cot_ref[at, :].astype(F32)
        level = cot - jnp.mean(cot, axis=-1, keepdims=True)
        along = jnp.mean(cot * normed, axis=-1, keepdims=True)
        message_cot = (factor * (level - normed * along)).astype(BF)
        message_cot_ref[edges, :] = message_cot
        held["hidden_cot", i] = dot_nt(message_cot, out_ref[...])
        if j == 0:
            new_all[at, :] = grid_ref[at, :].astype(F32) + normed
        else:
            new_all[at, :] += normed

    def back(i):
        j, at, edges = spot(i)
        before_cot = held.pop(("hidden_cot", i)) * held.pop(("slope", i))
        before_cot_ref[edges, :] = before_cot.astype(BF)
        if j == 0:
            received_cot_all[at, :] = before_cot
        else:
            received_cot_all[at, :] += before_cot
        rows = lax.broadcasted_iota(jnp.int32, (2 * third, tile), 0) + third
        picks = jnp.broadcast_to(idx_row_ref[j : j + 1, at], (16, tile)).astype(jnp.int16)[:1]
        onehot_t[:, edges] = one_hot(picks, rows.astype(jnp.int16))

    staggered([place, gather, activate, norm, back], degree * parts)
    left_tot_ref[...] = dot(onehot_t[:third, :], before_cot_ref[...]).astype(BF)
    new_ref[...] = new_all[...].astype(BF)
    right_tot_ref[...] = dot(onehot_t[third:, :], before_cot_ref[...]).astype(BF)
    received_cot_ref[...] = received_cot_all[...].astype(BF)


def decoder(idx, idx_rows, grid_rows, cot_rows, centre, left, right, dec_recv, dec_out):
    nodes, width = grid_rows.shape
    degree = idx.shape[1]
    third = centre.shape[0]
    edge_shape = jax.ShapeDtypeStruct((degree * nodes, width), BF)
    node_shape = jax.ShapeDtypeStruct((nodes, width), BF)
    side_shape = jax.ShapeDtypeStruct((third, width), BF)
    return pl.pallas_call(
        decoder_kernel,
        name="decoder",
        out_shape=[node_shape, edge_shape, edge_shape, edge_shape, node_shape, side_shape, side_shape],
        scratch_shapes=[
            pltpu.VMEM((degree * nodes, 3 * third), BF),
            pltpu.VMEM((2 * third, degree * nodes), BF),
            pltpu.VMEM((nodes, width), F32),
            pltpu.VMEM((nodes, width), F32),
            pltpu.VMEM((nodes, width), F32),
        ],
        compiler_params=kernel_params(),
    )(idx, idx_rows, grid_rows, cot_rows, centre, left, right, dec_recv, dec_out)


def decoder_rest_kernel(
    idx_row_ref, grid_ref, cot_ref, hidden_ref, message_cot_ref, before_cot_ref, received_cot_ref, recv_ref,
    part_ref, out_grad_ref, recv_grad_ref, centre_tot_ref,
    onehot_t,
):
    third, width = centre_tot_ref.shape
    degree, nodes = idx_row_ref.shape
    tile = DEC_TILE
    rows = places_of((third, tile), 0)
    for i in range(degree * nodes // tile):
        h, j = divmod(i, degree)
        picks = jnp.broadcast_to(idx_row_ref[j : j + 1, h * tile : (h + 1) * tile], (16, tile))
        onehot_t[:, i * tile : (i + 1) * tile] = one_hot(picks.astype(jnp.int16)[:1], rows)
    centre_tot_ref[...] = dot(onehot_t[...], before_cot_ref[...]).astype(BF)
    out_grad_ref[...] = dot_tn(hidden_ref[...], message_cot_ref[...]).astype(BF)
    received_cot = received_cot_ref[...]
    recv_grad_ref[...] = dot_tn(grid_ref[...], received_cot).astype(BF)
    part_ref[...] = cot_ref[...].astype(F32) + dot_nt(received_cot, recv_ref[...])


def decoder_rest(idx_rows, grid_rows, cot_rows, hidden, message_cot, before_cot, received_cot, dec_recv, third):
    degree, nodes = idx_rows.shape
    width = hidden.shape[1]
    return pl.pallas_call(
        decoder_rest_kernel,
        name="decoder_rest",
        out_shape=[
            jax.ShapeDtypeStruct((nodes, width), F32),
            jax.ShapeDtypeStruct((width, width), BF),
            jax.ShapeDtypeStruct((width, width), BF),
            jax.ShapeDtypeStruct((third, width), BF),
        ],
        scratch_shapes=[pltpu.VMEM((third, degree * nodes), BF)],
        compiler_params=kernel_params(),
        cost_estimate=pl.CostEstimate(
            flops=2 * degree * nodes * width * (third + 2 * width), bytes_accessed=8 * degree * nodes * width,
            transcendentals=0,
        ),
    )(idx_rows, grid_rows, cot_rows, hidden, message_cot, before_cot, received_cot, dec_recv)


def enc_backward_kernel(
    idx_row_ref, mesh_ref, moved_cot_ref, sum_ref, normed_ref, turned_ref, slope_ref, hidden_ref,
    own_ref, high_ref, low_ref, left_ref, right_ref,
    dec_send_ref, recv_ref, out_ref,
    mesh_grad_ref, band_cot_ref, grads_ref,
    onehot_t0, onehot_t1, cot0, cot1, weighted, totals, out_acc, node_cot, turned_level, received_cot,
):
    step = pl.program_id(0)
    nodes, width = mesh_ref.shape
    edges = normed_ref.shape[0]
    band_rows = totals.shape[0]
    tiles = pl.num_programs(0) - 1
    tile = ENC_TILE
    degree = edges // tile
    scaling = degree ** (-0.5)
    cots = (cot0, cot1)
    onehots = (onehot_t0, onehot_t1)

    @pl.when(step == 0)
    def _():
        totals[...] = jnp.zeros_like(totals)
        cot = dot_nt(moved_cot_ref[...], dec_send_ref[...])
        node_cot[...] = cot
        spread = scaling * cot
        level = (spread - jnp.mean(spread, axis=-1, keepdims=True)).astype(BF)
        turned_level[...] = dot_nt(level, out_ref[...])
        out_acc[...] = dot_tn(sum_ref[...], level)

    def scatter(slot, n):
        half = width // 2
        at = slice(n * half, (n + 1) * half)
        totals[:, at] += dot(onehots[slot][...], cots[slot][:, at])

    def edge_part(slot, beside):
        strips = tile // STRIP
        total = [jnp.zeros((STRIP, width), F32)] * strips
        for n in range(2):
            if beside is not None:
                scatter(beside, n)
            for k in range(n * degree // 2, (n + 1) * degree // 2):
                for i in range(strips):
                    at = slice(k * tile + i * STRIP, k * tile + (i + 1) * STRIP)
                    mine = pl.ds(pl.multiple_of(step * tile + i * STRIP, STRIP), STRIP)
                    spread = scaling * node_cot[mine, :]
                    along = jnp.mean(spread * normed_ref[at, :].astype(F32), axis=-1, keepdims=True)
                    turned = turned_level[mine, :] - along * turned_ref[at, :].astype(F32)
                    before_cot = slope_ref[at, :].astype(F32) * turned
                    total[i] = total[i] + before_cot
                    cots[slot][at, :] = before_cot.astype(BF)
                    weighted[at, :] = (hidden_ref[at, :].astype(F32) * (-along)).astype(BF)
            part = slice(n * edges // 2, (n + 1) * edges // 2)
            out_acc[...] += dot_tn(weighted[part, :], normed_ref[part, :])
        places = places_of((band_rows, edges), 0)
        spot = jnp.broadcast_to(idx_row_ref[0], (16, edges)).astype(jnp.int16)[:1]
        onehots[slot][...] = one_hot(spot, places)
        received_cot[pl.ds(pl.multiple_of(step * tile, tile), tile), :] = jnp.concatenate(total, axis=0).astype(BF)

    @pl.when(step == 0)
    def _():
        edge_part(0, None)

    for parity in range(2):
        @pl.when((step > 0) & (step < tiles) & (step % 2 == parity))
        def _():
            edge_part(parity, 1 - parity)

    @pl.when(step == tiles)
    def _():
        scatter(1, 0)
        scatter(1, 1)
        grads_ref[width : 2 * width, :] = dot_tn(mesh_ref[...], received_cot[...]).astype(BF)
        grads_ref[2 * width :, :] = out_acc[...].astype(BF)
        mesh_grad_ref[...] = (node_cot[...] + dot_nt(received_cot[...], recv_ref[...])).astype(BF)
        band_cot_ref[...] = totals[...].astype(BF)
        at = 0
        send_grad = jnp.zeros((width, width), F32)
        for piece in (own_ref, high_ref, low_ref, left_ref, right_ref):
            count = piece.shape[0]
            send_grad = send_grad + dot_tn(piece[...], band_cot_ref[at : at + count, :])
            at += count
        grads_ref[:width, :] = send_grad.astype(BF)


def enc_backward(idx_rows, mesh_rows, moved_cot, sums, normed, turned, slope, hidden, pieces, dec_send, enc_recv, enc_out):
    nodes, width = mesh_rows.shape
    tile = ENC_TILE
    tiles = nodes // tile
    assert tiles % 2 == 0
    edges = normed.shape[0] // tiles
    band_rows = sum(p.shape[0] for p in pieces)
    square = whole((width, width))
    last = tiles - 1
    per_node = whole((nodes, width))
    per_edge = pl.BlockSpec((edges, width), lambda t: (jnp.minimum(t, last), 0))
    return pl.pallas_call(
        enc_backward_kernel,
        name="enc_backward",
        grid=(tiles + 1,),
        in_specs=[pl.BlockSpec((1, 1, edges), lambda t: (jnp.minimum(t, last), 0, 0))]
        + [per_node] * 3
        + [per_edge] * 4
        + [whole(p.shape) for p in pieces]
        + [square] * 3,
        out_specs=[per_node, whole((band_rows, width)), whole((3 * width, width))],
        out_shape=[
            jax.ShapeDtypeStruct((nodes, width), BF),
            jax.ShapeDtypeStruct((band_rows, width), BF),
            jax.ShapeDtypeStruct((3 * width, width), BF),
        ],
        scratch_shapes=[
            pltpu.VMEM((band_rows, edges), BF),
            pltpu.VMEM((band_rows, edges), BF),
            pltpu.VMEM((edges, width), BF),
            pltpu.VMEM((edges, width), BF),
            pltpu.VMEM((edges, width), BF),
            pltpu.VMEM((band_rows, width), F32),
            pltpu.VMEM((width, width), F32),
            pltpu.VMEM((nodes, width), F32),
            pltpu.VMEM((nodes, width), F32),
            pltpu.VMEM((nodes, width), BF),
        ],
        compiler_params=kernel_params(),
    )(idx_rows, mesh_rows, moved_cot, sums, normed, turned, slope, hidden, *pieces, dec_send, enc_recv, enc_out)


def to_lon(shard, by):
    count = lax.axis_size("lon")
    return lax.ppermute(shard, "lon", [(i, (i + by) % count) for i in range(count)])


def to_lat(shard, by):
    count = lax.axis_size("lat")
    return lax.ppermute(shard, "lat", [(i, i + by) for i in range(count) if 0 <= i + by < count])


def core_swap(array):
    return lax.ppermute(array, "lon", [(i, i ^ 1) for i in range(lax.axis_size("lon"))])


def across_chips(parts):
    count = lax.axis_size("lat") * lax.axis_size("lon")
    alike = [[i for i in range(count) if i % 2 == c] for c in range(2)]
    return lax.all_to_all(parts, ("lat", "lon"), 0, 0, axis_index_groups=alike, tiled=True)


def on_device(
    grid, mesh_nodes, grid_cot, enc_send, enc_recv, enc_out, dec_send, dec_recv, dec_out,
    enc_src, enc_live, dec_src,
):
    lat_cells, lon_cells, width = grid.shape
    slots, degree = enc_src.shape[2:]
    lat_index = lax.axis_index("lat")
    lon_index = lax.axis_index("lon")
    lon_count = lax.axis_size("lon")
    lon_total = lon_cells * lon_count
    cells = lat_cells * lon_cells
    edge_rows = REACH * lon_cells
    tall = lat_cells + 2 * REACH

    grid_rows = grid.reshape(cells, width)
    mesh_rows = mesh_nodes.reshape(slots, width)
    high = to_lat(grid_rows[:edge_rows], -1)
    low = to_lat(grid_rows[cells - edge_rows :], 1)
    inner = jnp.concatenate([grid_rows, high, low], axis=0).reshape(tall, lon_cells, width)
    left = to_lon(inner[:, lon_cells - REACH :].reshape(tall * REACH, width), 1)
    right = to_lon(inner[:, :REACH].reshape(tall * REACH, width), -1)
    pieces = (grid_rows, high, low, left, right)

    source = enc_src.reshape(slots, degree)
    row = (source // lon_total - lat_index * lat_cells) % tall
    col = (source % lon_total - lon_index * lon_cells + REACH) % lon_total - REACH
    inner_rows = tall * lon_cells
    enc_idx = jnp.where(
        col < 0,
        inner_rows + row * REACH + col + REACH,
        jnp.where(
            col >= lon_cells,
            inner_rows + tall * REACH + row * REACH + col - lon_cells,
            row * lon_cells + col,
        ),
    )
    tiles = slots // ENC_TILE
    enc_idx_rows = enc_idx.reshape(tiles, ENC_TILE, degree).transpose(0, 2, 1)
    enc_idx_rows = enc_idx_rows.reshape(tiles, 1, ENC_TILE * degree)
    counts = jnp.sum(enc_live.reshape(slots, degree), axis=1, keepdims=True)

    picks = dec_src.reshape(3, cells)
    owner = picks // slots
    owner_lat = (owner // lon_count - lat_index) % 3
    owner_lon = (owner % lon_count - lon_index + lon_count) % lon_count
    owner_lon = jnp.where(owner_lon == lon_count - 1, 1, owner_lon * 2)
    dec_idx_rows = (owner_lon * 3 + owner_lat) * slots + picks % slots

    mesh_new, moved, before, normed, scale = enc_forward(
        enc_idx, counts, mesh_rows, pieces, enc_send, enc_recv, enc_out, dec_send
    )

    above = to_lat(moved, -1)
    below = to_lat(moved, 1)
    part = enc_between(scale, before, normed, enc_out, 0, 3)
    centre = jnp.concatenate([moved, above, below], axis=0)
    centre, part = lax.optimization_barrier((centre, part))
    west = to_lon(centre, 1)
    east = to_lon(centre, -1)
    part = enc_between(scale, before, normed, enc_out, 3, 3, part)
    west, east, part = lax.optimization_barrier((west, east, part))
    cot_rows = grid_cot.reshape(cells, width)
    grid_new, dec_hidden, dec_message_cot, dec_before_cot, dec_received_cot, west_tot, east_tot = decoder(
        dec_idx_rows.T, dec_idx_rows, grid_rows, cot_rows, centre, west, east, dec_recv, dec_out
    )
    from_east = to_lon(west_tot, -1)
    from_west = to_lon(east_tot, 1)
    grid_part, dec_out_grad, dec_recv_grad, centre_tot = decoder_rest(
        dec_idx_rows, grid_rows, cot_rows, dec_hidden, dec_message_cot, dec_before_cot, dec_received_cot,
        dec_recv, 3 * slots,
    )
    column = centre_tot.astype(F32) + from_east.astype(F32) + from_west.astype(F32)
    column, part = lax.optimization_barrier((column, part))
    turned, slope, hidden, sums = enc_between(scale, before, normed, enc_out, 6, 2, part)
    from_below = to_lat(column[slots : 2 * slots].astype(BF), 1)
    from_above = to_lat(column[2 * slots :].astype(BF), -1)
    moved_cot = column[:slots] + from_below.astype(F32) + from_above.astype(F32)
    moved_cot = moved_cot.astype(BF)
    dec_send_grad = dot_tn(mesh_new, moved_cot).astype(BF)

    mesh_grad, band_cot, enc_stack = enc_backward(
        enc_idx_rows, mesh_rows, moved_cot, sums, normed, turned, slope, hidden, pieces, dec_send, enc_recv, enc_out
    )
    dec_stack = jnp.concatenate([dec_send_grad, dec_recv_grad, dec_out_grad], axis=0)

    side = tall * REACH
    from_right = to_lon(band_cot[inner_rows : inner_rows + side], -1)
    from_left = to_lon(band_cot[inner_rows + side :], 1)

    leads = lon_index % 2 == 0
    chips = lax.axis_size("lat") * lon_count // 2
    swapped = core_swap(jnp.where(leads, dec_stack, enc_stack))
    kept = jnp.where(leads, enc_stack, dec_stack).astype(F32) + swapped.astype(F32)
    kept = kept.astype(BF).reshape(chips, 3 * width // chips, width)
    kept, from_right, from_left = lax.optimization_barrier((kept, from_right, from_left))

    inner_cot = band_cot[:inner_rows].astype(F32).reshape(tall, lon_cells, width)
    inner_cot = inner_cot.at[:, lon_cells - REACH :].add(from_right.astype(F32).reshape(tall, REACH, width))
    inner_cot = inner_cot.at[:, :REACH].add(from_left.astype(F32).reshape(tall, REACH, width))
    inner_cot = inner_cot.reshape(inner_rows, width)
    from_low = to_lat(inner_cot[cells : cells + edge_rows].astype(BF), 1)
    from_high = to_lat(inner_cot[cells + edge_rows :].astype(BF), -1)

    mine = jnp.sum(across_chips(kept).astype(F32), axis=0).astype(BF)
    mine, from_low, from_high = lax.optimization_barrier((mine, from_low, from_high))
    ours = across_chips(jnp.broadcast_to(mine[None], kept.shape)).reshape(3 * width, width)
    theirs = core_swap(ours)
    enc_grads = jnp.where(leads, ours, theirs).astype(F32)
    dec_grads = jnp.where(leads, theirs, ours).astype(F32)

    sent_cot = inner_cot[:cells] + jnp.concatenate([from_low, from_high], axis=0).astype(F32)
    grid_grad = (grid_part + dot_nt(sent_cot.astype(BF), enc_send)).astype(BF)

    return (
        grid_new.reshape(grid.shape),
        grid_grad.reshape(grid.shape),
        mesh_grad.reshape(mesh_nodes.shape),
        enc_grads[:width],
        enc_grads[width : 2 * width],
        enc_grads[2 * width :],
        dec_grads[:width],
        dec_grads[width : 2 * width],
        dec_grads[2 * width :],
    )


def solution(mesh):
    node = P("lat", "lon", None)
    block = P("lat", "lon", None, None)
    placed = (
        node, block, node, P(), P(), P(), P(), P(), P(), block, block, P(None, "lat", "lon"),
    )
    return jax.shard_map(
        on_device,
        mesh=mesh,
        in_specs=placed,
        out_specs=(node, node, block, P(), P(), P(), P(), P(), P()),
        check_vma=False,
    )
```

```python
import jax
import jax.numpy as jnp
from jax import lax
from jax.experimental import pallas as pl
from jax.experimental.pallas import tpu as pltpu
from jax.sharding import PartitionSpec as P

REACH = 4
NORM_EPSILON = 1e-05
BF = jnp.bfloat16
F32 = jnp.float32
VMEM_LIMIT = 56 * 1024 * 1024
ENC_TILE = 32
ENC_CHUNK = 4
STRIP = 16
DEC_TILE = 256


def dot(a, b):
    return jnp.dot(a, b, preferred_element_type=F32)


def dot_nt(a, b):
    return lax.dot_general(a, b, (((1,), (1,)), ((), ())), preferred_element_type=F32)


def dot_tn(a, b):
    return lax.dot_general(a, b, (((0,), (0,)), ((), ())), preferred_element_type=F32)


def sigma(v):
    return 0.5 * jnp.tanh(0.5 * v) + 0.5


def normalise(message):
    centred = message - jnp.mean(message, axis=-1, keepdims=True)
    factor = lax.rsqrt(jnp.mean(centred * centred, axis=-1, keepdims=True) + NORM_EPSILON)
    return centred, factor


def one_hot(index, places):
    return jnp.where(index == places, BF(1.0), BF(0.0))


def places_of(shape, dim):
    return lax.broadcasted_iota(jnp.int32, shape, dim).astype(jnp.int16)


def staggered(stages, count):
    for i in range(count + len(stages) - 1):
        for d in range(len(stages) - 1, -1, -1):
            if 0 <= i - d < count:
                stages[d](i - d)


def kernel_params():
    return pltpu.CompilerParams(vmem_limit_bytes=VMEM_LIMIT)


def whole(shape):
    return pl.BlockSpec(shape, lambda t: (0,) * len(shape))


def rows_of(count, width):
    return pl.BlockSpec((count, width), lambda t: (t, 0))


def enc_forward_kernel(
    idx_ref, count_ref, mesh_ref, own_ref, high_ref, low_ref, left_ref, right_ref,
    send_ref, recv_ref, out_ref, dec_send_ref,
    new_ref, moved_ref, slope_ref, hidden_ref, normed_ref, scale_ref,
    band, onehot, received_all,
):
    step = pl.program_id(0)
    tile, degree = idx_ref.shape
    width = mesh_ref.shape[1]
    band_rows = band.shape[0]
    own = pl.ds(pl.multiple_of(step * tile, tile), tile)

    @pl.when(step == 0)
    def _():
        received_all[...] = dot(mesh_ref[...], recv_ref[...])
        at = 0
        for piece in (own_ref, high_ref, low_ref, left_ref, right_ref):
            count = piece.shape[0]
            band[at : at + count, :] = dot(piece[...], send_ref[...]).astype(BF)
            at += count

    places = places_of((tile, band_rows), 1)
    index = idx_ref[...].astype(jnp.int16)
    received = received_all[own, :]
    lane = lax.broadcasted_iota(jnp.int32, (tile, degree), 1)
    rows = ENC_CHUNK * tile
    state = {"total": jnp.zeros((tile, width), F32), "scales": jnp.zeros((tile, degree), F32)}
    held = {}

    def place(c):
        for k in range(c * ENC_CHUNK, (c + 1) * ENC_CHUNK):
            onehot[k * tile : (k + 1) * tile, :] = one_hot(index[:, k : k + 1], places)

    def gather(c):
        held["gathered", c] = dot(onehot[c * rows : (c + 1) * rows, :], band[...])

    def activate(c):
        before = held.pop(("gathered", c)).reshape(ENC_CHUNK, tile, width) + received[None]
        sig = sigma(before)
        silu = before * sig
        part = slice(c * rows, (c + 1) * rows)
        slope_ref[part, :] = (sig + silu * (1.0 - sig)).reshape(rows, width).astype(BF)
        hidden = silu.reshape(rows, width).astype(BF)
        hidden_ref[part, :] = hidden
        held["hidden", c] = hidden

    def project(c):
        held["message", c] = dot(held.pop(("hidden", c)), out_ref[...])

    def norm(c):
        centred, factor = normalise(held.pop(("message", c)))
        normed = (centred * factor).reshape(ENC_CHUNK, tile, width)
        normed_ref[c * rows : (c + 1) * rows, :] = normed.reshape(rows, width).astype(BF)
        factor = factor.reshape(ENC_CHUNK, tile, 1)
        for j in range(ENC_CHUNK):
            k = c * ENC_CHUNK + j
            live = jnp.where(count_ref[...] > k, 1.0, 0.0)
            state["total"] = state["total"] + normed[j] * live
            state["scales"] = jnp.where(lane == k, factor[j] * live, state["scales"])

    staggered([place, gather, activate, project, norm], degree // ENC_CHUNK)
    scale_ref[...] = state["scales"]
    nodes = mesh_ref[own, :].astype(F32)
    new_ref[own, :] = (nodes + degree ** (-0.5) * state["total"]).astype(BF)

    @pl.when(step == pl.num_programs(0) - 1)
    def _():
        moved_ref[...] = dot(new_ref[...], dec_send_ref[...]).astype(BF)


def enc_forward(idx, counts, mesh_rows, pieces, enc_send, enc_recv, enc_out, dec_send):
    nodes, degree = idx.shape
    width = mesh_rows.shape[1]
    tile = ENC_TILE
    edges = tile * degree
    band_rows = sum(p.shape[0] for p in pieces)
    square = whole((width, width))
    return pl.pallas_call(
        enc_forward_kernel,
        name="enc_forward",
        grid=(nodes // tile,),
        in_specs=[rows_of(tile, degree), rows_of(tile, 1), whole((nodes, width))]
        + [whole(p.shape) for p in pieces]
        + [square] * 4,
        out_specs=[
            whole((nodes, width)), whole((nodes, width)),
            rows_of(edges, width), rows_of(edges, width), rows_of(edges, width), rows_of(tile, degree),
        ],
        out_shape=[
            jax.ShapeDtypeStruct((nodes, width), BF),
            jax.ShapeDtypeStruct((nodes, width), BF),
            jax.ShapeDtypeStruct((nodes * degree, width), BF),
            jax.ShapeDtypeStruct((nodes * degree, width), BF),
            jax.ShapeDtypeStruct((nodes * degree, width), BF),
            jax.ShapeDtypeStruct((nodes, degree), F32),
        ],
        scratch_shapes=[
            pltpu.VMEM((band_rows, width), BF),
            pltpu.VMEM((edges, band_rows), BF),
            pltpu.VMEM((nodes, width), F32),
        ],
        compiler_params=kernel_params(),
    )(idx, counts, mesh_rows, *pieces, enc_send, enc_recv, enc_out, dec_send)


def enc_between_kernel(normed_ref, out_ref, *refs):
    refs[-1][...] = dot_nt(normed_ref[...], out_ref[...]).astype(BF)


def enc_between(normed, enc_out, first, count, rows, done=None):
    width = normed.shape[1]
    per_edge = pl.BlockSpec((rows, width), lambda t: (t + first, 0))
    share = count * rows * width
    kept = () if done is None else (done,)
    return pl.pallas_call(
        enc_between_kernel,
        name="enc_between",
        grid=(count,),
        in_specs=[per_edge, whole((width, width))] + [pl.BlockSpec(memory_space=pl.ANY)] * len(kept),
        out_specs=per_edge,
        out_shape=jax.ShapeDtypeStruct(normed.shape, BF),
        input_output_aliases={2: 0} if kept else {},
        compiler_params=kernel_params(),
        cost_estimate=pl.CostEstimate(flops=2 * share * width, bytes_accessed=4 * share, transcendentals=0),
    )(normed, enc_out, *kept)


def decoder_kernel(
    idx_ref, idx_row_ref, grid_ref, cot_ref, centre_ref, left_ref, right_ref,
    recv_ref, out_ref,
    new_ref, hidden_ref, message_cot_ref, before_cot_ref, received_cot_ref, left_tot_ref, right_tot_ref,
    onehot, onehot_t, received_all, new_all, received_cot_all,
):
    nodes, width = grid_ref.shape
    degree = idx_ref.shape[1]
    third = centre_ref.shape[0]
    tile = DEC_TILE
    parts = nodes // tile
    index = idx_ref[...].astype(jnp.int16)
    places = places_of((tile, 3 * third), 1)
    held = {}

    received_all[...] = dot(grid_ref[...], recv_ref[...])

    def spot(i):
        h, j = divmod(i, degree)
        return j, slice(h * tile, (h + 1) * tile), slice(i * tile, (i + 1) * tile)

    def place(i):
        j, at, edges = spot(i)
        onehot[edges, :] = one_hot(index[at, j : j + 1], places)

    def gather(i):
        j, at, edges = spot(i)
        gathered = dot(onehot[edges, :third], centre_ref[...])
        gathered = gathered + dot(onehot[edges, third : 2 * third], left_ref[...])
        held["gathered", i] = gathered + dot(onehot[edges, 2 * third :], right_ref[...])

    def activate(i):
        j, at, edges = spot(i)
        before = held.pop(("gathered", i)) + received_all[at, :]
        sig = sigma(before)
        silu = before * sig
        hidden = silu.astype(BF)
        hidden_ref[edges, :] = hidden
        held["slope", i] = sig + silu * (1.0 - sig)
        held["message", i] = dot(hidden, out_ref[...])

    def norm(i):
        j, at, edges = spot(i)
        centred, factor = normalise(held.pop(("message", i)))
        normed = centred * factor
        cot = cot_ref[at, :].astype(F32)
        level = cot - jnp.mean(cot, axis=-1, keepdims=True)
        along = jnp.mean(cot * normed, axis=-1, keepdims=True)
        message_cot = (factor * (level - normed * along)).astype(BF)
        message_cot_ref[edges, :] = message_cot
        held["hidden_cot", i] = dot_nt(message_cot, out_ref[...])
        if j == 0:
            new_all[at, :] = grid_ref[at, :].astype(F32) + normed
        else:
            new_all[at, :] += normed

    def back(i):
        j, at, edges = spot(i)
        before_cot = held.pop(("hidden_cot", i)) * held.pop(("slope", i))
        before_cot_ref[edges, :] = before_cot.astype(BF)
        if j == 0:
            received_cot_all[at, :] = before_cot
        else:
            received_cot_all[at, :] += before_cot
        rows = lax.broadcasted_iota(jnp.int32, (2 * third, tile), 0) + third
        picks = jnp.broadcast_to(idx_row_ref[j : j + 1, at], (16, tile)).astype(jnp.int16)[:1]
        onehot_t[:, edges] = one_hot(picks, rows.astype(jnp.int16))

    staggered([place, gather, activate, norm, back], degree * parts)
    left_tot_ref[...] = dot(onehot_t[:third, :], before_cot_ref[...]).astype(BF)
    new_ref[...] = new_all[...].astype(BF)
    right_tot_ref[...] = dot(onehot_t[third:, :], before_cot_ref[...]).astype(BF)
    received_cot_ref[...] = received_cot_all[...].astype(BF)


def decoder(idx, idx_rows, grid_rows, cot_rows, centre, left, right, dec_recv, dec_out):
    nodes, width = grid_rows.shape
    degree = idx.shape[1]
    third = centre.shape[0]
    edge_shape = jax.ShapeDtypeStruct((degree * nodes, width), BF)
    node_shape = jax.ShapeDtypeStruct((nodes, width), BF)
    side_shape = jax.ShapeDtypeStruct((third, width), BF)
    return pl.pallas_call(
        decoder_kernel,
        name="decoder",
        out_shape=[node_shape, edge_shape, edge_shape, edge_shape, node_shape, side_shape, side_shape],
        scratch_shapes=[
            pltpu.VMEM((degree * nodes, 3 * third), BF),
            pltpu.VMEM((2 * third, degree * nodes), BF),
            pltpu.VMEM((nodes, width), F32),
            pltpu.VMEM((nodes, width), F32),
            pltpu.VMEM((nodes, width), F32),
        ],
        compiler_params=kernel_params(),
    )(idx, idx_rows, grid_rows, cot_rows, centre, left, right, dec_recv, dec_out)


def decoder_rest_kernel(
    idx_row_ref, grid_ref, cot_ref, hidden_ref, message_cot_ref, before_cot_ref, received_cot_ref, recv_ref,
    part_ref, out_grad_ref, recv_grad_ref, centre_tot_ref,
    onehot_t,
):
    third, width = centre_tot_ref.shape
    degree, nodes = idx_row_ref.shape
    tile = DEC_TILE
    rows = places_of((third, tile), 0)
    for i in range(degree * nodes // tile):
        h, j = divmod(i, degree)
        picks = jnp.broadcast_to(idx_row_ref[j : j + 1, h * tile : (h + 1) * tile], (16, tile))
        onehot_t[:, i * tile : (i + 1) * tile] = one_hot(picks.astype(jnp.int16)[:1], rows)
    centre_tot_ref[...] = dot(onehot_t[...], before_cot_ref[...]).astype(BF)
    out_grad_ref[...] = dot_tn(hidden_ref[...], message_cot_ref[...]).astype(BF)
    received_cot = received_cot_ref[...]
    recv_grad_ref[...] = dot_tn(grid_ref[...], received_cot).astype(BF)
    part_ref[...] = cot_ref[...].astype(F32) + dot_nt(received_cot, recv_ref[...])


def decoder_rest(idx_rows, grid_rows, cot_rows, hidden, message_cot, before_cot, received_cot, dec_recv, third):
    degree, nodes = idx_rows.shape
    width = hidden.shape[1]
    return pl.pallas_call(
        decoder_rest_kernel,
        name="decoder_rest",
        out_shape=[
            jax.ShapeDtypeStruct((nodes, width), F32),
            jax.ShapeDtypeStruct((width, width), BF),
            jax.ShapeDtypeStruct((width, width), BF),
            jax.ShapeDtypeStruct((third, width), BF),
        ],
        scratch_shapes=[pltpu.VMEM((third, degree * nodes), BF)],
        compiler_params=kernel_params(),
        cost_estimate=pl.CostEstimate(
            flops=2 * degree * nodes * width * (third + 2 * width), bytes_accessed=8 * degree * nodes * width,
            transcendentals=0,
        ),
    )(idx_rows, grid_rows, cot_rows, hidden, message_cot, before_cot, received_cot, dec_recv)


def enc_backward_kernel(
    idx_row_ref, scale_ref, mesh_ref, moved_cot_ref, normed_ref, turned_ref, slope_ref, hidden_ref,
    own_ref, high_ref, low_ref, left_ref, right_ref,
    dec_send_ref, recv_ref, out_ref,
    mesh_grad_ref, band_cot_ref, grads_ref,
    onehot_t0, onehot_t1, cot0, cot1, message_cot, totals, out_acc, node_cot, levels, turned_level, received_cot,
):
    step = pl.program_id(0)
    nodes, width = mesh_ref.shape
    edges = normed_ref.shape[0]
    band_rows = totals.shape[0]
    tiles = pl.num_programs(0) - 1
    tile = ENC_TILE
    degree = edges // tile
    scaling = degree ** (-0.5)
    cots = (cot0, cot1)
    onehots = (onehot_t0, onehot_t1)

    @pl.when(step == 0)
    def _():
        totals[...] = jnp.zeros_like(totals)
        cot = dot_nt(moved_cot_ref[...], dec_send_ref[...])
        node_cot[...] = cot
        spread = scaling * cot
        level = spread - jnp.mean(spread, axis=-1, keepdims=True)
        levels[...] = level
        turned_level[...] = dot_nt(level.astype(BF), out_ref[...])
        out_acc[...] = jnp.zeros_like(out_acc)

    def scatter(slot, n):
        half = width // 2
        at = slice(n * half, (n + 1) * half)
        totals[:, at] += dot(onehots[slot][...], cots[slot][:, at])

    def edge_part(slot, beside):
        strips = tile // STRIP
        total = [jnp.zeros((STRIP, width), F32)] * strips
        scales = scale_ref[...]
        for n in range(2):
            if beside is not None:
                scatter(beside, n)
            for k in range(n * degree // 2, (n + 1) * degree // 2):
                for i in range(strips):
                    at = slice(k * tile + i * STRIP, k * tile + (i + 1) * STRIP)
                    mine = pl.ds(pl.multiple_of(step * tile + i * STRIP, STRIP), STRIP)
                    spread = scaling * node_cot[mine, :]
                    normed = normed_ref[at, :].astype(F32)
                    along = jnp.mean(spread * normed, axis=-1, keepdims=True)
                    scale = scales[i * STRIP : (i + 1) * STRIP, k : k + 1]
                    message_cot[at, :] = (scale * (levels[mine, :] - along * normed)).astype(BF)
                    turned = scale * (turned_level[mine, :] - along * turned_ref[at, :].astype(F32))
                    before_cot = slope_ref[at, :].astype(F32) * turned
                    total[i] = total[i] + before_cot
                    cots[slot][at, :] = before_cot.astype(BF)
            part = slice(n * edges // 2, (n + 1) * edges // 2)
            out_acc[...] += dot_tn(hidden_ref[part, :], message_cot[part, :])
        places = places_of((band_rows, edges), 0)
        spot = jnp.broadcast_to(idx_row_ref[0], (16, edges)).astype(jnp.int16)[:1]
        onehots[slot][...] = one_hot(spot, places)
        received_cot[pl.ds(pl.multiple_of(step * tile, tile), tile), :] = jnp.concatenate(total, axis=0).astype(BF)

    @pl.when(step == 0)
    def _():
        edge_part(0, None)

    for parity in range(2):
        @pl.when((step > 0) & (step < tiles) & (step % 2 == parity))
        def _():
            edge_part(parity, 1 - parity)

    @pl.when(step == tiles)
    def _():
        scatter(1, 0)
        scatter(1, 1)
        grads_ref[width : 2 * width, :] = dot_tn(mesh_ref[...], received_cot[...]).astype(BF)
        grads_ref[2 * width :, :] = out_acc[...].astype(BF)
        mesh_grad_ref[...] = (node_cot[...] + dot_nt(received_cot[...], recv_ref[...])).astype(BF)
        band_cot_ref[...] = totals[...].astype(BF)
        at = 0
        send_grad = jnp.zeros((width, width), F32)
        for piece in (own_ref, high_ref, low_ref, left_ref, right_ref):
            count = piece.shape[0]
            send_grad = send_grad + dot_tn(piece[...], band_cot_ref[at : at + count, :])
            at += count
        grads_ref[:width, :] = send_grad.astype(BF)


def enc_backward(idx_rows, scale, mesh_rows, moved_cot, normed, turned, slope, hidden, pieces, dec_send, enc_recv, enc_out):
    nodes, width = mesh_rows.shape
    degree = scale.shape[1]
    tile = ENC_TILE
    tiles = nodes // tile
    assert tiles % 2 == 0
    edges = normed.shape[0] // tiles
    band_rows = sum(p.shape[0] for p in pieces)
    square = whole((width, width))
    last = tiles - 1
    per_node = whole((nodes, width))
    per_edge = pl.BlockSpec((edges, width), lambda t: (jnp.minimum(t, last), 0))
    return pl.pallas_call(
        enc_backward_kernel,
        name="enc_backward",
        grid=(tiles + 1,),
        in_specs=[
            pl.BlockSpec((1, 1, edges), lambda t: (jnp.minimum(t, last), 0, 0)),
            pl.BlockSpec((tile, degree), lambda t: (jnp.minimum(t, last), 0)),
        ]
        + [per_node] * 2
        + [per_edge] * 4
        + [whole(p.shape) for p in pieces]
        + [square] * 3,
        out_specs=[per_node, whole((band_rows, width)), whole((3 * width, width))],
        out_shape=[
            jax.ShapeDtypeStruct((nodes, width), BF),
            jax.ShapeDtypeStruct((band_rows, width), BF),
            jax.ShapeDtypeStruct((3 * width, width), BF),
        ],
        scratch_shapes=[
            pltpu.VMEM((band_rows, edges), BF),
            pltpu.VMEM((band_rows, edges), BF),
            pltpu.VMEM((edges, width), BF),
            pltpu.VMEM((edges, width), BF),
            pltpu.VMEM((edges, width), BF),
            pltpu.VMEM((band_rows, width), F32),
            pltpu.VMEM((width, width), F32),
            pltpu.VMEM((nodes, width), F32),
            pltpu.VMEM((nodes, width), F32),
            pltpu.VMEM((nodes, width), F32),
            pltpu.VMEM((nodes, width), BF),
        ],
        compiler_params=kernel_params(),
    )(idx_rows, scale, mesh_rows, moved_cot, normed, turned, slope, hidden, *pieces, dec_send, enc_recv, enc_out)


def to_lon(shard, by):
    count = lax.axis_size("lon")
    return lax.ppermute(shard, "lon", [(i, (i + by) % count) for i in range(count)])


def to_lat(shard, by):
    count = lax.axis_size("lat")
    return lax.ppermute(shard, "lat", [(i, i + by) for i in range(count) if 0 <= i + by < count])


def core_swap(array):
    return lax.ppermute(array, "lon", [(i, i ^ 1) for i in range(lax.axis_size("lon"))])


def across_chips(parts):
    count = lax.axis_size("lat") * lax.axis_size("lon")
    alike = [[i for i in range(count) if i % 2 == c] for c in range(2)]
    return lax.all_to_all(parts, ("lat", "lon"), 0, 0, axis_index_groups=alike, tiled=True)


def on_device(
    grid, mesh_nodes, grid_cot, enc_send, enc_recv, enc_out, dec_send, dec_recv, dec_out,
    enc_src, enc_live, dec_src,
):
    lat_cells, lon_cells, width = grid.shape
    slots, degree = enc_src.shape[2:]
    lat_index = lax.axis_index("lat")
    lon_index = lax.axis_index("lon")
    lon_count = lax.axis_size("lon")
    lon_total = lon_cells * lon_count
    cells = lat_cells * lon_cells
    edge_rows = REACH * lon_cells
    tall = lat_cells + 2 * REACH

    grid_rows = grid.reshape(cells, width)
    mesh_rows = mesh_nodes.reshape(slots, width)
    high = to_lat(grid_rows[:edge_rows], -1)
    low = to_lat(grid_rows[cells - edge_rows :], 1)
    inner = jnp.concatenate([grid_rows, high, low], axis=0).reshape(tall, lon_cells, width)
    left = to_lon(inner[:, lon_cells - REACH :].reshape(tall * REACH, width), 1)
    right = to_lon(inner[:, :REACH].reshape(tall * REACH, width), -1)
    pieces = (grid_rows, high, low, left, right)

    source = enc_src.reshape(slots, degree)
    row = (source // lon_total - lat_index * lat_cells) % tall
    col = (source % lon_total - lon_index * lon_cells + REACH) % lon_total - REACH
    inner_rows = tall * lon_cells
    enc_idx = jnp.where(
        col < 0,
        inner_rows + row * REACH + col + REACH,
        jnp.where(
            col >= lon_cells,
            inner_rows + tall * REACH + row * REACH + col - lon_cells,
            row * lon_cells + col,
        ),
    )
    tiles = slots // ENC_TILE
    enc_idx_rows = enc_idx.reshape(tiles, ENC_TILE, degree).transpose(0, 2, 1)
    enc_idx_rows = enc_idx_rows.reshape(tiles, 1, ENC_TILE * degree)
    counts = jnp.sum(enc_live.reshape(slots, degree), axis=1, keepdims=True)

    picks = dec_src.reshape(3, cells)
    owner = picks // slots
    owner_lat = (owner // lon_count - lat_index) % 3
    owner_lon = (owner % lon_count - lon_index + lon_count) % lon_count
    owner_lon = jnp.where(owner_lon == lon_count - 1, 1, owner_lon * 2)
    dec_idx_rows = (owner_lon * 3 + owner_lat) * slots + picks % slots

    mesh_new, moved, slope, hidden, normed, scale = enc_forward(
        enc_idx, counts, mesh_rows, pieces, enc_send, enc_recv, enc_out, dec_send
    )

    above = to_lat(moved, -1)
    below = to_lat(moved, 1)
    half = slots * degree // 2
    block = half // 4
    part = enc_between(normed, enc_out, 0, 4, block)
    centre = jnp.concatenate([moved, above, below], axis=0)
    centre, part = lax.optimization_barrier((centre, part))
    west = to_lon(centre, 1)
    east = to_lon(centre, -1)
    turned = enc_between(normed, enc_out, 4, 4, block, part)
    west, east, turned = lax.optimization_barrier((west, east, turned))
    cot_rows = grid_cot.reshape(cells, width)
    grid_new, dec_hidden, dec_message_cot, dec_before_cot, dec_received_cot, west_tot, east_tot = decoder(
        dec_idx_rows.T, dec_idx_rows, grid_rows, cot_rows, centre, west, east, dec_recv, dec_out
    )
    from_east = to_lon(west_tot, -1)
    from_west = to_lon(east_tot, 1)
    grid_part, dec_out_grad, dec_recv_grad, centre_tot = decoder_rest(
        dec_idx_rows, grid_rows, cot_rows, dec_hidden, dec_message_cot, dec_before_cot, dec_received_cot,
        dec_recv, 3 * slots,
    )
    column = centre_tot.astype(F32) + from_east.astype(F32) + from_west.astype(F32)
    from_below = to_lat(column[slots : 2 * slots].astype(BF), 1)
    from_above = to_lat(column[2 * slots :].astype(BF), -1)
    moved_cot = column[:slots] + from_below.astype(F32) + from_above.astype(F32)
    moved_cot = moved_cot.astype(BF)
    dec_send_grad = dot_tn(mesh_new, moved_cot).astype(BF)

    mesh_grad, band_cot, enc_stack = enc_backward(
        enc_idx_rows, scale, mesh_rows, moved_cot, normed, turned, slope, hidden, pieces, dec_send, enc_recv, enc_out
    )
    dec_stack = jnp.concatenate([dec_send_grad, dec_recv_grad, dec_out_grad], axis=0)

    side = tall * REACH
    from_right = to_lon(band_cot[inner_rows : inner_rows + side], -1)
    from_left = to_lon(band_cot[inner_rows + side :], 1)

    leads = lon_index % 2 == 0
    chips = lax.axis_size("lat") * lon_count // 2
    swapped = core_swap(jnp.where(leads, dec_stack, enc_stack))
    kept = jnp.where(leads, enc_stack, dec_stack).astype(F32) + swapped.astype(F32)
    kept = kept.astype(BF).reshape(chips, 3 * width // chips, width)
    kept, from_right, from_left = lax.optimization_barrier((kept, from_right, from_left))

    inner_cot = band_cot[:inner_rows].astype(F32).reshape(tall, lon_cells, width)
    inner_cot = inner_cot.at[:, lon_cells - REACH :].add(from_right.astype(F32).reshape(tall, REACH, width))
    inner_cot = inner_cot.at[:, :REACH].add(from_left.astype(F32).reshape(tall, REACH, width))
    inner_cot = inner_cot.reshape(inner_rows, width)
    from_low = to_lat(inner_cot[cells : cells + edge_rows].astype(BF), 1)
    from_high = to_lat(inner_cot[cells + edge_rows :].astype(BF), -1)

    mine = jnp.sum(across_chips(kept).astype(F32), axis=0).astype(BF)
    mine, from_low, from_high = lax.optimization_barrier((mine, from_low, from_high))
    ours = across_chips(jnp.broadcast_to(mine[None], kept.shape)).reshape(3 * width, width)
    theirs = core_swap(ours)
    enc_grads = jnp.where(leads, ours, theirs).astype(F32)
    dec_grads = jnp.where(leads, theirs, ours).astype(F32)

    sent_cot = inner_cot[:cells] + jnp.concatenate([from_low, from_high], axis=0).astype(F32)
    grid_grad = (grid_part + dot_nt(sent_cot.astype(BF), enc_send)).astype(BF)

    return (
        grid_new.reshape(grid.shape),
        grid_grad.reshape(grid.shape),
        mesh_grad.reshape(mesh_nodes.shape),
        enc_grads[:width],
        enc_grads[width : 2 * width],
        enc_grads[2 * width :],
        dec_grads[:width],
        dec_grads[width : 2 * width],
        dec_grads[2 * width :],
    )


def solution(mesh):
    node = P("lat", "lon", None)
    block = P("lat", "lon", None, None)
    placed = (
        node, block, node, P(), P(), P(), P(), P(), P(), block, block, P(None, "lat", "lon"),
    )
    return jax.shard_map(
        on_device,
        mesh=mesh,
        in_specs=placed,
        out_specs=(node, node, block, P(), P(), P(), P(), P(), P()),
        check_vma=False,
    )
```

```python
import jax
import jax.numpy as jnp
from jax import lax
from jax.experimental import pallas as pl
from jax.experimental.pallas import tpu as pltpu
from jax.sharding import PartitionSpec as P

REACH = 4
NORM_EPSILON = 1e-05
BF = jnp.bfloat16
F32 = jnp.float32
MIB = 1024 * 1024
ENC_TILE = 32
ENC_CHUNK = 4
STRIP = 16
DEC_TILE = 256


def dot(a, b):
    return jnp.dot(a, b, preferred_element_type=F32)


def dot_nt(a, b):
    return lax.dot_general(a, b, (((1,), (1,)), ((), ())), preferred_element_type=F32)


def dot_tn(a, b):
    return lax.dot_general(a, b, (((0,), (0,)), ((), ())), preferred_element_type=F32)


def sigma(v):
    return 0.5 * jnp.tanh(0.5 * v) + 0.5


def normalise(message):
    centred = message - jnp.mean(message, axis=-1, keepdims=True)
    factor = lax.rsqrt(jnp.mean(centred * centred, axis=-1, keepdims=True) + NORM_EPSILON)
    return centred, factor


def one_hot(index, places):
    return jnp.where(index == places, BF(1.0), BF(0.0))


def places_of(shape, dim):
    return lax.broadcasted_iota(jnp.int32, shape, dim).astype(jnp.int16)


def staggered(stages, count):
    for i in range(count + len(stages) - 1):
        for d in range(len(stages) - 1, -1, -1):
            if 0 <= i - d < count:
                stages[d](i - d)


def kernel_params(mib):
    return pltpu.CompilerParams(vmem_limit_bytes=mib * MIB)


def whole(shape):
    return pl.BlockSpec(shape, lambda t: (0,) * len(shape))


def rows_of(count, width):
    return pl.BlockSpec((count, width), lambda t: (t, 0))


def enc_forward_kernel(
    idx_ref, count_ref, mesh_ref, own_ref, high_ref, low_ref, left_ref, right_ref,
    send_ref, recv_ref, out_ref, dec_send_ref,
    new_ref, moved_ref, slope_ref, hidden_ref, normed_ref, scale_ref,
    band, onehot, received_all,
):
    step = pl.program_id(0)
    tile, degree = idx_ref.shape
    width = mesh_ref.shape[1]
    band_rows = band.shape[0]
    own = pl.ds(pl.multiple_of(step * tile, tile), tile)

    @pl.when(step == 0)
    def _():
        received_all[...] = dot(mesh_ref[...], recv_ref[...])
        at = 0
        for piece in (own_ref, high_ref, low_ref, left_ref, right_ref):
            count = piece.shape[0]
            band[at : at + count, :] = dot(piece[...], send_ref[...]).astype(BF)
            at += count

    places = places_of((tile, band_rows), 1)
    index = idx_ref[...].astype(jnp.int16)
    received = received_all[own, :]
    lane = lax.broadcasted_iota(jnp.int32, (tile, degree), 1)
    rows = ENC_CHUNK * tile
    state = {"total": jnp.zeros((tile, width), F32), "scales": jnp.zeros((tile, degree), F32)}
    held = {}

    def place(c):
        for k in range(c * ENC_CHUNK, (c + 1) * ENC_CHUNK):
            onehot[k * tile : (k + 1) * tile, :] = one_hot(index[:, k : k + 1], places)

    def gather(c):
        held["gathered", c] = dot(onehot[c * rows : (c + 1) * rows, :], band[...])

    def activate(c):
        before = held.pop(("gathered", c)).reshape(ENC_CHUNK, tile, width) + received[None]
        sig = sigma(before)
        silu = before * sig
        part = slice(c * rows, (c + 1) * rows)
        slope_ref[part, :] = (sig + silu * (1.0 - sig)).reshape(rows, width).astype(BF)
        hidden = silu.reshape(rows, width).astype(BF)
        hidden_ref[part, :] = hidden
        held["hidden", c] = hidden

    def project(c):
        held["message", c] = dot(held.pop(("hidden", c)), out_ref[...])

    def norm(c):
        centred, factor = normalise(held.pop(("message", c)))
        normed = (centred * factor).reshape(ENC_CHUNK, tile, width)
        normed_ref[c * rows : (c + 1) * rows, :] = normed.reshape(rows, width).astype(BF)
        factor = factor.reshape(ENC_CHUNK, tile, 1)
        for j in range(ENC_CHUNK):
            k = c * ENC_CHUNK + j
            live = jnp.where(count_ref[...] > k, 1.0, 0.0)
            state["total"] = state["total"] + normed[j] * live
            state["scales"] = jnp.where(lane == k, factor[j] * live, state["scales"])

    staggered([place, gather, activate, project, norm], degree // ENC_CHUNK)
    scale_ref[...] = state["scales"]
    nodes = mesh_ref[own, :].astype(F32)
    new_ref[own, :] = (nodes + degree ** (-0.5) * state["total"]).astype(BF)

    @pl.when(step == pl.num_programs(0) - 1)
    def _():
        moved_ref[...] = dot(new_ref[...], dec_send_ref[...]).astype(BF)


def enc_forward(idx, counts, mesh_rows, pieces, enc_send, enc_recv, enc_out, dec_send):
    nodes, degree = idx.shape
    width = mesh_rows.shape[1]
    tile = ENC_TILE
    edges = tile * degree
    band_rows = sum(p.shape[0] for p in pieces)
    square = whole((width, width))
    return pl.pallas_call(
        enc_forward_kernel,
        name="enc_forward",
        grid=(nodes // tile,),
        in_specs=[rows_of(tile, degree), rows_of(tile, 1), whole((nodes, width))]
        + [whole(p.shape) for p in pieces]
        + [square] * 4,
        out_specs=[
            whole((nodes, width)), whole((nodes, width)),
            rows_of(edges, width), rows_of(edges, width), rows_of(edges, width), rows_of(tile, degree),
        ],
        out_shape=[
            jax.ShapeDtypeStruct((nodes, width), BF),
            jax.ShapeDtypeStruct((nodes, width), BF),
            jax.ShapeDtypeStruct((nodes * degree, width), BF),
            jax.ShapeDtypeStruct((nodes * degree, width), BF),
            jax.ShapeDtypeStruct((nodes * degree, width), BF),
            jax.ShapeDtypeStruct((nodes, degree), F32),
        ],
        scratch_shapes=[
            pltpu.VMEM((band_rows, width), BF),
            pltpu.VMEM((edges, band_rows), BF),
            pltpu.VMEM((nodes, width), F32),
        ],
        compiler_params=kernel_params(26),
    )(idx, counts, mesh_rows, *pieces, enc_send, enc_recv, enc_out, dec_send)


def enc_between_kernel(normed_ref, out_ref, *refs):
    refs[-1][...] = dot_nt(normed_ref[...], out_ref[...]).astype(BF)


def enc_between(normed, enc_out, first, count, rows, done=None):
    width = normed.shape[1]
    per_edge = pl.BlockSpec((rows, width), lambda t: (t + first, 0))
    share = count * rows * width
    kept = () if done is None else (done,)
    return pl.pallas_call(
        enc_between_kernel,
        name="enc_between",
        grid=(count,),
        in_specs=[per_edge, whole((width, width))] + [pl.BlockSpec(memory_space=pl.ANY)] * len(kept),
        out_specs=per_edge,
        out_shape=jax.ShapeDtypeStruct(normed.shape, BF),
        input_output_aliases={2: 0} if kept else {},
        compiler_params=kernel_params(12),
        cost_estimate=pl.CostEstimate(flops=2 * share * width, bytes_accessed=4 * share, transcendentals=0),
    )(normed, enc_out, *kept)


def decoder_kernel(
    idx_ref, idx_row_ref, grid_ref, cot_ref, centre_ref, left_ref, right_ref,
    recv_ref, out_ref,
    new_ref, hidden_ref, message_cot_ref, before_cot_ref, received_cot_ref, left_tot_ref, right_tot_ref,
    onehot, onehot_t, received_all, new_all, received_cot_all,
):
    nodes, width = grid_ref.shape
    degree = idx_ref.shape[1]
    third = centre_ref.shape[0]
    tile = DEC_TILE
    parts = nodes // tile
    index = idx_ref[...].astype(jnp.int16)
    places = places_of((tile, 3 * third), 1)
    held = {}

    received_all[...] = dot(grid_ref[...], recv_ref[...])

    def spot(i):
        h, j = divmod(i, degree)
        return j, slice(h * tile, (h + 1) * tile), slice(i * tile, (i + 1) * tile)

    def place(i):
        j, at, edges = spot(i)
        onehot[edges, :] = one_hot(index[at, j : j + 1], places)

    def gather(i):
        j, at, edges = spot(i)
        gathered = dot(onehot[edges, :third], centre_ref[...])
        gathered = gathered + dot(onehot[edges, third : 2 * third], left_ref[...])
        held["gathered", i] = gathered + dot(onehot[edges, 2 * third :], right_ref[...])

    def activate(i):
        j, at, edges = spot(i)
        before = held.pop(("gathered", i)) + received_all[at, :]
        sig = sigma(before)
        silu = before * sig
        hidden = silu.astype(BF)
        hidden_ref[edges, :] = hidden
        held["slope", i] = sig + silu * (1.0 - sig)
        held["message", i] = dot(hidden, out_ref[...])

    def norm(i):
        j, at, edges = spot(i)
        centred, factor = normalise(held.pop(("message", i)))
        normed = centred * factor
        cot = cot_ref[at, :].astype(F32)
        level = cot - jnp.mean(cot, axis=-1, keepdims=True)
        along = jnp.mean(cot * normed, axis=-1, keepdims=True)
        message_cot = (factor * (level - normed * along)).astype(BF)
        message_cot_ref[edges, :] = message_cot
        held["hidden_cot", i] = dot_nt(message_cot, out_ref[...])
        if j == 0:
            new_all[at, :] = grid_ref[at, :].astype(F32) + normed
        else:
            new_all[at, :] += normed

    def back(i):
        j, at, edges = spot(i)
        before_cot = held.pop(("hidden_cot", i)) * held.pop(("slope", i))
        before_cot_ref[edges, :] = before_cot.astype(BF)
        if j == 0:
            received_cot_all[at, :] = before_cot
        else:
            received_cot_all[at, :] += before_cot
        rows = lax.broadcasted_iota(jnp.int32, (2 * third, tile), 0) + third
        picks = jnp.broadcast_to(idx_row_ref[j : j + 1, at], (16, tile)).astype(jnp.int16)[:1]
        onehot_t[:, edges] = one_hot(picks, rows.astype(jnp.int16))

    staggered([place, gather, activate, norm, back], degree * parts)
    left_tot_ref[...] = dot(onehot_t[:third, :], before_cot_ref[...]).astype(BF)
    new_ref[...] = new_all[...].astype(BF)
    right_tot_ref[...] = dot(onehot_t[third:, :], before_cot_ref[...]).astype(BF)
    received_cot_ref[...] = received_cot_all[...].astype(BF)


def decoder(idx, idx_rows, grid_rows, cot_rows, centre, left, right, dec_recv, dec_out):
    nodes, width = grid_rows.shape
    degree = idx.shape[1]
    third = centre.shape[0]
    edge_shape = jax.ShapeDtypeStruct((degree * nodes, width), BF)
    node_shape = jax.ShapeDtypeStruct((nodes, width), BF)
    side_shape = jax.ShapeDtypeStruct((third, width), BF)
    return pl.pallas_call(
        decoder_kernel,
        name="decoder",
        out_shape=[node_shape, edge_shape, edge_shape, edge_shape, node_shape, side_shape, side_shape],
        scratch_shapes=[
            pltpu.VMEM((degree * nodes, 3 * third), BF),
            pltpu.VMEM((2 * third, degree * nodes), BF),
            pltpu.VMEM((nodes, width), F32),
            pltpu.VMEM((nodes, width), F32),
            pltpu.VMEM((nodes, width), F32),
        ],
        compiler_params=kernel_params(36),
    )(idx, idx_rows, grid_rows, cot_rows, centre, left, right, dec_recv, dec_out)


def decoder_rest_kernel(
    idx_row_ref, grid_ref, cot_ref, hidden_ref, message_cot_ref, before_cot_ref, received_cot_ref, recv_ref,
    part_ref, out_grad_ref, recv_grad_ref, centre_tot_ref,
    onehot_t,
):
    third, width = centre_tot_ref.shape
    degree, nodes = idx_row_ref.shape
    tile = DEC_TILE
    rows = places_of((third, tile), 0)
    for i in range(degree * nodes // tile):
        h, j = divmod(i, degree)
        picks = jnp.broadcast_to(idx_row_ref[j : j + 1, h * tile : (h + 1) * tile], (16, tile))
        onehot_t[:, i * tile : (i + 1) * tile] = one_hot(picks.astype(jnp.int16)[:1], rows)
    centre_tot_ref[...] = dot(onehot_t[...], before_cot_ref[...]).astype(BF)
    out_grad_ref[...] = dot_tn(hidden_ref[...], message_cot_ref[...]).astype(BF)
    received_cot = received_cot_ref[...]
    recv_grad_ref[...] = dot_tn(grid_ref[...], received_cot).astype(BF)
    part_ref[...] = cot_ref[...].astype(F32) + dot_nt(received_cot, recv_ref[...])


def decoder_rest(idx_rows, grid_rows, cot_rows, hidden, message_cot, before_cot, received_cot, dec_recv, third):
    degree, nodes = idx_rows.shape
    width = hidden.shape[1]
    return pl.pallas_call(
        decoder_rest_kernel,
        name="decoder_rest",
        out_shape=[
            jax.ShapeDtypeStruct((nodes, width), F32),
            jax.ShapeDtypeStruct((width, width), BF),
            jax.ShapeDtypeStruct((width, width), BF),
            jax.ShapeDtypeStruct((third, width), BF),
        ],
        scratch_shapes=[pltpu.VMEM((third, degree * nodes), BF)],
        compiler_params=kernel_params(20),
        cost_estimate=pl.CostEstimate(
            flops=2 * degree * nodes * width * (third + 2 * width), bytes_accessed=8 * degree * nodes * width,
            transcendentals=0,
        ),
    )(idx_rows, grid_rows, cot_rows, hidden, message_cot, before_cot, received_cot, dec_recv)


def enc_backward_kernel(
    idx_row_ref, scale_ref, mesh_ref, moved_cot_ref, normed_ref, turned_ref, slope_ref, hidden_ref,
    own_ref, high_ref, low_ref, left_ref, right_ref,
    dec_send_ref, recv_ref, out_ref,
    mesh_grad_ref, band_cot_ref, grads_ref,
    onehot_t0, onehot_t1, cot0, cot1, message_cot, totals, out_acc, node_cot, levels, turned_level, received_cot,
):
    step = pl.program_id(0)
    nodes, width = mesh_ref.shape
    edges = normed_ref.shape[0]
    band_rows = totals.shape[0]
    tiles = pl.num_programs(0) - 1
    tile = ENC_TILE
    degree = edges // tile
    scaling = degree ** (-0.5)
    cots = (cot0, cot1)
    onehots = (onehot_t0, onehot_t1)

    @pl.when(step == 0)
    def _():
        totals[...] = jnp.zeros_like(totals)
        cot = dot_nt(moved_cot_ref[...], dec_send_ref[...])
        node_cot[...] = cot
        spread = scaling * cot
        level = spread - jnp.mean(spread, axis=-1, keepdims=True)
        levels[...] = level
        turned_level[...] = dot_nt(level.astype(BF), out_ref[...])
        out_acc[...] = jnp.zeros_like(out_acc)

    def scatter(slot, n):
        half = width // 2
        at = slice(n * half, (n + 1) * half)
        totals[:, at] += dot(onehots[slot][...], cots[slot][:, at])

    def edge_part(slot, beside):
        strips = tile // STRIP
        total = [jnp.zeros((STRIP, width), F32)] * strips
        scales = scale_ref[...]
        for n in range(2):
            if beside is not None:
                scatter(beside, n)
            for k in range(n * degree // 2, (n + 1) * degree // 2):
                for i in range(strips):
                    at = slice(k * tile + i * STRIP, k * tile + (i + 1) * STRIP)
                    mine = pl.ds(pl.multiple_of(step * tile + i * STRIP, STRIP), STRIP)
                    spread = scaling * node_cot[mine, :]
                    normed = normed_ref[at, :].astype(F32)
                    along = jnp.mean(spread * normed, axis=-1, keepdims=True)
                    scale = scales[i * STRIP : (i + 1) * STRIP, k : k + 1]
                    message_cot[at, :] = (scale * (levels[mine, :] - along * normed)).astype(BF)
                    turned = scale * (turned_level[mine, :] - along * turned_ref[at, :].astype(F32))
                    before_cot = slope_ref[at, :].astype(F32) * turned
                    total[i] = total[i] + before_cot
                    cots[slot][at, :] = before_cot.astype(BF)
            part = slice(n * edges // 2, (n + 1) * edges // 2)
            out_acc[...] += dot_tn(hidden_ref[part, :], message_cot[part, :])
        places = places_of((band_rows, edges), 0)
        spot = jnp.broadcast_to(idx_row_ref[0], (16, edges)).astype(jnp.int16)[:1]
        onehots[slot][...] = one_hot(spot, places)
        received_cot[pl.ds(pl.multiple_of(step * tile, tile), tile), :] = jnp.concatenate(total, axis=0).astype(BF)

    @pl.when(step == 0)
    def _():
        edge_part(0, None)

    for parity in range(2):
        @pl.when((step > 0) & (step < tiles) & (step % 2 == parity))
        def _():
            edge_part(parity, 1 - parity)

    @pl.when(step == tiles)
    def _():
        scatter(1, 0)
        scatter(1, 1)
        grads_ref[width : 2 * width, :] = dot_tn(mesh_ref[...], received_cot[...]).astype(BF)
        grads_ref[2 * width :, :] = out_acc[...].astype(BF)
        mesh_grad_ref[...] = (node_cot[...] + dot_nt(received_cot[...], recv_ref[...])).astype(BF)
        band_cot_ref[...] = totals[...].astype(BF)
        at = 0
        send_grad = jnp.zeros((width, width), F32)
        for piece in (own_ref, high_ref, low_ref, left_ref, right_ref):
            count = piece.shape[0]
            send_grad = send_grad + dot_tn(piece[...], band_cot_ref[at : at + count, :])
            at += count
        grads_ref[:width, :] = send_grad.astype(BF)


def enc_backward(idx_rows, scale, mesh_rows, moved_cot, normed, turned, slope, hidden, pieces, dec_send, enc_recv, enc_out):
    nodes, width = mesh_rows.shape
    degree = scale.shape[1]
    tile = ENC_TILE
    tiles = nodes // tile
    assert tiles % 2 == 0
    edges = normed.shape[0] // tiles
    band_rows = sum(p.shape[0] for p in pieces)
    square = whole((width, width))
    last = tiles - 1
    per_node = whole((nodes, width))
    per_edge = pl.BlockSpec((edges, width), lambda t: (jnp.minimum(t, last), 0))
    return pl.pallas_call(
        enc_backward_kernel,
        name="enc_backward",
        grid=(tiles + 1,),
        in_specs=[
            pl.BlockSpec((1, 1, edges), lambda t: (jnp.minimum(t, last), 0, 0)),
            pl.BlockSpec((tile, degree), lambda t: (jnp.minimum(t, last), 0)),
        ]
        + [per_node] * 2
        + [per_edge] * 4
        + [whole(p.shape) for p in pieces]
        + [square] * 3,
        out_specs=[per_node, whole((band_rows, width)), whole((3 * width, width))],
        out_shape=[
            jax.ShapeDtypeStruct((nodes, width), BF),
            jax.ShapeDtypeStruct((band_rows, width), BF),
            jax.ShapeDtypeStruct((3 * width, width), BF),
        ],
        scratch_shapes=[
            pltpu.VMEM((band_rows, edges), BF),
            pltpu.VMEM((band_rows, edges), BF),
            pltpu.VMEM((edges, width), BF),
            pltpu.VMEM((edges, width), BF),
            pltpu.VMEM((edges, width), BF),
            pltpu.VMEM((band_rows, width), F32),
            pltpu.VMEM((width, width), F32),
            pltpu.VMEM((nodes, width), F32),
            pltpu.VMEM((nodes, width), F32),
            pltpu.VMEM((nodes, width), F32),
            pltpu.VMEM((nodes, width), BF),
        ],
        compiler_params=kernel_params(40),
    )(idx_rows, scale, mesh_rows, moved_cot, normed, turned, slope, hidden, *pieces, dec_send, enc_recv, enc_out)


def to_lon(shard, by):
    count = lax.axis_size("lon")
    return lax.ppermute(shard, "lon", [(i, (i + by) % count) for i in range(count)])


def to_lat(shard, by):
    count = lax.axis_size("lat")
    return lax.ppermute(shard, "lat", [(i, i + by) for i in range(count) if 0 <= i + by < count])


def core_swap(array):
    return lax.ppermute(array, "lon", [(i, i ^ 1) for i in range(lax.axis_size("lon"))])


def across_chips(parts):
    count = lax.axis_size("lat") * lax.axis_size("lon")
    alike = [[i for i in range(count) if i % 2 == c] for c in range(2)]
    return lax.all_to_all(parts, ("lat", "lon"), 0, 0, axis_index_groups=alike, tiled=True)


def on_device(
    grid, mesh_nodes, grid_cot, enc_send, enc_recv, enc_out, dec_send, dec_recv, dec_out,
    enc_src, enc_live, dec_src,
):
    lat_cells, lon_cells, width = grid.shape
    slots, degree = enc_src.shape[2:]
    lat_index = lax.axis_index("lat")
    lon_index = lax.axis_index("lon")
    lon_count = lax.axis_size("lon")
    lon_total = lon_cells * lon_count
    cells = lat_cells * lon_cells
    edge_rows = REACH * lon_cells
    tall = lat_cells + 2 * REACH

    grid_rows = grid.reshape(cells, width)
    mesh_rows = mesh_nodes.reshape(slots, width)
    high = to_lat(grid_rows[:edge_rows], -1)
    low = to_lat(grid_rows[cells - edge_rows :], 1)
    inner = jnp.concatenate([grid_rows, high, low], axis=0).reshape(tall, lon_cells, width)
    left = to_lon(inner[:, lon_cells - REACH :].reshape(tall * REACH, width), 1)
    right = to_lon(inner[:, :REACH].reshape(tall * REACH, width), -1)
    pieces = (grid_rows, high, low, left, right)

    source = enc_src.reshape(slots, degree)
    row = (source // lon_total - lat_index * lat_cells) % tall
    col = (source % lon_total - lon_index * lon_cells + REACH) % lon_total - REACH
    inner_rows = tall * lon_cells
    enc_idx = jnp.where(
        col < 0,
        inner_rows + row * REACH + col + REACH,
        jnp.where(
            col >= lon_cells,
            inner_rows + tall * REACH + row * REACH + col - lon_cells,
            row * lon_cells + col,
        ),
    )
    tiles = slots // ENC_TILE
    enc_idx_rows = enc_idx.reshape(tiles, ENC_TILE, degree).transpose(0, 2, 1)
    enc_idx_rows = enc_idx_rows.reshape(tiles, 1, ENC_TILE * degree)
    counts = jnp.sum(enc_live.reshape(slots, degree), axis=1, keepdims=True)

    picks = dec_src.reshape(3, cells)
    owner = picks // slots
    owner_lat = (owner // lon_count - lat_index) % 3
    owner_lon = (owner % lon_count - lon_index + lon_count) % lon_count
    owner_lon = jnp.where(owner_lon == lon_count - 1, 1, owner_lon * 2)
    dec_idx_rows = (owner_lon * 3 + owner_lat) * slots + picks % slots

    mesh_new, moved, slope, hidden, normed, scale = enc_forward(
        enc_idx, counts, mesh_rows, pieces, enc_send, enc_recv, enc_out, dec_send
    )

    above = to_lat(moved, -1)
    below = to_lat(moved, 1)
    half = slots * degree // 2
    block = half // 4
    part = enc_between(normed, enc_out, 0, 4, block)
    centre = jnp.concatenate([moved, above, below], axis=0)
    centre, part = lax.optimization_barrier((centre, part))
    west = to_lon(centre, 1)
    east = to_lon(centre, -1)
    turned = enc_between(normed, enc_out, 4, 4, block, part)
    west, east, turned = lax.optimization_barrier((west, east, turned))
    cot_rows = grid_cot.reshape(cells, width)
    grid_new, dec_hidden, dec_message_cot, dec_before_cot, dec_received_cot, west_tot, east_tot = decoder(
        dec_idx_rows.T, dec_idx_rows, grid_rows, cot_rows, centre, west, east, dec_recv, dec_out
    )
    from_east = to_lon(west_tot, -1)
    from_west = to_lon(east_tot, 1)
    grid_part, dec_out_grad, dec_recv_grad, centre_tot = decoder_rest(
        dec_idx_rows, grid_rows, cot_rows, dec_hidden, dec_message_cot, dec_before_cot, dec_received_cot,
        dec_recv, 3 * slots,
    )
    column = centre_tot.astype(F32) + from_east.astype(F32) + from_west.astype(F32)
    from_below = to_lat(column[slots : 2 * slots].astype(BF), 1)
    from_above = to_lat(column[2 * slots :].astype(BF), -1)
    moved_cot = column[:slots] + from_below.astype(F32) + from_above.astype(F32)
    moved_cot = moved_cot.astype(BF)
    dec_send_grad = dot_tn(mesh_new, moved_cot).astype(BF)

    mesh_grad, band_cot, enc_stack = enc_backward(
        enc_idx_rows, scale, mesh_rows, moved_cot, normed, turned, slope, hidden, pieces, dec_send, enc_recv, enc_out
    )
    dec_stack = jnp.concatenate([dec_send_grad, dec_recv_grad, dec_out_grad], axis=0)

    side = tall * REACH
    from_right = to_lon(band_cot[inner_rows : inner_rows + side], -1)
    from_left = to_lon(band_cot[inner_rows + side :], 1)

    leads = lon_index % 2 == 0
    chips = lax.axis_size("lat") * lon_count // 2
    swapped = core_swap(jnp.where(leads, dec_stack, enc_stack))
    kept = jnp.where(leads, enc_stack, dec_stack).astype(F32) + swapped.astype(F32)
    kept = kept.astype(BF).reshape(chips, 3 * width // chips, width)
    kept, from_right, from_left = lax.optimization_barrier((kept, from_right, from_left))

    inner_cot = band_cot[:inner_rows].astype(F32).reshape(tall, lon_cells, width)
    inner_cot = inner_cot.at[:, lon_cells - REACH :].add(from_right.astype(F32).reshape(tall, REACH, width))
    inner_cot = inner_cot.at[:, :REACH].add(from_left.astype(F32).reshape(tall, REACH, width))
    inner_cot = inner_cot.reshape(inner_rows, width)
    from_low = to_lat(inner_cot[cells : cells + edge_rows].astype(BF), 1)
    from_high = to_lat(inner_cot[cells + edge_rows :].astype(BF), -1)

    mine = jnp.sum(across_chips(kept).astype(F32), axis=0).astype(BF)
    mine, from_low, from_high = lax.optimization_barrier((mine, from_low, from_high))
    ours = across_chips(jnp.broadcast_to(mine[None], kept.shape)).reshape(3 * width, width)
    theirs = core_swap(ours)
    enc_grads = jnp.where(leads, ours, theirs).astype(F32)
    dec_grads = jnp.where(leads, theirs, ours).astype(F32)

    sent_cot = inner_cot[:cells] + jnp.concatenate([from_low, from_high], axis=0).astype(F32)
    grid_grad = (grid_part + dot_nt(sent_cot.astype(BF), enc_send)).astype(BF)

    return (
        grid_new.reshape(grid.shape),
        grid_grad.reshape(grid.shape),
        mesh_grad.reshape(mesh_nodes.shape),
        enc_grads[:width],
        enc_grads[width : 2 * width],
        enc_grads[2 * width :],
        dec_grads[:width],
        dec_grads[width : 2 * width],
        dec_grads[2 * width :],
    )


def solution(mesh):
    node = P("lat", "lon", None)
    block = P("lat", "lon", None, None)
    placed = (
        node, block, node, P(), P(), P(), P(), P(), P(), block, block, P(None, "lat", "lon"),
    )
    return jax.shard_map(
        on_device,
        mesh=mesh,
        in_specs=placed,
        out_specs=(node, node, block, P(), P(), P(), P(), P(), P()),
        check_vma=False,
    )
```

```python
import jax
import jax.numpy as jnp
from jax import lax
from jax.experimental import pallas as pl
from jax.experimental.pallas import tpu as pltpu
from jax.sharding import PartitionSpec as P

REACH = 4
NORM_EPSILON = 1e-05
BF = jnp.bfloat16
F32 = jnp.float32
MIB = 1024 * 1024
ENC_TILE = 32
ENC_CHUNK = 4
STRIP = 16
DEC_TILE = 256


def dot(a, b):
    return jnp.dot(a, b, preferred_element_type=F32)


def dot_nt(a, b):
    return lax.dot_general(a, b, (((1,), (1,)), ((), ())), preferred_element_type=F32)


def dot_tn(a, b):
    return lax.dot_general(a, b, (((0,), (0,)), ((), ())), preferred_element_type=F32)


def sigma(v):
    return 0.5 * jnp.tanh(0.5 * v) + 0.5


def normalise(message):
    centred = message - jnp.mean(message, axis=-1, keepdims=True)
    factor = lax.rsqrt(jnp.mean(centred * centred, axis=-1, keepdims=True) + NORM_EPSILON)
    return centred, factor


def one_hot(index, places):
    return jnp.where(index == places, BF(1.0), BF(0.0))


def places_of(shape, dim):
    return lax.broadcasted_iota(jnp.int32, shape, dim).astype(jnp.int16)


def staggered(stages, count):
    for i in range(count + len(stages) - 1):
        for d in range(len(stages) - 1, -1, -1):
            if 0 <= i - d < count:
                stages[d](i - d)


def kernel_params(mib):
    return pltpu.CompilerParams(vmem_limit_bytes=mib * MIB)


def whole(shape):
    return pl.BlockSpec(shape, lambda t: (0,) * len(shape))


def rows_of(count, width):
    return pl.BlockSpec((count, width), lambda t: (t, 0))


def enc_forward_kernel(
    idx_ref, count_ref, mesh_ref, own_ref, high_ref, low_ref, left_ref, right_ref,
    send_ref, recv_ref, out_ref, dec_send_ref,
    new_ref, moved_ref, slope_ref, hidden_ref, normed_ref, scale_ref,
    band, onehot, received_all,
):
    step = pl.program_id(0)
    tile, degree = idx_ref.shape
    width = mesh_ref.shape[1]
    band_rows = band.shape[0]
    own = pl.ds(pl.multiple_of(step * tile, tile), tile)

    @pl.when(step == 0)
    def _():
        received_all[...] = dot(mesh_ref[...], recv_ref[...])
        at = 0
        for piece in (own_ref, high_ref, low_ref, left_ref, right_ref):
            count = piece.shape[0]
            band[at : at + count, :] = dot(piece[...], send_ref[...]).astype(BF)
            at += count

    places = places_of((tile, band_rows), 1)
    index = idx_ref[...].astype(jnp.int16)
    received = received_all[own, :]
    lane = lax.broadcasted_iota(jnp.int32, (tile, degree), 1)
    rows = ENC_CHUNK * tile
    state = {"total": jnp.zeros((tile, width), F32), "scales": jnp.zeros((tile, degree), F32)}
    held = {}

    def place(c):
        for k in range(c * ENC_CHUNK, (c + 1) * ENC_CHUNK):
            onehot[k * tile : (k + 1) * tile, :] = one_hot(index[:, k : k + 1], places)

    def gather(c):
        held["gathered", c] = dot(onehot[c * rows : (c + 1) * rows, :], band[...])

    def activate(c):
        before = held.pop(("gathered", c)).reshape(ENC_CHUNK, tile, width) + received[None]
        sig = sigma(before)
        silu = before * sig
        part = slice(c * rows, (c + 1) * rows)
        slope_ref[part, :] = (sig + silu * (1.0 - sig)).reshape(rows, width).astype(BF)
        hidden = silu.reshape(rows, width).astype(BF)
        hidden_ref[part, :] = hidden
        held["hidden", c] = hidden

    def project(c):
        held["message", c] = dot(held.pop(("hidden", c)), out_ref[...])

    def norm(c):
        centred, factor = normalise(held.pop(("message", c)))
        normed = (centred * factor).reshape(ENC_CHUNK, tile, width)
        normed_ref[c * rows : (c + 1) * rows, :] = normed.reshape(rows, width).astype(BF)
        factor = factor.reshape(ENC_CHUNK, tile, 1)
        for j in range(ENC_CHUNK):
            k = c * ENC_CHUNK + j
            live = jnp.where(count_ref[...] > k, 1.0, 0.0)
            state["total"] = state["total"] + normed[j] * live
            state["scales"] = jnp.where(lane == k, factor[j] * live, state["scales"])

    staggered([place, gather, activate, project, norm], degree // ENC_CHUNK)
    scale_ref[...] = state["scales"]
    nodes = mesh_ref[own, :].astype(F32)
    new_ref[own, :] = (nodes + degree ** (-0.5) * state["total"]).astype(BF)

    @pl.when(step == pl.num_programs(0) - 1)
    def _():
        moved_ref[...] = dot(new_ref[...], dec_send_ref[...]).astype(BF)


def enc_forward(idx, counts, mesh_rows, pieces, enc_send, enc_recv, enc_out, dec_send):
    nodes, degree = idx.shape
    width = mesh_rows.shape[1]
    tile = ENC_TILE
    edges = tile * degree
    band_rows = sum(p.shape[0] for p in pieces)
    square = whole((width, width))
    return pl.pallas_call(
        enc_forward_kernel,
        name="enc_forward",
        grid=(nodes // tile,),
        in_specs=[rows_of(tile, degree), rows_of(tile, 1), whole((nodes, width))]
        + [whole(p.shape) for p in pieces]
        + [square] * 4,
        out_specs=[
            whole((nodes, width)), whole((nodes, width)),
            rows_of(edges, width), rows_of(edges, width), rows_of(edges, width), rows_of(tile, degree),
        ],
        out_shape=[
            jax.ShapeDtypeStruct((nodes, width), BF),
            jax.ShapeDtypeStruct((nodes, width), BF),
            pltpu.HBM((nodes * degree, width), BF),
            pltpu.HBM((nodes * degree, width), BF),
            pltpu.HBM((nodes * degree, width), BF),
            jax.ShapeDtypeStruct((nodes, degree), F32),
        ],
        scratch_shapes=[
            pltpu.VMEM((band_rows, width), BF),
            pltpu.VMEM((edges, band_rows), BF),
            pltpu.VMEM((nodes, width), F32),
        ],
        compiler_params=kernel_params(26),
    )(idx, counts, mesh_rows, *pieces, enc_send, enc_recv, enc_out, dec_send)


def enc_between_kernel(normed_ref, out_ref, *refs):
    refs[-1][...] = dot_nt(normed_ref[...], out_ref[...]).astype(BF)


def enc_between(normed, enc_out, first, count, rows, done=None):
    width = normed.shape[1]
    per_edge = pl.BlockSpec((rows, width), lambda t: (t + first, 0))
    share = count * rows * width
    kept = () if done is None else (done,)
    return pl.pallas_call(
        enc_between_kernel,
        name="enc_between",
        grid=(count,),
        in_specs=[per_edge, whole((width, width))] + [pl.BlockSpec(memory_space=pl.ANY)] * len(kept),
        out_specs=per_edge,
        out_shape=pltpu.HBM(normed.shape, BF),
        input_output_aliases={2: 0} if kept else {},
        compiler_params=kernel_params(56),
        cost_estimate=pl.CostEstimate(flops=2 * share * width, bytes_accessed=4 * share, transcendentals=0),
    )(normed, enc_out, *kept)


def decoder_kernel(
    idx_ref, idx_row_ref, grid_ref, cot_ref, centre_ref, left_ref, right_ref,
    recv_ref, out_ref,
    new_ref, hidden_ref, message_cot_ref, before_cot_ref, received_cot_ref, left_tot_ref, right_tot_ref,
    onehot, onehot_t, received_all, new_all, received_cot_all,
):
    nodes, width = grid_ref.shape
    degree = idx_ref.shape[1]
    third = centre_ref.shape[0]
    tile = DEC_TILE
    parts = nodes // tile
    index = idx_ref[...].astype(jnp.int16)
    places = places_of((tile, 3 * third), 1)
    held = {}

    received_all[...] = dot(grid_ref[...], recv_ref[...])

    def spot(i):
        h, j = divmod(i, degree)
        return j, slice(h * tile, (h + 1) * tile), slice(i * tile, (i + 1) * tile)

    def place(i):
        j, at, edges = spot(i)
        onehot[edges, :] = one_hot(index[at, j : j + 1], places)

    def gather(i):
        j, at, edges = spot(i)
        gathered = dot(onehot[edges, :third], centre_ref[...])
        gathered = gathered + dot(onehot[edges, third : 2 * third], left_ref[...])
        held["gathered", i] = gathered + dot(onehot[edges, 2 * third :], right_ref[...])

    def activate(i):
        j, at, edges = spot(i)
        before = held.pop(("gathered", i)) + received_all[at, :]
        sig = sigma(before)
        silu = before * sig
        hidden = silu.astype(BF)
        hidden_ref[edges, :] = hidden
        held["slope", i] = sig + silu * (1.0 - sig)
        held["message", i] = dot(hidden, out_ref[...])

    def norm(i):
        j, at, edges = spot(i)
        centred, factor = normalise(held.pop(("message", i)))
        normed = centred * factor
        cot = cot_ref[at, :].astype(F32)
        level = cot - jnp.mean(cot, axis=-1, keepdims=True)
        along = jnp.mean(cot * normed, axis=-1, keepdims=True)
        message_cot = (factor * (level - normed * along)).astype(BF)
        message_cot_ref[edges, :] = message_cot
        held["hidden_cot", i] = dot_nt(message_cot, out_ref[...])
        if j == 0:
            new_all[at, :] = grid_ref[at, :].astype(F32) + normed
        else:
            new_all[at, :] += normed

    def back(i):
        j, at, edges = spot(i)
        before_cot = held.pop(("hidden_cot", i)) * held.pop(("slope", i))
        before_cot_ref[edges, :] = before_cot.astype(BF)
        if j == 0:
            received_cot_all[at, :] = before_cot
        else:
            received_cot_all[at, :] += before_cot
        rows = lax.broadcasted_iota(jnp.int32, (2 * third, tile), 0) + third
        picks = jnp.broadcast_to(idx_row_ref[j : j + 1, at], (16, tile)).astype(jnp.int16)[:1]
        onehot_t[:, edges] = one_hot(picks, rows.astype(jnp.int16))

    staggered([place, gather, activate, norm, back], degree * parts)
    left_tot_ref[...] = dot(onehot_t[:third, :], before_cot_ref[...]).astype(BF)
    new_ref[...] = new_all[...].astype(BF)
    right_tot_ref[...] = dot(onehot_t[third:, :], before_cot_ref[...]).astype(BF)
    received_cot_ref[...] = received_cot_all[...].astype(BF)


def decoder(idx, idx_rows, grid_rows, cot_rows, centre, left, right, dec_recv, dec_out):
    nodes, width = grid_rows.shape
    degree = idx.shape[1]
    third = centre.shape[0]
    edge_shape = jax.ShapeDtypeStruct((degree * nodes, width), BF)
    node_shape = jax.ShapeDtypeStruct((nodes, width), BF)
    side_shape = jax.ShapeDtypeStruct((third, width), BF)
    return pl.pallas_call(
        decoder_kernel,
        name="decoder",
        out_shape=[node_shape, edge_shape, edge_shape, edge_shape, node_shape, side_shape, side_shape],
        scratch_shapes=[
            pltpu.VMEM((degree * nodes, 3 * third), BF),
            pltpu.VMEM((2 * third, degree * nodes), BF),
            pltpu.VMEM((nodes, width), F32),
            pltpu.VMEM((nodes, width), F32),
            pltpu.VMEM((nodes, width), F32),
        ],
        compiler_params=kernel_params(36),
    )(idx, idx_rows, grid_rows, cot_rows, centre, left, right, dec_recv, dec_out)


def decoder_rest_kernel(
    idx_row_ref, grid_ref, cot_ref, hidden_ref, message_cot_ref, before_cot_ref, received_cot_ref, recv_ref,
    part_ref, out_grad_ref, recv_grad_ref, centre_tot_ref,
    onehot_t,
):
    third, width = centre_tot_ref.shape
    degree, nodes = idx_row_ref.shape
    tile = DEC_TILE
    rows = places_of((third, tile), 0)
    for i in range(degree * nodes // tile):
        h, j = divmod(i, degree)
        picks = jnp.broadcast_to(idx_row_ref[j : j + 1, h * tile : (h + 1) * tile], (16, tile))
        onehot_t[:, i * tile : (i + 1) * tile] = one_hot(picks.astype(jnp.int16)[:1], rows)
    centre_tot_ref[...] = dot(onehot_t[...], before_cot_ref[...]).astype(BF)
    out_grad_ref[...] = dot_tn(hidden_ref[...], message_cot_ref[...]).astype(BF)
    received_cot = received_cot_ref[...]
    recv_grad_ref[...] = dot_tn(grid_ref[...], received_cot).astype(BF)
    part_ref[...] = cot_ref[...].astype(F32) + dot_nt(received_cot, recv_ref[...])


def decoder_rest(idx_rows, grid_rows, cot_rows, hidden, message_cot, before_cot, received_cot, dec_recv, third):
    degree, nodes = idx_rows.shape
    width = hidden.shape[1]
    return pl.pallas_call(
        decoder_rest_kernel,
        name="decoder_rest",
        out_shape=[
            jax.ShapeDtypeStruct((nodes, width), F32),
            jax.ShapeDtypeStruct((width, width), BF),
            jax.ShapeDtypeStruct((width, width), BF),
            jax.ShapeDtypeStruct((third, width), BF),
        ],
        scratch_shapes=[pltpu.VMEM((third, degree * nodes), BF)],
        compiler_params=kernel_params(20),
        cost_estimate=pl.CostEstimate(
            flops=2 * degree * nodes * width * (third + 2 * width), bytes_accessed=8 * degree * nodes * width,
            transcendentals=0,
        ),
    )(idx_rows, grid_rows, cot_rows, hidden, message_cot, before_cot, received_cot, dec_recv)


def enc_backward_kernel(
    idx_row_ref, scale_ref, mesh_ref, moved_cot_ref, normed_ref, turned_ref, slope_ref, hidden_ref,
    own_ref, high_ref, low_ref, left_ref, right_ref,
    dec_send_ref, recv_ref, out_ref,
    mesh_grad_ref, band_cot_ref, grads_ref,
    onehot_t0, onehot_t1, cot0, cot1, message_cot, totals, out_acc, node_cot, levels, turned_level, received_cot,
):
    step = pl.program_id(0)
    nodes, width = mesh_ref.shape
    edges = normed_ref.shape[0]
    band_rows = totals.shape[0]
    tiles = pl.num_programs(0) - 1
    tile = ENC_TILE
    degree = edges // tile
    scaling = degree ** (-0.5)
    cots = (cot0, cot1)
    onehots = (onehot_t0, onehot_t1)

    @pl.when(step == 0)
    def _():
        totals[...] = jnp.zeros_like(totals)
        cot = dot_nt(moved_cot_ref[...], dec_send_ref[...])
        node_cot[...] = cot
        spread = scaling * cot
        level = spread - jnp.mean(spread, axis=-1, keepdims=True)
        levels[...] = level
        turned_level[...] = dot_nt(level.astype(BF), out_ref[...])
        out_acc[...] = jnp.zeros_like(out_acc)

    def scatter(slot, n):
        half = width // 2
        at = slice(n * half, (n + 1) * half)
        totals[:, at] += dot(onehots[slot][...], cots[slot][:, at])

    def edge_part(slot, beside):
        strips = tile // STRIP
        total = [jnp.zeros((STRIP, width), F32)] * strips
        scales = scale_ref[...]
        for n in range(2):
            if beside is not None:
                scatter(beside, n)
            for k in range(n * degree // 2, (n + 1) * degree // 2):
                for i in range(strips):
                    at = slice(k * tile + i * STRIP, k * tile + (i + 1) * STRIP)
                    mine = pl.ds(pl.multiple_of(step * tile + i * STRIP, STRIP), STRIP)
                    spread = scaling * node_cot[mine, :]
                    normed = normed_ref[at, :].astype(F32)
                    along = jnp.mean(spread * normed, axis=-1, keepdims=True)
                    scale = scales[i * STRIP : (i + 1) * STRIP, k : k + 1]
                    message_cot[at, :] = (scale * (levels[mine, :] - along * normed)).astype(BF)
                    turned = scale * (turned_level[mine, :] - along * turned_ref[at, :].astype(F32))
                    before_cot = slope_ref[at, :].astype(F32) * turned
                    total[i] = total[i] + before_cot
                    cots[slot][at, :] = before_cot.astype(BF)
            part = slice(n * edges // 2, (n + 1) * edges // 2)
            out_acc[...] += dot_tn(hidden_ref[part, :], message_cot[part, :])
        places = places_of((band_rows, edges), 0)
        spot = jnp.broadcast_to(idx_row_ref[0], (16, edges)).astype(jnp.int16)[:1]
        onehots[slot][...] = one_hot(spot, places)
        received_cot[pl.ds(pl.multiple_of(step * tile, tile), tile), :] = jnp.concatenate(total, axis=0).astype(BF)

    @pl.when(step == 0)
    def _():
        edge_part(0, None)

    for parity in range(2):
        @pl.when((step > 0) & (step < tiles) & (step % 2 == parity))
        def _():
            edge_part(parity, 1 - parity)

    @pl.when(step == tiles)
    def _():
        scatter(1, 0)
        scatter(1, 1)
        grads_ref[width : 2 * width, :] = dot_tn(mesh_ref[...], received_cot[...]).astype(BF)
        grads_ref[2 * width :, :] = out_acc[...].astype(BF)
        mesh_grad_ref[...] = (node_cot[...] + dot_nt(received_cot[...], recv_ref[...])).astype(BF)
        band_cot_ref[...] = totals[...].astype(BF)
        at = 0
        send_grad = jnp.zeros((width, width), F32)
        for piece in (own_ref, high_ref, low_ref, left_ref, right_ref):
            count = piece.shape[0]
            send_grad = send_grad + dot_tn(piece[...], band_cot_ref[at : at + count, :])
            at += count
        grads_ref[:width, :] = send_grad.astype(BF)


def enc_backward(idx_rows, scale, mesh_rows, moved_cot, normed, turned, slope, hidden, pieces, dec_send, enc_recv, enc_out):
    nodes, width = mesh_rows.shape
    degree = scale.shape[1]
    tile = ENC_TILE
    tiles = nodes // tile
    assert tiles % 2 == 0
    edges = normed.shape[0] // tiles
    band_rows = sum(p.shape[0] for p in pieces)
    square = whole((width, width))
    last = tiles - 1
    per_node = whole((nodes, width))
    per_edge = pl.BlockSpec((edges, width), lambda t: (jnp.minimum(t, last), 0))
    return pl.pallas_call(
        enc_backward_kernel,
        name="enc_backward",
        grid=(tiles + 1,),
        in_specs=[
            pl.BlockSpec((1, 1, edges), lambda t: (jnp.minimum(t, last), 0, 0)),
            pl.BlockSpec((tile, degree), lambda t: (jnp.minimum(t, last), 0)),
        ]
        + [per_node] * 2
        + [per_edge] * 4
        + [whole(p.shape) for p in pieces]
        + [square] * 3,
        out_specs=[per_node, whole((band_rows, width)), whole((3 * width, width))],
        out_shape=[
            jax.ShapeDtypeStruct((nodes, width), BF),
            jax.ShapeDtypeStruct((band_rows, width), BF),
            jax.ShapeDtypeStruct((3 * width, width), BF),
        ],
        scratch_shapes=[
            pltpu.VMEM((band_rows, edges), BF),
            pltpu.VMEM((band_rows, edges), BF),
            pltpu.VMEM((edges, width), BF),
            pltpu.VMEM((edges, width), BF),
            pltpu.VMEM((edges, width), BF),
            pltpu.VMEM((band_rows, width), F32),
            pltpu.VMEM((width, width), F32),
            pltpu.VMEM((nodes, width), F32),
            pltpu.VMEM((nodes, width), F32),
            pltpu.VMEM((nodes, width), F32),
            pltpu.VMEM((nodes, width), BF),
        ],
        compiler_params=kernel_params(56),
    )(idx_rows, scale, mesh_rows, moved_cot, normed, turned, slope, hidden, *pieces, dec_send, enc_recv, enc_out)


def to_lon(shard, by):
    count = lax.axis_size("lon")
    return lax.ppermute(shard, "lon", [(i, (i + by) % count) for i in range(count)])


def to_lat(shard, by):
    count = lax.axis_size("lat")
    return lax.ppermute(shard, "lat", [(i, i + by) for i in range(count) if 0 <= i + by < count])


def core_swap(array):
    return lax.ppermute(array, "lon", [(i, i ^ 1) for i in range(lax.axis_size("lon"))])


def across_chips(parts):
    count = lax.axis_size("lat") * lax.axis_size("lon")
    alike = [[i for i in range(count) if i % 2 == c] for c in range(2)]
    return lax.all_to_all(parts, ("lat", "lon"), 0, 0, axis_index_groups=alike, tiled=True)


def on_device(
    grid, mesh_nodes, grid_cot, enc_send, enc_recv, enc_out, dec_send, dec_recv, dec_out,
    enc_src, enc_live, dec_src,
):
    lat_cells, lon_cells, width = grid.shape
    slots, degree = enc_src.shape[2:]
    lat_index = lax.axis_index("lat")
    lon_index = lax.axis_index("lon")
    lon_count = lax.axis_size("lon")
    lon_total = lon_cells * lon_count
    cells = lat_cells * lon_cells
    edge_rows = REACH * lon_cells
    tall = lat_cells + 2 * REACH

    grid_rows = grid.reshape(cells, width)
    mesh_rows = mesh_nodes.reshape(slots, width)
    high = to_lat(grid_rows[:edge_rows], -1)
    low = to_lat(grid_rows[cells - edge_rows :], 1)
    inner = jnp.concatenate([grid_rows, high, low], axis=0).reshape(tall, lon_cells, width)
    left = to_lon(inner[:, lon_cells - REACH :].reshape(tall * REACH, width), 1)
    right = to_lon(inner[:, :REACH].reshape(tall * REACH, width), -1)
    pieces = (grid_rows, high, low, left, right)

    source = enc_src.reshape(slots, degree)
    row = (source // lon_total - lat_index * lat_cells) % tall
    col = (source % lon_total - lon_index * lon_cells + REACH) % lon_total - REACH
    inner_rows = tall * lon_cells
    enc_idx = jnp.where(
        col < 0,
        inner_rows + row * REACH + col + REACH,
        jnp.where(
            col >= lon_cells,
            inner_rows + tall * REACH + row * REACH + col - lon_cells,
            row * lon_cells + col,
        ),
    )
    tiles = slots // ENC_TILE
    enc_idx_rows = enc_idx.reshape(tiles, ENC_TILE, degree).transpose(0, 2, 1)
    enc_idx_rows = enc_idx_rows.reshape(tiles, 1, ENC_TILE * degree)
    counts = jnp.sum(enc_live.reshape(slots, degree), axis=1, keepdims=True)

    picks = dec_src.reshape(3, cells)
    owner = picks // slots
    owner_lat = (owner // lon_count - lat_index) % 3
    owner_lon = (owner % lon_count - lon_index + lon_count) % lon_count
    owner_lon = jnp.where(owner_lon == lon_count - 1, 1, owner_lon * 2)
    dec_idx_rows = (owner_lon * 3 + owner_lat) * slots + picks % slots

    mesh_new, moved, slope, hidden, normed, scale = enc_forward(
        enc_idx, counts, mesh_rows, pieces, enc_send, enc_recv, enc_out, dec_send
    )

    above = to_lat(moved, -1)
    below = to_lat(moved, 1)
    half = slots * degree // 2
    block = half // 4
    part = enc_between(normed, enc_out, 0, 4, block)
    centre = jnp.concatenate([moved, above, below], axis=0)
    centre, part = lax.optimization_barrier((centre, part))
    west = to_lon(centre, 1)
    east = to_lon(centre, -1)
    turned = enc_between(normed, enc_out, 4, 4, block, part)
    west, east, turned = lax.optimization_barrier((west, east, turned))
    cot_rows = grid_cot.reshape(cells, width)
    grid_new, dec_hidden, dec_message_cot, dec_before_cot, dec_received_cot, west_tot, east_tot = decoder(
        dec_idx_rows.T, dec_idx_rows, grid_rows, cot_rows, centre, west, east, dec_recv, dec_out
    )
    from_east = to_lon(west_tot, -1)
    from_west = to_lon(east_tot, 1)
    grid_part, dec_out_grad, dec_recv_grad, centre_tot = decoder_rest(
        dec_idx_rows, grid_rows, cot_rows, dec_hidden, dec_message_cot, dec_before_cot, dec_received_cot,
        dec_recv, 3 * slots,
    )
    column = centre_tot.astype(F32) + from_east.astype(F32) + from_west.astype(F32)
    from_below = to_lat(column[slots : 2 * slots].astype(BF), 1)
    from_above = to_lat(column[2 * slots :].astype(BF), -1)
    moved_cot = column[:slots] + from_below.astype(F32) + from_above.astype(F32)
    moved_cot = moved_cot.astype(BF)
    dec_send_grad = dot_tn(mesh_new, moved_cot).astype(BF)

    mesh_grad, band_cot, enc_stack = enc_backward(
        enc_idx_rows, scale, mesh_rows, moved_cot, normed, turned, slope, hidden, pieces, dec_send, enc_recv, enc_out
    )
    dec_stack = jnp.concatenate([dec_send_grad, dec_recv_grad, dec_out_grad], axis=0)

    side = tall * REACH
    from_right = to_lon(band_cot[inner_rows : inner_rows + side], -1)
    from_left = to_lon(band_cot[inner_rows + side :], 1)

    leads = lon_index % 2 == 0
    chips = lax.axis_size("lat") * lon_count // 2
    swapped = core_swap(jnp.where(leads, dec_stack, enc_stack))
    kept = jnp.where(leads, enc_stack, dec_stack).astype(F32) + swapped.astype(F32)
    kept = kept.astype(BF).reshape(chips, 3 * width // chips, width)
    kept, from_right, from_left = lax.optimization_barrier((kept, from_right, from_left))

    inner_cot = band_cot[:inner_rows].astype(F32).reshape(tall, lon_cells, width)
    inner_cot = inner_cot.at[:, lon_cells - REACH :].add(from_right.astype(F32).reshape(tall, REACH, width))
    inner_cot = inner_cot.at[:, :REACH].add(from_left.astype(F32).reshape(tall, REACH, width))
    inner_cot = inner_cot.reshape(inner_rows, width)
    from_low = to_lat(inner_cot[cells : cells + edge_rows].astype(BF), 1)
    from_high = to_lat(inner_cot[cells + edge_rows :].astype(BF), -1)

    mine = jnp.sum(across_chips(kept).astype(F32), axis=0).astype(BF)
    mine, from_low, from_high = lax.optimization_barrier((mine, from_low, from_high))
    ours = across_chips(jnp.broadcast_to(mine[None], kept.shape)).reshape(3 * width, width)
    theirs = core_swap(ours)
    enc_grads = jnp.where(leads, ours, theirs).astype(F32)
    dec_grads = jnp.where(leads, theirs, ours).astype(F32)

    sent_cot = inner_cot[:cells] + jnp.concatenate([from_low, from_high], axis=0).astype(F32)
    grid_grad = (grid_part + dot_nt(sent_cot.astype(BF), enc_send)).astype(BF)

    return (
        grid_new.reshape(grid.shape),
        grid_grad.reshape(grid.shape),
        mesh_grad.reshape(mesh_nodes.shape),
        enc_grads[:width],
        enc_grads[width : 2 * width],
        enc_grads[2 * width :],
        dec_grads[:width],
        dec_grads[width : 2 * width],
        dec_grads[2 * width :],
    )


def solution(mesh):
    node = P("lat", "lon", None)
    block = P("lat", "lon", None, None)
    placed = (
        node, block, node, P(), P(), P(), P(), P(), P(), block, block, P(None, "lat", "lon"),
    )
    return jax.shard_map(
        on_device,
        mesh=mesh,
        in_specs=placed,
        out_specs=(node, node, block, P(), P(), P(), P(), P(), P()),
        check_vma=False,
    )
```

```python
import jax
import jax.numpy as jnp
from jax import lax
from jax.experimental import pallas as pl
from jax.experimental.pallas import tpu as pltpu
from jax.sharding import PartitionSpec as P

REACH = 4
NORM_EPSILON = 1e-05
BF = jnp.bfloat16
F32 = jnp.float32
MIB = 1024 * 1024
ENC_TILE = 32
ENC_CHUNK = 4
STRIP = 16
DEC_TILE = 256


def dot(a, b):
    return jnp.dot(a, b, preferred_element_type=F32)


def dot_nt(a, b):
    return lax.dot_general(a, b, (((1,), (1,)), ((), ())), preferred_element_type=F32)


def dot_tn(a, b):
    return lax.dot_general(a, b, (((0,), (0,)), ((), ())), preferred_element_type=F32)


def sigma(v):
    return 0.5 * jnp.tanh(0.5 * v) + 0.5


def normalise(message):
    centred = message - jnp.mean(message, axis=-1, keepdims=True)
    factor = lax.rsqrt(jnp.mean(centred * centred, axis=-1, keepdims=True) + NORM_EPSILON)
    return centred, factor


def one_hot(index, places):
    return jnp.where(index == places, BF(1.0), BF(0.0))


def places_of(shape, dim):
    return lax.broadcasted_iota(jnp.int32, shape, dim).astype(jnp.int16)


def staggered(stages, count):
    for i in range(count + len(stages) - 1):
        for d in range(len(stages) - 1, -1, -1):
            if 0 <= i - d < count:
                stages[d](i - d)


def kernel_params(mib=56):
    return pltpu.CompilerParams(vmem_limit_bytes=mib * MIB)


def whole(shape):
    return pl.BlockSpec(shape, lambda t: (0,) * len(shape))


def rows_of(count, width):
    return pl.BlockSpec((count, width), lambda t: (t, 0))


def enc_forward_kernel(
    idx_ref, count_ref, mesh_ref, own_ref, high_ref, low_ref, left_ref, right_ref,
    send_ref, recv_ref, out_ref, dec_send_ref,
    new_ref, moved_ref, slope_ref, hidden_ref, normed_ref, scale_ref,
    band, onehot, received_all,
):
    step = pl.program_id(0)
    tile, degree = idx_ref.shape
    width = mesh_ref.shape[1]
    band_rows = band.shape[0]
    own = pl.ds(pl.multiple_of(step * tile, tile), tile)

    @pl.when(step == 0)
    def _():
        received_all[...] = dot(mesh_ref[...], recv_ref[...])
        at = 0
        for piece in (own_ref, high_ref, low_ref, left_ref, right_ref):
            count = piece.shape[0]
            band[at : at + count, :] = dot(piece[...], send_ref[...]).astype(BF)
            at += count

    places = places_of((tile, band_rows), 1)
    index = idx_ref[...].astype(jnp.int16)
    received = received_all[own, :]
    lane = lax.broadcasted_iota(jnp.int32, (tile, degree), 1)
    rows = ENC_CHUNK * tile
    state = {"total": jnp.zeros((tile, width), F32), "scales": jnp.zeros((tile, degree), F32)}
    held = {}

    def place(c):
        for k in range(c * ENC_CHUNK, (c + 1) * ENC_CHUNK):
            onehot[k * tile : (k + 1) * tile, :] = one_hot(index[:, k : k + 1], places)

    def gather(c):
        held["gathered", c] = dot(onehot[c * rows : (c + 1) * rows, :], band[...])

    def activate(c):
        before = held.pop(("gathered", c)).reshape(ENC_CHUNK, tile, width) + received[None]
        sig = sigma(before)
        silu = before * sig
        part = slice(c * rows, (c + 1) * rows)
        slope_ref[part, :] = (sig + silu * (1.0 - sig)).reshape(rows, width).astype(BF)
        hidden = silu.reshape(rows, width).astype(BF)
        hidden_ref[part, :] = hidden
        held["hidden", c] = hidden

    def project(c):
        held["message", c] = dot(held.pop(("hidden", c)), out_ref[...])

    def norm(c):
        centred, factor = normalise(held.pop(("message", c)))
        normed = (centred * factor).reshape(ENC_CHUNK, tile, width)
        normed_ref[c * rows : (c + 1) * rows, :] = normed.reshape(rows, width).astype(BF)
        factor = factor.reshape(ENC_CHUNK, tile, 1)
        for j in range(ENC_CHUNK):
            k = c * ENC_CHUNK + j
            live = jnp.where(count_ref[...] > k, 1.0, 0.0)
            state["total"] = state["total"] + normed[j] * live
            state["scales"] = jnp.where(lane == k, factor[j] * live, state["scales"])

    staggered([place, gather, activate, project, norm], degree // ENC_CHUNK)
    scale_ref[...] = state["scales"]
    nodes = mesh_ref[own, :].astype(F32)
    new_ref[own, :] = (nodes + degree ** (-0.5) * state["total"]).astype(BF)

    @pl.when(step == pl.num_programs(0) - 1)
    def _():
        moved_ref[...] = dot(new_ref[...], dec_send_ref[...]).astype(BF)


def enc_forward(idx, counts, mesh_rows, pieces, enc_send, enc_recv, enc_out, dec_send):
    nodes, degree = idx.shape
    width = mesh_rows.shape[1]
    tile = ENC_TILE
    edges = tile * degree
    band_rows = sum(p.shape[0] for p in pieces)
    square = whole((width, width))
    return pl.pallas_call(
        enc_forward_kernel,
        name="enc_forward",
        grid=(nodes // tile,),
        in_specs=[rows_of(tile, degree), rows_of(tile, 1), whole((nodes, width))]
        + [whole(p.shape) for p in pieces]
        + [square] * 4,
        out_specs=[
            whole((nodes, width)), whole((nodes, width)),
            rows_of(edges, width), rows_of(edges, width), rows_of(edges, width), rows_of(tile, degree),
        ],
        out_shape=[
            jax.ShapeDtypeStruct((nodes, width), BF),
            jax.ShapeDtypeStruct((nodes, width), BF),
            jax.ShapeDtypeStruct((nodes * degree, width), BF),
            jax.ShapeDtypeStruct((nodes * degree, width), BF),
            jax.ShapeDtypeStruct((nodes * degree, width), BF),
            jax.ShapeDtypeStruct((nodes, degree), F32),
        ],
        scratch_shapes=[
            pltpu.VMEM((band_rows, width), BF),
            pltpu.VMEM((edges, band_rows), BF),
            pltpu.VMEM((nodes, width), F32),
        ],
        compiler_params=kernel_params(56),
    )(idx, counts, mesh_rows, *pieces, enc_send, enc_recv, enc_out, dec_send)


def enc_between_kernel(normed_ref, out_ref, *refs):
    refs[-1][...] = dot_nt(normed_ref[...], out_ref[...]).astype(BF)


def enc_between(normed, enc_out, first, count, rows, done=None):
    width = normed.shape[1]
    per_edge = pl.BlockSpec((rows, width), lambda t: (t + first, 0))
    share = count * rows * width
    kept = () if done is None else (done,)
    return pl.pallas_call(
        enc_between_kernel,
        name="enc_between",
        grid=(count,),
        in_specs=[per_edge, whole((width, width))] + [pl.BlockSpec(memory_space=pl.ANY)] * len(kept),
        out_specs=per_edge,
        out_shape=jax.ShapeDtypeStruct(normed.shape, BF),
        input_output_aliases={2: 0} if kept else {},
        compiler_params=kernel_params(56),
        cost_estimate=pl.CostEstimate(flops=2 * share * width, bytes_accessed=4 * share, transcendentals=0),
    )(normed, enc_out, *kept)


def decoder_kernel(
    idx_ref, idx_row_ref, grid_ref, cot_ref, centre_ref, left_ref, right_ref,
    recv_ref, out_ref,
    new_ref, hidden_ref, message_cot_ref, before_cot_ref, received_cot_ref, left_tot_ref, right_tot_ref,
    onehot, onehot_t, received_all, new_all, received_cot_all,
):
    nodes, width = grid_ref.shape
    degree = idx_ref.shape[1]
    third = centre_ref.shape[0]
    tile = DEC_TILE
    parts = nodes // tile
    index = idx_ref[...].astype(jnp.int16)
    places = places_of((tile, 3 * third), 1)
    held = {}

    received_all[...] = dot(grid_ref[...], recv_ref[...])

    def spot(i):
        h, j = divmod(i, degree)
        return j, slice(h * tile, (h + 1) * tile), slice(i * tile, (i + 1) * tile)

    def place(i):
        j, at, edges = spot(i)
        onehot[edges, :] = one_hot(index[at, j : j + 1], places)

    def gather(i):
        j, at, edges = spot(i)
        gathered = dot(onehot[edges, :third], centre_ref[...])
        gathered = gathered + dot(onehot[edges, third : 2 * third], left_ref[...])
        held["gathered", i] = gathered + dot(onehot[edges, 2 * third :], right_ref[...])

    def activate(i):
        j, at, edges = spot(i)
        before = held.pop(("gathered", i)) + received_all[at, :]
        sig = sigma(before)
        silu = before * sig
        hidden = silu.astype(BF)
        hidden_ref[edges, :] = hidden
        held["slope", i] = sig + silu * (1.0 - sig)
        held["message", i] = dot(hidden, out_ref[...])

    def norm(i):
        j, at, edges = spot(i)
        centred, factor = normalise(held.pop(("message", i)))
        normed = centred * factor
        cot = cot_ref[at, :].astype(F32)
        level = cot - jnp.mean(cot, axis=-1, keepdims=True)
        along = jnp.mean(cot * normed, axis=-1, keepdims=True)
        message_cot = (factor * (level - normed * along)).astype(BF)
        message_cot_ref[edges, :] = message_cot
        held["hidden_cot", i] = dot_nt(message_cot, out_ref[...])
        if j == 0:
            new_all[at, :] = grid_ref[at, :].astype(F32) + normed
        else:
            new_all[at, :] += normed

    def back(i):
        j, at, edges = spot(i)
        before_cot = held.pop(("hidden_cot", i)) * held.pop(("slope", i))
        before_cot_ref[edges, :] = before_cot.astype(BF)
        if j == 0:
            received_cot_all[at, :] = before_cot
        else:
            received_cot_all[at, :] += before_cot
        rows = lax.broadcasted_iota(jnp.int32, (2 * third, tile), 0) + third
        picks = jnp.broadcast_to(idx_row_ref[j : j + 1, at], (16, tile)).astype(jnp.int16)[:1]
        onehot_t[:, edges] = one_hot(picks, rows.astype(jnp.int16))

    staggered([place, gather, activate, norm, back], degree * parts)
    left_tot_ref[...] = dot(onehot_t[:third, :], before_cot_ref[...]).astype(BF)
    new_ref[...] = new_all[...].astype(BF)
    right_tot_ref[...] = dot(onehot_t[third:, :], before_cot_ref[...]).astype(BF)
    received_cot_ref[...] = received_cot_all[...].astype(BF)


def decoder(idx, idx_rows, grid_rows, cot_rows, centre, left, right, dec_recv, dec_out):
    nodes, width = grid_rows.shape
    degree = idx.shape[1]
    third = centre.shape[0]
    edge_shape = jax.ShapeDtypeStruct((degree * nodes, width), BF)
    node_shape = jax.ShapeDtypeStruct((nodes, width), BF)
    side_shape = jax.ShapeDtypeStruct((third, width), BF)
    return pl.pallas_call(
        decoder_kernel,
        name="decoder",
        out_shape=[node_shape, edge_shape, edge_shape, edge_shape, node_shape, side_shape, side_shape],
        scratch_shapes=[
            pltpu.VMEM((degree * nodes, 3 * third), BF),
            pltpu.VMEM((2 * third, degree * nodes), BF),
            pltpu.VMEM((nodes, width), F32),
            pltpu.VMEM((nodes, width), F32),
            pltpu.VMEM((nodes, width), F32),
        ],
        compiler_params=kernel_params(36),
    )(idx, idx_rows, grid_rows, cot_rows, centre, left, right, dec_recv, dec_out)


def decoder_rest_kernel(
    idx_row_ref, grid_ref, cot_ref, hidden_ref, message_cot_ref, before_cot_ref, received_cot_ref, recv_ref,
    part_ref, out_grad_ref, recv_grad_ref, centre_tot_ref,
    onehot_t,
):
    third, width = centre_tot_ref.shape
    degree, nodes = idx_row_ref.shape
    tile = DEC_TILE
    rows = places_of((third, tile), 0)
    for i in range(degree * nodes // tile):
        h, j = divmod(i, degree)
        picks = jnp.broadcast_to(idx_row_ref[j : j + 1, h * tile : (h + 1) * tile], (16, tile))
        onehot_t[:, i * tile : (i + 1) * tile] = one_hot(picks.astype(jnp.int16)[:1], rows)
    centre_tot_ref[...] = dot(onehot_t[...], before_cot_ref[...]).astype(BF)
    out_grad_ref[...] = dot_tn(hidden_ref[...], message_cot_ref[...]).astype(BF)
    received_cot = received_cot_ref[...]
    recv_grad_ref[...] = dot_tn(grid_ref[...], received_cot).astype(BF)
    part_ref[...] = cot_ref[...].astype(F32) + dot_nt(received_cot, recv_ref[...])


def decoder_rest(idx_rows, grid_rows, cot_rows, hidden, message_cot, before_cot, received_cot, dec_recv, third):
    degree, nodes = idx_rows.shape
    width = hidden.shape[1]
    return pl.pallas_call(
        decoder_rest_kernel,
        name="decoder_rest",
        out_shape=[
            jax.ShapeDtypeStruct((nodes, width), F32),
            jax.ShapeDtypeStruct((width, width), BF),
            jax.ShapeDtypeStruct((width, width), BF),
            jax.ShapeDtypeStruct((third, width), BF),
        ],
        scratch_shapes=[pltpu.VMEM((third, degree * nodes), BF)],
        compiler_params=kernel_params(20),
        cost_estimate=pl.CostEstimate(
            flops=2 * degree * nodes * width * (third + 2 * width), bytes_accessed=8 * degree * nodes * width,
            transcendentals=0,
        ),
    )(idx_rows, grid_rows, cot_rows, hidden, message_cot, before_cot, received_cot, dec_recv)


def enc_backward_kernel(
    idx_row_ref, scale_ref, mesh_ref, moved_cot_ref, normed_ref, turned_ref, slope_ref, hidden_ref,
    own_ref, high_ref, low_ref, left_ref, right_ref,
    dec_send_ref, recv_ref, out_ref,
    mesh_grad_ref, band_cot_ref, grads_ref,
    onehot_t0, onehot_t1, cot0, cot1, message_cot, totals, out_acc, node_cot, levels, turned_level, received_cot,
):
    step = pl.program_id(0)
    nodes, width = mesh_ref.shape
    edges = normed_ref.shape[0]
    band_rows = totals.shape[0]
    tiles = pl.num_programs(0) - 1
    tile = ENC_TILE
    degree = edges // tile
    scaling = degree ** (-0.5)
    cots = (cot0, cot1)
    onehots = (onehot_t0, onehot_t1)

    @pl.when(step == 0)
    def _():
        totals[...] = jnp.zeros_like(totals)
        cot = dot_nt(moved_cot_ref[...], dec_send_ref[...])
        node_cot[...] = cot
        spread = scaling * cot
        level = spread - jnp.mean(spread, axis=-1, keepdims=True)
        levels[...] = level
        turned_level[...] = dot_nt(level.astype(BF), out_ref[...])
        out_acc[...] = jnp.zeros_like(out_acc)

    def scatter(slot):
        totals[...] += dot(onehots[slot][...], cots[slot][...])

    def edge_part(slot, beside):
        strips = tile // STRIP
        total = [jnp.zeros((STRIP, width), F32)] * strips
        scales = scale_ref[...]
        for n in range(2):
            if beside is not None and n == 0:
                scatter(beside)
            for k in range(n * degree // 2, (n + 1) * degree // 2):
                for i in range(strips):
                    at = slice(k * tile + i * STRIP, k * tile + (i + 1) * STRIP)
                    mine = pl.ds(pl.multiple_of(step * tile + i * STRIP, STRIP), STRIP)
                    normed = normed_ref[at, :].astype(F32)
                    along = scaling * jnp.mean(node_cot[mine, :] * normed, axis=-1, keepdims=True)
                    scale = scales[i * STRIP : (i + 1) * STRIP, k : k + 1]
                    message_cot[at, :] = (scale * (levels[mine, :] - along * normed)).astype(BF)
                    turned = scale * (turned_level[mine, :] - along * turned_ref[at, :].astype(F32))
                    before_cot = slope_ref[at, :].astype(F32) * turned
                    total[i] = total[i] + before_cot
                    cots[slot][at, :] = before_cot.astype(BF)
            part = slice(n * edges // 2, (n + 1) * edges // 2)
            out_acc[...] += dot_tn(hidden_ref[part, :], message_cot[part, :])
        places = places_of((band_rows, edges), 0)
        spot = jnp.broadcast_to(idx_row_ref[0], (16, edges)).astype(jnp.int16)[:1]
        onehots[slot][...] = one_hot(spot, places)
        received_cot[pl.ds(pl.multiple_of(step * tile, tile), tile), :] = jnp.concatenate(total, axis=0).astype(BF)

    @pl.when(step == 0)
    def _():
        edge_part(0, None)

    for parity in range(2):
        @pl.when((step > 0) & (step < tiles) & (step % 2 == parity))
        def _():
            edge_part(parity, 1 - parity)

    @pl.when(step == tiles)
    def _():
        scatter(1)
        grads_ref[width : 2 * width, :] = dot_tn(mesh_ref[...], received_cot[...]).astype(BF)
        grads_ref[2 * width :, :] = out_acc[...].astype(BF)
        mesh_grad_ref[...] = (node_cot[...] + dot_nt(received_cot[...], recv_ref[...])).astype(BF)
        band_cot_ref[...] = totals[...].astype(BF)
        at = 0
        send_grad = jnp.zeros((width, width), F32)
        for piece in (own_ref, high_ref, low_ref, left_ref, right_ref):
            count = piece.shape[0]
            send_grad = send_grad + dot_tn(piece[...], band_cot_ref[at : at + count, :])
            at += count
        grads_ref[:width, :] = send_grad.astype(BF)


def enc_backward(idx_rows, scale, mesh_rows, moved_cot, normed, turned, slope, hidden, pieces, dec_send, enc_recv, enc_out):
    nodes, width = mesh_rows.shape
    degree = scale.shape[1]
    tile = ENC_TILE
    tiles = nodes // tile
    assert tiles % 2 == 0
    edges = normed.shape[0] // tiles
    band_rows = sum(p.shape[0] for p in pieces)
    square = whole((width, width))
    last = tiles - 1
    per_node = whole((nodes, width))
    per_edge = pl.BlockSpec((edges, width), lambda t: (jnp.minimum(t, last), 0))
    return pl.pallas_call(
        enc_backward_kernel,
        name="enc_backward",
        grid=(tiles + 1,),
        in_specs=[
            pl.BlockSpec((1, 1, edges), lambda t: (jnp.minimum(t, last), 0, 0)),
            pl.BlockSpec((tile, degree), lambda t: (jnp.minimum(t, last), 0)),
        ]
        + [per_node] * 2
        + [per_edge] * 4
        + [whole(p.shape) for p in pieces]
        + [square] * 3,
        out_specs=[per_node, whole((band_rows, width)), whole((3 * width, width))],
        out_shape=[
            jax.ShapeDtypeStruct((nodes, width), BF),
            jax.ShapeDtypeStruct((band_rows, width), BF),
            jax.ShapeDtypeStruct((3 * width, width), BF),
        ],
        scratch_shapes=[
            pltpu.VMEM((band_rows, edges), BF),
            pltpu.VMEM((band_rows, edges), BF),
            pltpu.VMEM((edges, width), BF),
            pltpu.VMEM((edges, width), BF),
            pltpu.VMEM((edges, width), BF),
            pltpu.VMEM((band_rows, width), F32),
            pltpu.VMEM((width, width), F32),
            pltpu.VMEM((nodes, width), F32),
            pltpu.VMEM((nodes, width), F32),
            pltpu.VMEM((nodes, width), F32),
            pltpu.VMEM((nodes, width), BF),
        ],
        compiler_params=kernel_params(56),
    )(idx_rows, scale, mesh_rows, moved_cot, normed, turned, slope, hidden, *pieces, dec_send, enc_recv, enc_out)


def to_lon(shard, by):
    count = lax.axis_size("lon")
    return lax.ppermute(shard, "lon", [(i, (i + by) % count) for i in range(count)])


def to_lat(shard, by):
    count = lax.axis_size("lat")
    return lax.ppermute(shard, "lat", [(i, i + by) for i in range(count) if 0 <= i + by < count])


def core_swap(array):
    return lax.ppermute(array, "lon", [(i, i ^ 1) for i in range(lax.axis_size("lon"))])


def across_chips(parts):
    count = lax.axis_size("lat") * lax.axis_size("lon")
    alike = [[i for i in range(count) if i % 2 == c] for c in range(2)]
    return lax.all_to_all(parts, ("lat", "lon"), 0, 0, axis_index_groups=alike, tiled=True)


def on_device(
    grid, mesh_nodes, grid_cot, enc_send, enc_recv, enc_out, dec_send, dec_recv, dec_out,
    enc_src, enc_live, dec_src,
):
    lat_cells, lon_cells, width = grid.shape
    slots, degree = enc_src.shape[2:]
    lat_index = lax.axis_index("lat")
    lon_index = lax.axis_index("lon")
    lon_count = lax.axis_size("lon")
    lon_total = lon_cells * lon_count
    cells = lat_cells * lon_cells
    edge_rows = REACH * lon_cells
    tall = lat_cells + 2 * REACH

    grid_rows = grid.reshape(cells, width)
    mesh_rows = mesh_nodes.reshape(slots, width)
    high = to_lat(grid_rows[:edge_rows], -1)
    low = to_lat(grid_rows[cells - edge_rows :], 1)
    inner = jnp.concatenate([grid_rows, high, low], axis=0).reshape(tall, lon_cells, width)
    left = to_lon(inner[:, lon_cells - REACH :].reshape(tall * REACH, width), 1)
    right = to_lon(inner[:, :REACH].reshape(tall * REACH, width), -1)
    pieces = (grid_rows, high, low, left, right)

    source = enc_src.reshape(slots, degree)
    row = (source // lon_total - lat_index * lat_cells) % tall
    col = (source % lon_total - lon_index * lon_cells + REACH) % lon_total - REACH
    inner_rows = tall * lon_cells
    enc_idx = jnp.where(
        col < 0,
        inner_rows + row * REACH + col + REACH,
        jnp.where(
            col >= lon_cells,
            inner_rows + tall * REACH + row * REACH + col - lon_cells,
            row * lon_cells + col,
        ),
    )
    tiles = slots // ENC_TILE
    enc_idx_rows = enc_idx.reshape(tiles, ENC_TILE, degree).transpose(0, 2, 1)
    enc_idx_rows = enc_idx_rows.reshape(tiles, 1, ENC_TILE * degree)
    counts = jnp.sum(enc_live.reshape(slots, degree), axis=1, keepdims=True)

    picks = dec_src.reshape(3, cells)
    owner = picks // slots
    owner_lat = (owner // lon_count - lat_index) % 3
    owner_lon = (owner % lon_count - lon_index + lon_count) % lon_count
    owner_lon = jnp.where(owner_lon == lon_count - 1, 1, owner_lon * 2)
    dec_idx_rows = (owner_lon * 3 + owner_lat) * slots + picks % slots

    mesh_new, moved, slope, hidden, normed, scale = enc_forward(
        enc_idx, counts, mesh_rows, pieces, enc_send, enc_recv, enc_out, dec_send
    )

    above = to_lat(moved, -1)
    below = to_lat(moved, 1)
    half = slots * degree // 2
    block = half // 4
    part = enc_between(normed, enc_out, 0, 4, block)
    centre = jnp.concatenate([moved, above, below], axis=0)
    centre, part = lax.optimization_barrier((centre, part))
    west = to_lon(centre, 1)
    east = to_lon(centre, -1)
    turned = enc_between(normed, enc_out, 4, 4, block, part)
    west, east, turned = lax.optimization_barrier((west, east, turned))
    cot_rows = grid_cot.reshape(cells, width)
    grid_new, dec_hidden, dec_message_cot, dec_before_cot, dec_received_cot, west_tot, east_tot = decoder(
        dec_idx_rows.T, dec_idx_rows, grid_rows, cot_rows, centre, west, east, dec_recv, dec_out
    )
    from_east = to_lon(west_tot, -1)
    from_west = to_lon(east_tot, 1)
    grid_part, dec_out_grad, dec_recv_grad, centre_tot = decoder_rest(
        dec_idx_rows, grid_rows, cot_rows, dec_hidden, dec_message_cot, dec_before_cot, dec_received_cot,
        dec_recv, 3 * slots,
    )
    def met(at):
        return centre_tot[at].astype(F32) + from_east[at].astype(F32) + from_west[at].astype(F32)

    from_below = to_lat(met(slice(slots, 2 * slots)).astype(BF), 1)
    from_above = to_lat(met(slice(2 * slots, 3 * slots)).astype(BF), -1)
    moved_cot = met(slice(0, slots)) + from_below.astype(F32) + from_above.astype(F32)
    moved_cot = moved_cot.astype(BF)
    dec_send_grad = dot_tn(mesh_new, moved_cot).astype(BF)

    mesh_grad, band_cot, enc_stack = enc_backward(
        enc_idx_rows, scale, mesh_rows, moved_cot, normed, turned, slope, hidden, pieces, dec_send, enc_recv, enc_out
    )
    dec_stack = jnp.concatenate([dec_send_grad, dec_recv_grad, dec_out_grad], axis=0)

    side = tall * REACH
    from_right = to_lon(band_cot[inner_rows : inner_rows + side], -1)
    from_left = to_lon(band_cot[inner_rows + side :], 1)

    leads = lon_index % 2 == 0
    chips = lax.axis_size("lat") * lon_count // 2
    swapped = core_swap(jnp.where(leads, dec_stack, enc_stack))
    kept = jnp.where(leads, enc_stack, dec_stack).astype(F32) + swapped.astype(F32)
    kept = kept.astype(BF).reshape(chips, 3 * width // chips, width)

    def met_cells(first, count):
        rows = band_cot[first * lon_cells : (first + count) * lon_cells].astype(F32).reshape(count, lon_cells, width)
        at = slice(first * REACH, (first + count) * REACH)
        gap = jnp.zeros((count, lon_cells - 2 * REACH, width), F32)
        east = from_right[at].astype(F32).reshape(count, REACH, width)
        west = from_left[at].astype(F32).reshape(count, REACH, width)
        return (rows + jnp.concatenate([west, gap, east], axis=1)).reshape(count * lon_cells, width)

    to_upper = met_cells(lat_cells, REACH).astype(BF)
    to_lower = met_cells(lat_cells + REACH, REACH).astype(BF)
    kept, to_upper, to_lower = lax.optimization_barrier((kept, to_upper, to_lower))
    from_low = to_lat(to_upper, 1)
    from_high = to_lat(to_lower, -1)

    mine = jnp.sum(across_chips(kept).astype(F32), axis=0).astype(BF)
    mine, from_low, from_high = lax.optimization_barrier((mine, from_low, from_high))
    ours = across_chips(jnp.broadcast_to(mine[None], kept.shape)).reshape(3 * width, width)
    theirs = core_swap(ours)
    enc_grads = jnp.where(leads, ours, theirs).astype(F32)
    dec_grads = jnp.where(leads, theirs, ours).astype(F32)

    sent_cot = met_cells(0, lat_cells) + jnp.concatenate([from_low, from_high], axis=0).astype(F32)
    grid_grad = (grid_part + dot_nt(sent_cot.astype(BF), enc_send)).astype(BF)

    return (
        grid_new.reshape(grid.shape),
        grid_grad.reshape(grid.shape),
        mesh_grad.reshape(mesh_nodes.shape),
        enc_grads[:width],
        enc_grads[width : 2 * width],
        enc_grads[2 * width :],
        dec_grads[:width],
        dec_grads[width : 2 * width],
        dec_grads[2 * width :],
    )


def solution(mesh):
    node = P("lat", "lon", None)
    block = P("lat", "lon", None, None)
    placed = (
        node, block, node, P(), P(), P(), P(), P(), P(), block, block, P(None, "lat", "lon"),
    )
    return jax.shard_map(
        on_device,
        mesh=mesh,
        in_specs=placed,
        out_specs=(node, node, block, P(), P(), P(), P(), P(), P()),
        check_vma=False,
    )
```

```python
import jax
import jax.numpy as jnp
from jax import lax
from jax.experimental import pallas as pl
from jax.experimental.pallas import tpu as pltpu
from jax.sharding import PartitionSpec as P

REACH = 4
NORM_EPSILON = 1e-05
BF = jnp.bfloat16
F32 = jnp.float32
MIB = 1024 * 1024
ENC_TILE = 32
ENC_CHUNK = 4
STRIP = 16
DEC_TILE = 256


def dot(a, b):
    return jnp.dot(a, b, preferred_element_type=F32)


def dot_nt(a, b):
    return lax.dot_general(a, b, (((1,), (1,)), ((), ())), preferred_element_type=F32)


def dot_tn(a, b):
    return lax.dot_general(a, b, (((0,), (0,)), ((), ())), preferred_element_type=F32)


def sigma(v):
    return 0.5 * jnp.tanh(0.5 * v) + 0.5


def normalise(message):
    centred = message - jnp.mean(message, axis=-1, keepdims=True)
    factor = lax.rsqrt(jnp.mean(centred * centred, axis=-1, keepdims=True) + NORM_EPSILON)
    return centred, factor


def one_hot(index, places):
    return jnp.where(index == places, BF(1.0), BF(0.0))


def places_of(shape, dim):
    return lax.broadcasted_iota(jnp.int32, shape, dim).astype(jnp.int16)


def staggered(stages, count):
    for i in range(count + len(stages) - 1):
        for d in range(len(stages) - 1, -1, -1):
            if 0 <= i - d < count:
                stages[d](i - d)


def kernel_params(mib=56):
    return pltpu.CompilerParams(vmem_limit_bytes=mib * MIB)


def whole(shape):
    return pl.BlockSpec(shape, lambda t: (0,) * len(shape))


def rows_of(count, width):
    return pl.BlockSpec((count, width), lambda t: (t, 0))


def enc_forward_kernel(
    idx_ref, count_ref, mesh_ref, own_ref, high_ref, low_ref, left_ref, right_ref,
    send_ref, recv_ref, out_ref, dec_send_ref,
    new_ref, moved_ref, slope_ref, hidden_ref, normed_ref, scale_ref,
    band, onehot, received_all,
):
    step = pl.program_id(0)
    tile, degree = idx_ref.shape
    width = mesh_ref.shape[1]
    band_rows = band.shape[0]
    own = pl.ds(pl.multiple_of(step * tile, tile), tile)

    @pl.when(step == 0)
    def _():
        received_all[...] = dot(mesh_ref[...], recv_ref[...])
        at = 0
        for piece in (own_ref, high_ref, low_ref, left_ref, right_ref):
            count = piece.shape[0]
            band[at : at + count, :] = dot(piece[...], send_ref[...]).astype(BF)
            at += count

    places = places_of((tile, band_rows), 1)
    index = idx_ref[...].astype(jnp.int16)
    received = received_all[own, :]
    lane = lax.broadcasted_iota(jnp.int32, (tile, degree), 1)
    rows = ENC_CHUNK * tile
    state = {"total": jnp.zeros((tile, width), F32), "scales": jnp.zeros((tile, degree), F32)}
    held = {}

    def place(c):
        for k in range(c * ENC_CHUNK, (c + 1) * ENC_CHUNK):
            onehot[k * tile : (k + 1) * tile, :] = one_hot(index[:, k : k + 1], places)

    def gather(c):
        held["gathered", c] = dot(onehot[c * rows : (c + 1) * rows, :], band[...])

    def activate(c):
        before = held.pop(("gathered", c)).reshape(ENC_CHUNK, tile, width) + received[None]
        sig = sigma(before)
        silu = before * sig
        part = slice(c * rows, (c + 1) * rows)
        slope_ref[part, :] = (sig + silu * (1.0 - sig)).reshape(rows, width).astype(BF)
        hidden = silu.reshape(rows, width).astype(BF)
        hidden_ref[part, :] = hidden
        held["hidden", c] = hidden

    def project(c):
        held["message", c] = dot(held.pop(("hidden", c)), out_ref[...])

    def norm(c):
        centred, factor = normalise(held.pop(("message", c)))
        normed = (centred * factor).reshape(ENC_CHUNK, tile, width)
        normed_ref[c * rows : (c + 1) * rows, :] = normed.reshape(rows, width).astype(BF)
        factor = factor.reshape(ENC_CHUNK, tile, 1)
        for j in range(ENC_CHUNK):
            k = c * ENC_CHUNK + j
            live = jnp.where(count_ref[...] > k, 1.0, 0.0)
            state["total"] = state["total"] + normed[j] * live
            state["scales"] = jnp.where(lane == k, factor[j] * live, state["scales"])

    staggered([place, gather, activate, project, norm], degree // ENC_CHUNK)
    scale_ref[...] = state["scales"]
    nodes = mesh_ref[own, :].astype(F32)
    new_ref[own, :] = (nodes + degree ** (-0.5) * state["total"]).astype(BF)

    @pl.when(step == pl.num_programs(0) - 1)
    def _():
        moved_ref[...] = dot(new_ref[...], dec_send_ref[...]).astype(BF)


def enc_forward(idx, counts, mesh_rows, pieces, enc_send, enc_recv, enc_out, dec_send):
    nodes, degree = idx.shape
    width = mesh_rows.shape[1]
    tile = ENC_TILE
    edges = tile * degree
    band_rows = sum(p.shape[0] for p in pieces)
    square = whole((width, width))
    return pl.pallas_call(
        enc_forward_kernel,
        name="enc_forward",
        grid=(nodes // tile,),
        in_specs=[rows_of(tile, degree), rows_of(tile, 1), whole((nodes, width))]
        + [whole(p.shape) for p in pieces]
        + [square] * 4,
        out_specs=[
            whole((nodes, width)), whole((nodes, width)),
            rows_of(edges, width), rows_of(edges, width), rows_of(edges, width), rows_of(tile, degree),
        ],
        out_shape=[
            jax.ShapeDtypeStruct((nodes, width), BF),
            jax.ShapeDtypeStruct((nodes, width), BF),
            jax.ShapeDtypeStruct((nodes * degree, width), BF),
            jax.ShapeDtypeStruct((nodes * degree, width), BF),
            jax.ShapeDtypeStruct((nodes * degree, width), BF),
            jax.ShapeDtypeStruct((nodes, degree), F32),
        ],
        scratch_shapes=[
            pltpu.VMEM((band_rows, width), BF),
            pltpu.VMEM((edges, band_rows), BF),
            pltpu.VMEM((nodes, width), F32),
        ],
        compiler_params=kernel_params(56),
    )(idx, counts, mesh_rows, *pieces, enc_send, enc_recv, enc_out, dec_send)


def enc_between_kernel(normed_ref, out_ref, *refs):
    refs[-1][...] = dot_nt(normed_ref[...], out_ref[...]).astype(BF)


def enc_between(normed, enc_out, first, count, rows, done=None):
    width = normed.shape[1]
    per_edge = pl.BlockSpec((rows, width), lambda t: (t + first, 0))
    share = count * rows * width
    kept = () if done is None else (done,)
    return pl.pallas_call(
        enc_between_kernel,
        name="enc_between",
        grid=(count,),
        in_specs=[per_edge, whole((width, width))] + [pl.BlockSpec(memory_space=pl.ANY)] * len(kept),
        out_specs=per_edge,
        out_shape=jax.ShapeDtypeStruct(normed.shape, BF),
        input_output_aliases={2: 0} if kept else {},
        compiler_params=kernel_params(56),
        cost_estimate=pl.CostEstimate(flops=2 * share * width, bytes_accessed=4 * share, transcendentals=0),
    )(normed, enc_out, *kept)


def decoder_kernel(
    idx_ref, idx_row_ref, grid_ref, cot_ref, centre_ref, left_ref, right_ref,
    recv_ref, out_ref,
    new_ref, hidden_ref, message_cot_ref, before_cot_ref, received_cot_ref, left_tot_ref, right_tot_ref,
    onehot, onehot_t, received_all, new_all, received_cot_all,
):
    nodes, width = grid_ref.shape
    degree = idx_ref.shape[1]
    third = centre_ref.shape[0]
    tile = DEC_TILE
    parts = nodes // tile
    index = idx_ref[...].astype(jnp.int16)
    places = places_of((tile, 3 * third), 1)
    held = {}

    received_all[...] = dot(grid_ref[...], recv_ref[...])

    def spot(i):
        h, j = divmod(i, degree)
        return j, slice(h * tile, (h + 1) * tile), slice(i * tile, (i + 1) * tile)

    def place(i):
        j, at, edges = spot(i)
        onehot[edges, :] = one_hot(index[at, j : j + 1], places)

    def gather(i):
        j, at, edges = spot(i)
        gathered = dot(onehot[edges, :third], centre_ref[...])
        gathered = gathered + dot(onehot[edges, third : 2 * third], left_ref[...])
        held["gathered", i] = gathered + dot(onehot[edges, 2 * third :], right_ref[...])

    def activate(i):
        j, at, edges = spot(i)
        before = held.pop(("gathered", i)) + received_all[at, :]
        sig = sigma(before)
        silu = before * sig
        hidden = silu.astype(BF)
        hidden_ref[edges, :] = hidden
        held["slope", i] = sig + silu * (1.0 - sig)
        held["message", i] = dot(hidden, out_ref[...])

    def norm(i):
        j, at, edges = spot(i)
        centred, factor = normalise(held.pop(("message", i)))
        normed = centred * factor
        cot = cot_ref[at, :].astype(F32)
        level = cot - jnp.mean(cot, axis=-1, keepdims=True)
        along = jnp.mean(cot * normed, axis=-1, keepdims=True)
        message_cot = (factor * (level - normed * along)).astype(BF)
        message_cot_ref[edges, :] = message_cot
        held["hidden_cot", i] = dot_nt(message_cot, out_ref[...])
        if j == 0:
            new_all[at, :] = grid_ref[at, :].astype(F32) + normed
        else:
            new_all[at, :] += normed

    def back(i):
        j, at, edges = spot(i)
        before_cot = held.pop(("hidden_cot", i)) * held.pop(("slope", i))
        before_cot_ref[edges, :] = before_cot.astype(BF)
        if j == 0:
            received_cot_all[at, :] = before_cot
        else:
            received_cot_all[at, :] += before_cot
        rows = lax.broadcasted_iota(jnp.int32, (2 * third, tile), 0) + third
        picks = jnp.broadcast_to(idx_row_ref[j : j + 1, at], (16, tile)).astype(jnp.int16)[:1]
        onehot_t[:, edges] = one_hot(picks, rows.astype(jnp.int16))

    staggered([place, gather, activate, norm, back], degree * parts)
    left_tot_ref[...] = dot(onehot_t[:third, :], before_cot_ref[...]).astype(BF)
    new_ref[...] = new_all[...].astype(BF)
    right_tot_ref[...] = dot(onehot_t[third:, :], before_cot_ref[...]).astype(BF)
    received_cot_ref[...] = received_cot_all[...].astype(BF)


def decoder(idx, idx_rows, grid_rows, cot_rows, centre, left, right, dec_recv, dec_out):
    nodes, width = grid_rows.shape
    degree = idx.shape[1]
    third = centre.shape[0]
    edge_shape = jax.ShapeDtypeStruct((degree * nodes, width), BF)
    node_shape = jax.ShapeDtypeStruct((nodes, width), BF)
    side_shape = jax.ShapeDtypeStruct((third, width), BF)
    return pl.pallas_call(
        decoder_kernel,
        name="decoder",
        out_shape=[node_shape, edge_shape, edge_shape, edge_shape, node_shape, side_shape, side_shape],
        scratch_shapes=[
            pltpu.VMEM((degree * nodes, 3 * third), BF),
            pltpu.VMEM((2 * third, degree * nodes), BF),
            pltpu.VMEM((nodes, width), F32),
            pltpu.VMEM((nodes, width), F32),
            pltpu.VMEM((nodes, width), F32),
        ],
        compiler_params=kernel_params(36),
    )(idx, idx_rows, grid_rows, cot_rows, centre, left, right, dec_recv, dec_out)


def decoder_rest_kernel(
    idx_row_ref, grid_ref, cot_ref, hidden_ref, message_cot_ref, before_cot_ref, received_cot_ref, recv_ref,
    part_ref, out_grad_ref, recv_grad_ref, centre_tot_ref,
    onehot_t,
):
    third, width = centre_tot_ref.shape
    degree, nodes = idx_row_ref.shape
    tile = DEC_TILE
    rows = places_of((third, tile), 0)
    for i in range(degree * nodes // tile):
        h, j = divmod(i, degree)
        picks = jnp.broadcast_to(idx_row_ref[j : j + 1, h * tile : (h + 1) * tile], (16, tile))
        onehot_t[:, i * tile : (i + 1) * tile] = one_hot(picks.astype(jnp.int16)[:1], rows)
    centre_tot_ref[...] = dot(onehot_t[...], before_cot_ref[...]).astype(BF)
    out_grad_ref[...] = dot_tn(hidden_ref[...], message_cot_ref[...]).astype(BF)
    received_cot = received_cot_ref[...]
    recv_grad_ref[...] = dot_tn(grid_ref[...], received_cot).astype(BF)
    part_ref[...] = cot_ref[...].astype(F32) + dot_nt(received_cot, recv_ref[...])


def decoder_rest(idx_rows, grid_rows, cot_rows, hidden, message_cot, before_cot, received_cot, dec_recv, third):
    degree, nodes = idx_rows.shape
    width = hidden.shape[1]
    return pl.pallas_call(
        decoder_rest_kernel,
        name="decoder_rest",
        out_shape=[
            jax.ShapeDtypeStruct((nodes, width), F32),
            jax.ShapeDtypeStruct((width, width), BF),
            jax.ShapeDtypeStruct((width, width), BF),
            jax.ShapeDtypeStruct((third, width), BF),
        ],
        scratch_shapes=[pltpu.VMEM((third, degree * nodes), BF)],
        compiler_params=kernel_params(20),
        cost_estimate=pl.CostEstimate(
            flops=2 * degree * nodes * width * (third + 2 * width), bytes_accessed=8 * degree * nodes * width,
            transcendentals=0,
        ),
    )(idx_rows, grid_rows, cot_rows, hidden, message_cot, before_cot, received_cot, dec_recv)


def enc_backward_kernel(
    idx_row_ref, scale_ref, mesh_ref, moved_cot_ref, normed_ref, turned_ref, slope_ref, hidden_ref,
    own_ref, high_ref, low_ref, left_ref, right_ref,
    dec_send_ref, recv_ref, out_ref,
    mesh_grad_ref, band_cot_ref, grads_ref,
    onehot_t0, onehot_t1, cot0, cot1, message_cot, totals, out_acc, node_cot, levels, turned_level, received_cot,
):
    step = pl.program_id(0)
    nodes, width = mesh_ref.shape
    edges = normed_ref.shape[0]
    band_rows = totals.shape[0]
    tiles = pl.num_programs(0) - 1
    tile = ENC_TILE
    degree = edges // tile
    scaling = degree ** (-0.5)
    cots = (cot0, cot1)
    onehots = (onehot_t0, onehot_t1)

    @pl.when(step == 0)
    def _():
        totals[...] = jnp.zeros_like(totals)
        cot = dot_nt(moved_cot_ref[...], dec_send_ref[...])
        node_cot[...] = cot
        spread = scaling * cot
        level = spread - jnp.mean(spread, axis=-1, keepdims=True)
        levels[...] = level
        turned_level[...] = dot_nt(level.astype(BF), out_ref[...])
        out_acc[...] = jnp.zeros_like(out_acc)

    def scatter(slot):
        totals[...] += dot(onehots[slot][...], cots[slot][...])

    def edge_part(slot, beside):
        strips = tile // STRIP
        total = [jnp.zeros((STRIP, width), F32)] * strips
        scales = scale_ref[...]
        for n in range(2):
            if beside is not None and n == 0:
                scatter(beside)
            for k in range(n * degree // 2, (n + 1) * degree // 2):
                for i in range(strips):
                    at = slice(k * tile + i * STRIP, k * tile + (i + 1) * STRIP)
                    mine = pl.ds(pl.multiple_of(step * tile + i * STRIP, STRIP), STRIP)
                    normed = normed_ref[at, :].astype(F32)
                    along = scaling * jnp.mean(node_cot[mine, :] * normed, axis=-1, keepdims=True)
                    scale = scales[i * STRIP : (i + 1) * STRIP, k : k + 1]
                    message_cot[at, :] = (scale * (levels[mine, :] - along * normed)).astype(BF)
                    turned = scale * (turned_level[mine, :] - along * turned_ref[at, :].astype(F32))
                    before_cot = slope_ref[at, :].astype(F32) * turned
                    total[i] = total[i] + before_cot
                    cots[slot][at, :] = before_cot.astype(BF)
            part = slice(n * edges // 2, (n + 1) * edges // 2)
            out_acc[...] += dot_tn(hidden_ref[part, :], message_cot[part, :])
        places = places_of((band_rows, edges), 0)
        spot = jnp.broadcast_to(idx_row_ref[0], (16, edges)).astype(jnp.int16)[:1]
        onehots[slot][...] = one_hot(spot, places)
        received_cot[pl.ds(pl.multiple_of(step * tile, tile), tile), :] = jnp.concatenate(total, axis=0).astype(BF)

    @pl.when(step == 0)
    def _():
        edge_part(0, None)

    for parity in range(2):
        @pl.when((step > 0) & (step < tiles) & (step % 2 == parity))
        def _():
            edge_part(parity, 1 - parity)

    @pl.when(step == tiles)
    def _():
        scatter(1)
        grads_ref[width : 2 * width, :] = dot_tn(mesh_ref[...], received_cot[...]).astype(BF)
        grads_ref[2 * width :, :] = out_acc[...].astype(BF)
        mesh_grad_ref[...] = (node_cot[...] + dot_nt(received_cot[...], recv_ref[...])).astype(BF)
        band_cot_ref[...] = totals[...].astype(BF)
        at = 0
        send_grad = jnp.zeros((width, width), F32)
        for piece in (own_ref, high_ref, low_ref, left_ref, right_ref):
            count = piece.shape[0]
            send_grad = send_grad + dot_tn(piece[...], band_cot_ref[at : at + count, :])
            at += count
        grads_ref[:width, :] = send_grad.astype(BF)


def enc_backward(idx_rows, scale, mesh_rows, moved_cot, normed, turned, slope, hidden, pieces, dec_send, enc_recv, enc_out):
    nodes, width = mesh_rows.shape
    degree = scale.shape[1]
    tile = ENC_TILE
    tiles = nodes // tile
    assert tiles % 2 == 0
    edges = normed.shape[0] // tiles
    band_rows = sum(p.shape[0] for p in pieces)
    square = whole((width, width))
    last = tiles - 1
    per_node = whole((nodes, width))
    per_edge = pl.BlockSpec((edges, width), lambda t: (jnp.minimum(t, last), 0))
    return pl.pallas_call(
        enc_backward_kernel,
        name="enc_backward",
        grid=(tiles + 1,),
        in_specs=[
            pl.BlockSpec((1, 1, edges), lambda t: (jnp.minimum(t, last), 0, 0)),
            pl.BlockSpec((tile, degree), lambda t: (jnp.minimum(t, last), 0)),
        ]
        + [per_node] * 2
        + [per_edge] * 4
        + [whole(p.shape) for p in pieces]
        + [square] * 3,
        out_specs=[per_node, whole((band_rows, width)), whole((3 * width, width))],
        out_shape=[
            jax.ShapeDtypeStruct((nodes, width), BF),
            jax.ShapeDtypeStruct((band_rows, width), BF),
            jax.ShapeDtypeStruct((3 * width, width), BF),
        ],
        scratch_shapes=[
            pltpu.VMEM((band_rows, edges), BF),
            pltpu.VMEM((band_rows, edges), BF),
            pltpu.VMEM((edges, width), BF),
            pltpu.VMEM((edges, width), BF),
            pltpu.VMEM((edges, width), BF),
            pltpu.VMEM((band_rows, width), F32),
            pltpu.VMEM((width, width), F32),
            pltpu.VMEM((nodes, width), F32),
            pltpu.VMEM((nodes, width), F32),
            pltpu.VMEM((nodes, width), F32),
            pltpu.VMEM((nodes, width), BF),
        ],
        compiler_params=kernel_params(56),
    )(idx_rows, scale, mesh_rows, moved_cot, normed, turned, slope, hidden, *pieces, dec_send, enc_recv, enc_out)


def to_lon(shard, by):
    count = lax.axis_size("lon")
    return lax.ppermute(shard, "lon", [(i, (i + by) % count) for i in range(count)])


def to_lat(shard, by):
    count = lax.axis_size("lat")
    return lax.ppermute(shard, "lat", [(i, i + by) for i in range(count) if 0 <= i + by < count])


def core_swap(array):
    return lax.ppermute(array, "lon", [(i, i ^ 1) for i in range(lax.axis_size("lon"))])


def across_chips(parts):
    count = lax.axis_size("lat") * lax.axis_size("lon")
    alike = [[i for i in range(count) if i % 2 == c] for c in range(2)]
    return lax.all_to_all(parts, ("lat", "lon"), 0, 0, axis_index_groups=alike, tiled=True)


def on_device(
    grid, mesh_nodes, grid_cot, enc_send, enc_recv, enc_out, dec_send, dec_recv, dec_out,
    enc_src, enc_live, dec_src,
):
    lat_cells, lon_cells, width = grid.shape
    slots, degree = enc_src.shape[2:]
    lat_index = lax.axis_index("lat")
    lon_index = lax.axis_index("lon")
    lon_count = lax.axis_size("lon")
    lon_total = lon_cells * lon_count
    cells = lat_cells * lon_cells
    edge_rows = REACH * lon_cells
    tall = lat_cells + 2 * REACH

    grid_rows = grid.reshape(cells, width)
    mesh_rows = mesh_nodes.reshape(slots, width)
    high = to_lat(grid_rows[:edge_rows], -1)
    low = to_lat(grid_rows[cells - edge_rows :], 1)
    inner = jnp.concatenate([grid_rows, high, low], axis=0).reshape(tall, lon_cells, width)
    left = to_lon(inner[:, lon_cells - REACH :].reshape(tall * REACH, width), 1)
    right = to_lon(inner[:, :REACH].reshape(tall * REACH, width), -1)
    pieces = (grid_rows, high, low, left, right)

    source = enc_src.reshape(slots, degree)
    row = (source // lon_total - lat_index * lat_cells) % tall
    col = (source % lon_total - lon_index * lon_cells + REACH) % lon_total - REACH
    inner_rows = tall * lon_cells
    enc_idx = jnp.where(
        col < 0,
        inner_rows + row * REACH + col + REACH,
        jnp.where(
            col >= lon_cells,
            inner_rows + tall * REACH + row * REACH + col - lon_cells,
            row * lon_cells + col,
        ),
    )
    tiles = slots // ENC_TILE
    enc_idx_rows = enc_idx.reshape(tiles, ENC_TILE, degree).transpose(0, 2, 1)
    enc_idx_rows = enc_idx_rows.reshape(tiles, 1, ENC_TILE * degree)
    counts = jnp.sum(enc_live.reshape(slots, degree), axis=1, keepdims=True)

    picks = dec_src.reshape(3, cells)
    owner = picks // slots
    owner_lat = (owner // lon_count - lat_index) % 3
    owner_lon = (owner % lon_count - lon_index + lon_count) % lon_count
    owner_lon = jnp.where(owner_lon == lon_count - 1, 1, owner_lon * 2)
    dec_idx_rows = (owner_lon * 3 + owner_lat) * slots + picks % slots

    mesh_new, moved, slope, hidden, normed, scale = enc_forward(
        enc_idx, counts, mesh_rows, pieces, enc_send, enc_recv, enc_out, dec_send
    )

    above = to_lat(moved, -1)
    below = to_lat(moved, 1)
    half = slots * degree // 2
    block = half // 4
    part = enc_between(normed, enc_out, 0, 4, block)
    centre = jnp.concatenate([moved, above, below], axis=0)
    centre, part = lax.optimization_barrier((centre, part))
    west = to_lon(centre, 1)
    east = to_lon(centre, -1)
    turned = enc_between(normed, enc_out, 4, 4, block, part)
    west, east, turned = lax.optimization_barrier((west, east, turned))
    cot_rows = grid_cot.reshape(cells, width)
    grid_new, dec_hidden, dec_message_cot, dec_before_cot, dec_received_cot, west_tot, east_tot = decoder(
        dec_idx_rows.T, dec_idx_rows, grid_rows, cot_rows, centre, west, east, dec_recv, dec_out
    )
    from_east = to_lon(west_tot, -1)
    from_west = to_lon(east_tot, 1)
    grid_part, dec_out_grad, dec_recv_grad, centre_tot = decoder_rest(
        dec_idx_rows, grid_rows, cot_rows, dec_hidden, dec_message_cot, dec_before_cot, dec_received_cot,
        dec_recv, 3 * slots,
    )
    def met(at):
        return centre_tot[at].astype(F32) + from_east[at].astype(F32) + from_west[at].astype(F32)

    from_below = to_lat(met(slice(slots, 2 * slots)).astype(BF), 1)
    from_above = to_lat(met(slice(2 * slots, 3 * slots)).astype(BF), -1)
    moved_cot = met(slice(0, slots)) + from_below.astype(F32) + from_above.astype(F32)
    moved_cot = moved_cot.astype(BF)
    dec_send_grad = dot_tn(mesh_new, moved_cot).astype(BF)

    mesh_grad, band_cot, enc_stack = enc_backward(
        enc_idx_rows, scale, mesh_rows, moved_cot, normed, turned, slope, hidden, pieces, dec_send, enc_recv, enc_out
    )
    dec_stack = jnp.concatenate([dec_send_grad, dec_recv_grad, dec_out_grad], axis=0)

    side = tall * REACH
    from_right = to_lon(band_cot[inner_rows : inner_rows + side], -1)
    from_left = to_lon(band_cot[inner_rows + side :], 1)

    leads = lon_index % 2 == 0
    chips = lax.axis_size("lat") * lon_count // 2
    swapped = core_swap(jnp.where(leads, dec_stack, enc_stack))
    kept = jnp.where(leads, enc_stack, dec_stack).astype(F32) + swapped.astype(F32)
    kept = kept.astype(BF).reshape(chips, 3 * width // chips, width)
    kept, from_right, from_left = lax.optimization_barrier((kept, from_right, from_left))

    inner_cot = band_cot[:inner_rows].astype(F32).reshape(tall, lon_cells, width)
    inner_cot = inner_cot.at[:, lon_cells - REACH :].add(from_right.astype(F32).reshape(tall, REACH, width))
    inner_cot = inner_cot.at[:, :REACH].add(from_left.astype(F32).reshape(tall, REACH, width))
    inner_cot = inner_cot.reshape(inner_rows, width)
    from_low = to_lat(inner_cot[cells : cells + edge_rows].astype(BF), 1)
    from_high = to_lat(inner_cot[cells + edge_rows :].astype(BF), -1)

    mine = jnp.sum(across_chips(kept).astype(F32), axis=0).astype(BF)
    mine, from_low, from_high = lax.optimization_barrier((mine, from_low, from_high))
    ours = across_chips(jnp.broadcast_to(mine[None], kept.shape)).reshape(3 * width, width)
    theirs = core_swap(ours)
    enc_grads = jnp.where(leads, ours, theirs).astype(F32)
    dec_grads = jnp.where(leads, theirs, ours).astype(F32)

    sent_cot = inner_cot[:cells] + jnp.concatenate([from_low, from_high], axis=0).astype(F32)
    grid_grad = (grid_part + dot_nt(sent_cot.astype(BF), enc_send)).astype(BF)

    return (
        grid_new.reshape(grid.shape),
        grid_grad.reshape(grid.shape),
        mesh_grad.reshape(mesh_nodes.shape),
        enc_grads[:width],
        enc_grads[width : 2 * width],
        enc_grads[2 * width :],
        dec_grads[:width],
        dec_grads[width : 2 * width],
        dec_grads[2 * width :],
    )


def solution(mesh):
    node = P("lat", "lon", None)
    block = P("lat", "lon", None, None)
    placed = (
        node, block, node, P(), P(), P(), P(), P(), P(), block, block, P(None, "lat", "lon"),
    )
    return jax.shard_map(
        on_device,
        mesh=mesh,
        in_specs=placed,
        out_specs=(node, node, block, P(), P(), P(), P(), P(), P()),
        check_vma=False,
    )
```

```python
import jax
import jax.numpy as jnp
from jax import lax
from jax.experimental import pallas as pl
from jax.experimental.pallas import tpu as pltpu
from jax.sharding import PartitionSpec as P

REACH = 4
NORM_EPSILON = 1e-05
BF = jnp.bfloat16
F32 = jnp.float32
MIB = 1024 * 1024
ENC_TILE = 32
ENC_CHUNK = 4
STRIP = 16
DEC_TILE = 256


def dot(a, b):
    return jnp.dot(a, b, preferred_element_type=F32)


def dot_nt(a, b):
    return lax.dot_general(a, b, (((1,), (1,)), ((), ())), preferred_element_type=F32)


def dot_tn(a, b):
    return lax.dot_general(a, b, (((0,), (0,)), ((), ())), preferred_element_type=F32)


def sigma(v):
    return 0.5 * jnp.tanh(0.5 * v) + 0.5


def normalise(message):
    centred = message - jnp.mean(message, axis=-1, keepdims=True)
    factor = lax.rsqrt(jnp.mean(centred * centred, axis=-1, keepdims=True) + NORM_EPSILON)
    return centred, factor


def one_hot(index, places):
    return jnp.where(index == places, BF(1.0), BF(0.0))


def places_of(shape, dim):
    return lax.broadcasted_iota(jnp.int32, shape, dim).astype(jnp.int16)


def staggered(stages, count):
    for i in range(count + len(stages) - 1):
        for d in range(len(stages) - 1, -1, -1):
            if 0 <= i - d < count:
                stages[d](i - d)


def kernel_params(mib=56):
    return pltpu.CompilerParams(vmem_limit_bytes=mib * MIB)


def whole(shape):
    return pl.BlockSpec(shape, lambda t: (0,) * len(shape))


def rows_of(count, width):
    return pl.BlockSpec((count, width), lambda t: (t, 0))


def enc_forward_kernel(
    idx_ref, count_ref, mesh_ref, own_ref, high_ref, low_ref, left_ref, right_ref,
    send_ref, recv_ref, out_ref, dec_send_ref,
    new_ref, moved_ref, slope_ref, hidden_ref, normed_ref, scale_ref,
    band, onehot, received_all,
):
    step = pl.program_id(0)
    tile, degree = idx_ref.shape
    width = mesh_ref.shape[1]
    band_rows = band.shape[0]
    own = pl.ds(pl.multiple_of(step * tile, tile), tile)

    @pl.when(step == 0)
    def _():
        received_all[...] = dot(mesh_ref[...], recv_ref[...])
        at = 0
        for piece in (own_ref, high_ref, low_ref, left_ref, right_ref):
            count = piece.shape[0]
            band[at : at + count, :] = dot(piece[...], send_ref[...]).astype(BF)
            at += count

    places = places_of((tile, band_rows), 1)
    index = idx_ref[...].astype(jnp.int16)
    received = received_all[own, :]
    lane = lax.broadcasted_iota(jnp.int32, (tile, degree), 1)
    rows = ENC_CHUNK * tile
    state = {"total": jnp.zeros((tile, width), F32), "scales": jnp.zeros((tile, degree), F32)}
    held = {}

    def place(c):
        for k in range(c * ENC_CHUNK, (c + 1) * ENC_CHUNK):
            onehot[k * tile : (k + 1) * tile, :] = one_hot(index[:, k : k + 1], places)

    def gather(c):
        held["gathered", c] = dot(onehot[c * rows : (c + 1) * rows, :], band[...])

    def activate(c):
        before = held.pop(("gathered", c)).reshape(ENC_CHUNK, tile, width) + received[None]
        sig = sigma(before)
        silu = before * sig
        part = slice(c * rows, (c + 1) * rows)
        slope_ref[part, :] = (sig + silu * (1.0 - sig)).reshape(rows, width).astype(BF)
        hidden = silu.reshape(rows, width).astype(BF)
        hidden_ref[part, :] = hidden
        held["hidden", c] = hidden

    def project(c):
        held["message", c] = dot(held.pop(("hidden", c)), out_ref[...])

    def norm(c):
        centred, factor = normalise(held.pop(("message", c)))
        normed = (centred * factor).reshape(ENC_CHUNK, tile, width)
        normed_ref[c * rows : (c + 1) * rows, :] = normed.reshape(rows, width).astype(BF)
        factor = factor.reshape(ENC_CHUNK, tile, 1)
        for j in range(ENC_CHUNK):
            k = c * ENC_CHUNK + j
            live = jnp.where(count_ref[...] > k, 1.0, 0.0)
            state["total"] = state["total"] + normed[j] * live
            state["scales"] = jnp.where(lane == k, factor[j] * live, state["scales"])

    staggered([place, gather, activate, project, norm], degree // ENC_CHUNK)
    scale_ref[...] = state["scales"]
    nodes = mesh_ref[own, :].astype(F32)
    new_ref[own, :] = (nodes + degree ** (-0.5) * state["total"]).astype(BF)

    @pl.when(step == pl.num_programs(0) - 1)
    def _():
        moved_ref[...] = dot(new_ref[...], dec_send_ref[...]).astype(BF)


def enc_forward(idx, counts, mesh_rows, pieces, enc_send, enc_recv, enc_out, dec_send):
    nodes, degree = idx.shape
    width = mesh_rows.shape[1]
    tile = ENC_TILE
    edges = tile * degree
    band_rows = sum(p.shape[0] for p in pieces)
    square = whole((width, width))
    return pl.pallas_call(
        enc_forward_kernel,
        name="enc_forward",
        grid=(nodes // tile,),
        in_specs=[rows_of(tile, degree), rows_of(tile, 1), whole((nodes, width))]
        + [whole(p.shape) for p in pieces]
        + [square] * 4,
        out_specs=[
            whole((nodes, width)), whole((nodes, width)),
            rows_of(edges, width), rows_of(edges, width), rows_of(edges, width), rows_of(tile, degree),
        ],
        out_shape=[
            jax.ShapeDtypeStruct((nodes, width), BF),
            jax.ShapeDtypeStruct((nodes, width), BF),
            jax.ShapeDtypeStruct((nodes * degree, width), BF),
            jax.ShapeDtypeStruct((nodes * degree, width), BF),
            jax.ShapeDtypeStruct((nodes * degree, width), BF),
            jax.ShapeDtypeStruct((nodes, degree), F32),
        ],
        scratch_shapes=[
            pltpu.VMEM((band_rows, width), BF),
            pltpu.VMEM((edges, band_rows), BF),
            pltpu.VMEM((nodes, width), F32),
        ],
        compiler_params=kernel_params(56),
    )(idx, counts, mesh_rows, *pieces, enc_send, enc_recv, enc_out, dec_send)


def enc_between_kernel(normed_ref, out_ref, *refs):
    refs[-1][...] = dot_nt(normed_ref[...], out_ref[...]).astype(BF)


def enc_between(normed, enc_out, first, count, rows, done=None):
    width = normed.shape[1]
    per_edge = pl.BlockSpec((rows, width), lambda t: (t + first, 0))
    share = count * rows * width
    kept = () if done is None else (done,)
    return pl.pallas_call(
        enc_between_kernel,
        name="enc_between",
        grid=(count,),
        in_specs=[per_edge, whole((width, width))] + [pl.BlockSpec(memory_space=pl.ANY)] * len(kept),
        out_specs=per_edge,
        out_shape=jax.ShapeDtypeStruct(normed.shape, BF),
        input_output_aliases={2: 0} if kept else {},
        compiler_params=kernel_params(56),
        cost_estimate=pl.CostEstimate(flops=2 * share * width, bytes_accessed=4 * share, transcendentals=0),
    )(normed, enc_out, *kept)


def decoder_kernel(
    idx_ref, idx_row_ref, grid_ref, cot_ref, b0_ref, b1_ref, b2_ref, b3_ref, b4_ref, b5_ref,
    recv_ref, out_ref,
    new_ref, hidden_ref, message_cot_ref, before_cot_ref, received_cot_ref,
    left_own_ref, left_ref, right_own_ref, right_ref,
    onehot, onehot_t, received_all, new_all, received_cot_all,
):
    nodes, width = grid_ref.shape
    degree = idx_ref.shape[1]
    blocks = (b0_ref, b1_ref, b2_ref, b3_ref, b4_ref, b5_ref)
    third = b0_ref.shape[0] + b1_ref.shape[0]
    slots = b0_ref.shape[0]
    tile = DEC_TILE
    parts = nodes // tile
    index = idx_ref[...].astype(jnp.int16)
    places = places_of((tile, 3 * third), 1)
    held = {}

    received_all[...] = dot(grid_ref[...], recv_ref[...])

    def spot(i):
        h, j = divmod(i, degree)
        return j, slice(h * tile, (h + 1) * tile), slice(i * tile, (i + 1) * tile)

    def place(i):
        j, at, edges = spot(i)
        onehot[edges, :] = one_hot(index[at, j : j + 1], places)

    def gather(i):
        j, at, edges = spot(i)
        gathered, first = 0.0, 0
        for block in blocks:
            last = first + block.shape[0]
            gathered = gathered + dot(onehot[edges, first:last], block[...])
            first = last
        held["gathered", i] = gathered

    def activate(i):
        j, at, edges = spot(i)
        before = held.pop(("gathered", i)) + received_all[at, :]
        sig = sigma(before)
        silu = before * sig
        hidden = silu.astype(BF)
        hidden_ref[edges, :] = hidden
        held["slope", i] = sig + silu * (1.0 - sig)
        held["message", i] = dot(hidden, out_ref[...])

    def norm(i):
        j, at, edges = spot(i)
        centred, factor = normalise(held.pop(("message", i)))
        normed = centred * factor
        cot = cot_ref[at, :].astype(F32)
        level = cot - jnp.mean(cot, axis=-1, keepdims=True)
        along = jnp.mean(cot * normed, axis=-1, keepdims=True)
        message_cot = (factor * (level - normed * along)).astype(BF)
        message_cot_ref[edges, :] = message_cot
        held["hidden_cot", i] = dot_nt(message_cot, out_ref[...])
        if j == 0:
            new_all[at, :] = grid_ref[at, :].astype(F32) + normed
        else:
            new_all[at, :] += normed

    def back(i):
        j, at, edges = spot(i)
        before_cot = held.pop(("hidden_cot", i)) * held.pop(("slope", i))
        before_cot_ref[edges, :] = before_cot.astype(BF)
        if j == 0:
            received_cot_all[at, :] = before_cot
        else:
            received_cot_all[at, :] += before_cot
        rows = lax.broadcasted_iota(jnp.int32, (2 * third, tile), 0) + third
        picks = jnp.broadcast_to(idx_row_ref[j : j + 1, at], (16, tile)).astype(jnp.int16)[:1]
        onehot_t[:, edges] = one_hot(picks, rows.astype(jnp.int16))

    staggered([place, gather, activate, norm, back], degree * parts)
    left_tot = dot(onehot_t[:third, :], before_cot_ref[...]).astype(BF)
    left_own_ref[...] = left_tot[:slots, :]
    left_ref[...] = left_tot[slots:, :]
    new_ref[...] = new_all[...].astype(BF)
    right_tot = dot(onehot_t[third:, :], before_cot_ref[...]).astype(BF)
    right_own_ref[...] = right_tot[:slots, :]
    right_ref[...] = right_tot[slots:, :]
    received_cot_ref[...] = received_cot_all[...].astype(BF)


def decoder(idx, idx_rows, grid_rows, cot_rows, blocks, dec_recv, dec_out):
    nodes, width = grid_rows.shape
    degree = idx.shape[1]
    third = blocks[0].shape[0] + blocks[1].shape[0]
    edge_shape = jax.ShapeDtypeStruct((degree * nodes, width), BF)
    node_shape = jax.ShapeDtypeStruct((nodes, width), BF)
    own_shape = jax.ShapeDtypeStruct(blocks[0].shape, BF)
    side_shape = jax.ShapeDtypeStruct(blocks[1].shape, BF)
    return pl.pallas_call(
        decoder_kernel,
        name="decoder",
        out_shape=[node_shape, edge_shape, edge_shape, edge_shape, node_shape, own_shape, side_shape, own_shape, side_shape],
        scratch_shapes=[
            pltpu.VMEM((degree * nodes, 3 * third), BF),
            pltpu.VMEM((2 * third, degree * nodes), BF),
            pltpu.VMEM((nodes, width), F32),
            pltpu.VMEM((nodes, width), F32),
            pltpu.VMEM((nodes, width), F32),
        ],
        compiler_params=kernel_params(36),
    )(idx, idx_rows, grid_rows, cot_rows, *blocks, dec_recv, dec_out)


def decoder_rest_kernel(
    idx_row_ref, grid_ref, cot_ref, hidden_ref, message_cot_ref, before_cot_ref, received_cot_ref, recv_ref,
    part_ref, out_grad_ref, recv_grad_ref, centre_tot_ref,
    onehot_t,
):
    third, width = centre_tot_ref.shape
    degree, nodes = idx_row_ref.shape
    tile = DEC_TILE
    rows = places_of((third, tile), 0)
    for i in range(degree * nodes // tile):
        h, j = divmod(i, degree)
        picks = jnp.broadcast_to(idx_row_ref[j : j + 1, h * tile : (h + 1) * tile], (16, tile))
        onehot_t[:, i * tile : (i + 1) * tile] = one_hot(picks.astype(jnp.int16)[:1], rows)
    centre_tot_ref[...] = dot(onehot_t[...], before_cot_ref[...]).astype(BF)
    out_grad_ref[...] = dot_tn(hidden_ref[...], message_cot_ref[...]).astype(BF)
    received_cot = received_cot_ref[...]
    recv_grad_ref[...] = dot_tn(grid_ref[...], received_cot).astype(BF)
    part_ref[...] = cot_ref[...].astype(F32) + dot_nt(received_cot, recv_ref[...])


def decoder_rest(idx_rows, grid_rows, cot_rows, hidden, message_cot, before_cot, received_cot, dec_recv, third):
    degree, nodes = idx_rows.shape
    width = hidden.shape[1]
    return pl.pallas_call(
        decoder_rest_kernel,
        name="decoder_rest",
        out_shape=[
            jax.ShapeDtypeStruct((nodes, width), F32),
            jax.ShapeDtypeStruct((width, width), BF),
            jax.ShapeDtypeStruct((width, width), BF),
            jax.ShapeDtypeStruct((third, width), BF),
        ],
        scratch_shapes=[pltpu.VMEM((third, degree * nodes), BF)],
        compiler_params=kernel_params(20),
        cost_estimate=pl.CostEstimate(
            flops=2 * degree * nodes * width * (third + 2 * width), bytes_accessed=8 * degree * nodes * width,
            transcendentals=0,
        ),
    )(idx_rows, grid_rows, cot_rows, hidden, message_cot, before_cot, received_cot, dec_recv)


def enc_backward_kernel(
    idx_row_ref, scale_ref, mesh_ref, moved_cot_ref, normed_ref, turned_ref, slope_ref, hidden_ref,
    own_ref, high_ref, low_ref, left_ref, right_ref,
    dec_send_ref, recv_ref, out_ref,
    mesh_grad_ref, band_cot_ref, grads_ref,
    onehot_t0, onehot_t1, cot0, cot1, message_cot, totals, out_acc, node_cot, levels, turned_level, received_cot,
):
    step = pl.program_id(0)
    nodes, width = mesh_ref.shape
    edges = normed_ref.shape[0]
    band_rows = totals.shape[0]
    tiles = pl.num_programs(0) - 1
    tile = ENC_TILE
    degree = edges // tile
    scaling = degree ** (-0.5)
    cots = (cot0, cot1)
    onehots = (onehot_t0, onehot_t1)

    @pl.when(step == 0)
    def _():
        totals[...] = jnp.zeros_like(totals)
        cot = dot_nt(moved_cot_ref[...], dec_send_ref[...])
        node_cot[...] = cot
        spread = scaling * cot
        level = spread - jnp.mean(spread, axis=-1, keepdims=True)
        levels[...] = level
        turned_level[...] = dot_nt(level.astype(BF), out_ref[...])
        out_acc[...] = jnp.zeros_like(out_acc)

    def scatter(slot):
        totals[...] += dot(onehots[slot][...], cots[slot][...])

    def edge_part(slot, beside):
        strips = tile // STRIP
        total = [jnp.zeros((STRIP, width), F32)] * strips
        scales = scale_ref[...]
        for n in range(2):
            if beside is not None and n == 0:
                scatter(beside)
            for k in range(n * degree // 2, (n + 1) * degree // 2):
                for i in range(strips):
                    at = slice(k * tile + i * STRIP, k * tile + (i + 1) * STRIP)
                    mine = pl.ds(pl.multiple_of(step * tile + i * STRIP, STRIP), STRIP)
                    normed = normed_ref[at, :].astype(F32)
                    along = scaling * jnp.mean(node_cot[mine, :] * normed, axis=-1, keepdims=True)
                    scale = scales[i * STRIP : (i + 1) * STRIP, k : k + 1]
                    message_cot[at, :] = (scale * (levels[mine, :] - along * normed)).astype(BF)
                    turned = scale * (turned_level[mine, :] - along * turned_ref[at, :].astype(F32))
                    before_cot = slope_ref[at, :].astype(F32) * turned
                    total[i] = total[i] + before_cot
                    cots[slot][at, :] = before_cot.astype(BF)
            part = slice(n * edges // 2, (n + 1) * edges // 2)
            out_acc[...] += dot_tn(hidden_ref[part, :], message_cot[part, :])
        places = places_of((band_rows, edges), 0)
        spot = jnp.broadcast_to(idx_row_ref[0], (16, edges)).astype(jnp.int16)[:1]
        onehots[slot][...] = one_hot(spot, places)
        received_cot[pl.ds(pl.multiple_of(step * tile, tile), tile), :] = jnp.concatenate(total, axis=0).astype(BF)

    @pl.when(step == 0)
    def _():
        edge_part(0, None)

    for parity in range(2):
        @pl.when((step > 0) & (step < tiles) & (step % 2 == parity))
        def _():
            edge_part(parity, 1 - parity)

    @pl.when(step == tiles)
    def _():
        scatter(1)
        grads_ref[width : 2 * width, :] = dot_tn(mesh_ref[...], received_cot[...]).astype(BF)
        grads_ref[2 * width :, :] = out_acc[...].astype(BF)
        mesh_grad_ref[...] = (node_cot[...] + dot_nt(received_cot[...], recv_ref[...])).astype(BF)
        band_cot_ref[...] = totals[...].astype(BF)
        at = 0
        send_grad = jnp.zeros((width, width), F32)
        for piece in (own_ref, high_ref, low_ref, left_ref, right_ref):
            count = piece.shape[0]
            send_grad = send_grad + dot_tn(piece[...], band_cot_ref[at : at + count, :])
            at += count
        grads_ref[:width, :] = send_grad.astype(BF)


def enc_backward(idx_rows, scale, mesh_rows, moved_cot, normed, turned, slope, hidden, pieces, dec_send, enc_recv, enc_out):
    nodes, width = mesh_rows.shape
    degree = scale.shape[1]
    tile = ENC_TILE
    tiles = nodes // tile
    assert tiles % 2 == 0
    edges = normed.shape[0] // tiles
    band_rows = sum(p.shape[0] for p in pieces)
    square = whole((width, width))
    last = tiles - 1
    per_node = whole((nodes, width))
    per_edge = pl.BlockSpec((edges, width), lambda t: (jnp.minimum(t, last), 0))
    return pl.pallas_call(
        enc_backward_kernel,
        name="enc_backward",
        grid=(tiles + 1,),
        in_specs=[
            pl.BlockSpec((1, 1, edges), lambda t: (jnp.minimum(t, last), 0, 0)),
            pl.BlockSpec((tile, degree), lambda t: (jnp.minimum(t, last), 0)),
        ]
        + [per_node] * 2
        + [per_edge] * 4
        + [whole(p.shape) for p in pieces]
        + [square] * 3,
        out_specs=[per_node, whole((band_rows, width)), whole((3 * width, width))],
        out_shape=[
            jax.ShapeDtypeStruct((nodes, width), BF),
            jax.ShapeDtypeStruct((band_rows, width), BF),
            jax.ShapeDtypeStruct((3 * width, width), BF),
        ],
        scratch_shapes=[
            pltpu.VMEM((band_rows, edges), BF),
            pltpu.VMEM((band_rows, edges), BF),
            pltpu.VMEM((edges, width), BF),
            pltpu.VMEM((edges, width), BF),
            pltpu.VMEM((edges, width), BF),
            pltpu.VMEM((band_rows, width), F32),
            pltpu.VMEM((width, width), F32),
            pltpu.VMEM((nodes, width), F32),
            pltpu.VMEM((nodes, width), F32),
            pltpu.VMEM((nodes, width), F32),
            pltpu.VMEM((nodes, width), BF),
        ],
        compiler_params=kernel_params(56),
    )(idx_rows, scale, mesh_rows, moved_cot, normed, turned, slope, hidden, *pieces, dec_send, enc_recv, enc_out)


def to_lon(shard, by):
    count = lax.axis_size("lon")
    return lax.ppermute(shard, "lon", [(i, (i + by) % count) for i in range(count)])


def to_lat(shard, by):
    count = lax.axis_size("lat")
    return lax.ppermute(shard, "lat", [(i, i + by) for i in range(count) if 0 <= i + by < count])


def core_swap(array):
    return lax.ppermute(array, "lon", [(i, i ^ 1) for i in range(lax.axis_size("lon"))])


def across_chips(parts):
    count = lax.axis_size("lat") * lax.axis_size("lon")
    alike = [[i for i in range(count) if i % 2 == c] for c in range(2)]
    return lax.all_to_all(parts, ("lat", "lon"), 0, 0, axis_index_groups=alike, tiled=True)


def on_device(
    grid, mesh_nodes, grid_cot, enc_send, enc_recv, enc_out, dec_send, dec_recv, dec_out,
    enc_src, enc_live, dec_src,
):
    lat_cells, lon_cells, width = grid.shape
    slots, degree = enc_src.shape[2:]
    lat_index = lax.axis_index("lat")
    lon_index = lax.axis_index("lon")
    lon_count = lax.axis_size("lon")
    lon_total = lon_cells * lon_count
    cells = lat_cells * lon_cells
    edge_rows = REACH * lon_cells
    tall = lat_cells + 2 * REACH

    grid_rows = grid.reshape(cells, width)
    mesh_rows = mesh_nodes.reshape(slots, width)
    high = to_lat(grid_rows[:edge_rows], -1)
    low = to_lat(grid_rows[cells - edge_rows :], 1)
    inner = jnp.concatenate([grid_rows, high, low], axis=0).reshape(tall, lon_cells, width)
    left = to_lon(inner[:, lon_cells - REACH :].reshape(tall * REACH, width), 1)
    right = to_lon(inner[:, :REACH].reshape(tall * REACH, width), -1)
    pieces = (grid_rows, high, low, left, right)

    source = enc_src.reshape(slots, degree)
    row = (source // lon_total - lat_index * lat_cells) % tall
    col = (source % lon_total - lon_index * lon_cells + REACH) % lon_total - REACH
    inner_rows = tall * lon_cells
    enc_idx = jnp.where(
        col < 0,
        inner_rows + row * REACH + col + REACH,
        jnp.where(
            col >= lon_cells,
            inner_rows + tall * REACH + row * REACH + col - lon_cells,
            row * lon_cells + col,
        ),
    )
    tiles = slots // ENC_TILE
    enc_idx_rows = enc_idx.reshape(tiles, ENC_TILE, degree).transpose(0, 2, 1)
    enc_idx_rows = enc_idx_rows.reshape(tiles, 1, ENC_TILE * degree)
    counts = jnp.sum(enc_live.reshape(slots, degree), axis=1, keepdims=True)

    picks = dec_src.reshape(3, cells)
    owner = picks // slots
    owner_lat = (owner // lon_count - lat_index) % 3
    owner_lon = (owner % lon_count - lon_index + lon_count) % lon_count
    owner_lon = jnp.where(owner_lon == lon_count - 1, 1, owner_lon * 2)
    dec_idx_rows = (owner_lon * 3 + owner_lat) * slots + picks % slots

    mesh_new, moved, slope, hidden, normed, scale = enc_forward(
        enc_idx, counts, mesh_rows, pieces, enc_send, enc_recv, enc_out, dec_send
    )

    above = to_lat(moved, -1)
    below = to_lat(moved, 1)
    half = slots * degree // 2
    block = half // 4
    part = enc_between(normed, enc_out, 0, 4, block)
    own_west = to_lon(moved, 1)
    own_east = to_lon(moved, -1)
    sides = jnp.concatenate([above, below], axis=0)
    sides, part = lax.optimization_barrier((sides, part))
    west = to_lon(sides, 1)
    east = to_lon(sides, -1)
    turned = enc_between(normed, enc_out, 4, 4, block, part)
    west, east, turned = lax.optimization_barrier((west, east, turned))
    cot_rows = grid_cot.reshape(cells, width)
    (
        grid_new, dec_hidden, dec_message_cot, dec_before_cot, dec_received_cot, west_own, west_tot, east_own, east_tot,
    ) = decoder(
        dec_idx_rows.T, dec_idx_rows, grid_rows, cot_rows, (moved, sides, own_west, west, own_east, east),
        dec_recv, dec_out,
    )
    from_east = to_lon(west_tot, -1)
    from_west = to_lon(east_tot, 1)
    grid_part, dec_out_grad, dec_recv_grad, centre_tot = decoder_rest(
        dec_idx_rows, grid_rows, cot_rows, dec_hidden, dec_message_cot, dec_before_cot, dec_received_cot,
        dec_recv, 3 * slots,
    )
    from_east, from_west, west_own, east_own = lax.optimization_barrier((from_east, from_west, west_own, east_own))

    def met(first):
        at = slice(first, first + slots)
        other = centre_tot[slots + first : 2 * slots + first].astype(F32)
        return (other + from_east[at].astype(F32) + from_west[at].astype(F32)).astype(BF)

    from_below = to_lat(met(0), 1)
    from_above = to_lat(met(slots), -1)
    own_cot = to_lon(west_own, -1).astype(F32) + to_lon(east_own, 1).astype(F32)
    moved_cot = centre_tot[:slots].astype(F32) + own_cot + from_below.astype(F32) + from_above.astype(F32)
    moved_cot = moved_cot.astype(BF)
    dec_send_grad = dot_tn(mesh_new, moved_cot).astype(BF)

    mesh_grad, band_cot, enc_stack = enc_backward(
        enc_idx_rows, scale, mesh_rows, moved_cot, normed, turned, slope, hidden, pieces, dec_send, enc_recv, enc_out
    )
    dec_stack = jnp.concatenate([dec_send_grad, dec_recv_grad, dec_out_grad], axis=0)

    side = tall * REACH
    from_right = to_lon(band_cot[inner_rows : inner_rows + side], -1)
    from_left = to_lon(band_cot[inner_rows + side :], 1)

    leads = lon_index % 2 == 0
    chips = lax.axis_size("lat") * lon_count // 2
    swapped = core_swap(jnp.where(leads, dec_stack, enc_stack))
    kept = jnp.where(leads, enc_stack, dec_stack).astype(F32) + swapped.astype(F32)
    kept = kept.astype(BF).reshape(chips, 3 * width // chips, width)
    kept, from_right, from_left = lax.optimization_barrier((kept, from_right, from_left))

    inner_cot = band_cot[:inner_rows].astype(F32).reshape(tall, lon_cells, width)
    inner_cot = inner_cot.at[:, lon_cells - REACH :].add(from_right.astype(F32).reshape(tall, REACH, width))
    inner_cot = inner_cot.at[:, :REACH].add(from_left.astype(F32).reshape(tall, REACH, width))
    inner_cot = inner_cot.reshape(inner_rows, width)
    from_low = to_lat(inner_cot[cells : cells + edge_rows].astype(BF), 1)
    from_high = to_lat(inner_cot[cells + edge_rows :].astype(BF), -1)

    mine = jnp.sum(across_chips(kept).astype(F32), axis=0).astype(BF)
    mine, from_low, from_high = lax.optimization_barrier((mine, from_low, from_high))
    ours = across_chips(jnp.broadcast_to(mine[None], kept.shape)).reshape(3 * width, width)
    theirs = core_swap(ours)
    enc_grads = jnp.where(leads, ours, theirs).astype(F32)
    dec_grads = jnp.where(leads, theirs, ours).astype(F32)

    sent_cot = inner_cot[:cells] + jnp.concatenate([from_low, from_high], axis=0).astype(F32)
    grid_grad = (grid_part + dot_nt(sent_cot.astype(BF), enc_send)).astype(BF)

    return (
        grid_new.reshape(grid.shape),
        grid_grad.reshape(grid.shape),
        mesh_grad.reshape(mesh_nodes.shape),
        enc_grads[:width],
        enc_grads[width : 2 * width],
        enc_grads[2 * width :],
        dec_grads[:width],
        dec_grads[width : 2 * width],
        dec_grads[2 * width :],
    )


def solution(mesh):
    node = P("lat", "lon", None)
    block = P("lat", "lon", None, None)
    placed = (
        node, block, node, P(), P(), P(), P(), P(), P(), block, block, P(None, "lat", "lon"),
    )
    return jax.shard_map(
        on_device,
        mesh=mesh,
        in_specs=placed,
        out_specs=(node, node, block, P(), P(), P(), P(), P(), P()),
        check_vma=False,
    )
```
